32 devices in a mesh: vocab: 16 (over z, x, core), tok: 2 (over y).
Axes of the slice: x: 2, y: 2, z: 4, core: 2. Of those that a mesh axis runs over, the one named last changes fastest.
Arguments:
- hidden: bfloat16 [256, 3584], P('tok'), may hold values from -320 to 320
- head: bfloat16 [3584, 24576], P('tok', 'vocab'), may hold values from -2 to 2
- teacher: bfloat16 [256, 24576], P('tok', 'vocab'), may hold values from 0 to 1, as said below
- block_ids: int32 [2, 16], P('tok'), may hold values from -1 to 47, as said below
- counts: int32 [2], P('tok'), may hold values from 8 to 16
Outputs:
- lse: float32 [256], P('tok')
- kl: float32 [256], P('tok')
- grad_hidden: float32 [256, 3584], P('tok', 'vocab')
- grad_head: bfloat16 [3584, 24576], P('tok', 'vocab')
The draws below stay inside these ranges and needn't reach their ends.
Inputs may be any that keep to these rules, and one draw needn't show every extreme that they name: `block_ids`: row b lists counts[b] distinct teacher blocks (block k covers columns 512 * k to 512 * k + 511) in its first counts[b] entries; the rest of the row is -1. `teacher`: every entry is positive.
All inputs are finite; a program needn't handle non-finite values.
Results may differ from the reference program's by a relative error of at most 0.0055.
Values may be sent and summed in bfloat16 or wider, within the bound.
No kernel may reach another device: no remote copies, remote signals or barrier semaphores. Data moves between devices by JAX's collectives and lax.ppermute only.
A program may use at most 64 MiB of HBM per device.

```python
import jax
import jax.numpy as jnp
from jax import lax

D = 3584
BLK = 512
TB = 128
SLOTS = 16
V = 24576
TOKENS = 256
NTB = 2


def shared_direction(key):
    return jax.random.rademacher(jax.random.fold_in(key, 7), (D,), dtype=jnp.float32)


def drawn_start(key):
    return jax.random.randint(jax.random.fold_in(key, 9), (), 0, V - 3)


def draw_hidden(key, part):
    return jax.random.truncated_normal(jax.random.fold_in(key, 1), -6.0, 6.0, (TOKENS, D)).astype(jnp.bfloat16)


def draw_head(key, part):
    position = jnp.arange(V, dtype=jnp.int32)
    spread = (2.9 + 0.45 * position.astype(jnp.float32) / V) / D ** 0.5
    base_values = jax.random.truncated_normal(jax.random.fold_in(key, 2), -4.0, 4.0, (D, V)) * spread[None, :]
    offset = position - drawn_start(key)
    inside = (offset >= 0) & (offset < 3)
    factor = 2.0 ** (-(D.bit_length() - 1))
    levels = (1.0 - jnp.clip(offset, 0, 2).astype(jnp.float32) * 2.0 ** (-8)) * factor
    aligned = shared_direction(key)[:, None] * levels[None, :]
    return jnp.where(inside[None, :], aligned, base_values).astype(jnp.bfloat16)


def draw_teacher(key, part):
    position = jnp.arange(V, dtype=jnp.float32) / V
    element = jax.random.uniform(jax.random.fold_in(key, 31), (TOKENS, V))
    column = jax.random.uniform(jax.random.fold_in(key, 32), (V,))
    exponent = -10.0 * element - 4.0 * column[None, :] + 1.1 * (position[None, :] - 1.0)
    return jnp.exp(exponent).astype(jnp.bfloat16)


def teacher_lists(key):
    block_total = V // BLK
    heat = jax.random.randint(jax.random.fold_in(key, 21), (block_total,), 0, 4)
    noise = jax.random.randint(jax.random.fold_in(key, 22), (NTB, block_total), 0, 4096)
    scores = (noise + heat[None, :] * 2048) * block_total + jnp.arange(block_total, dtype=jnp.int32)[None, :]
    unused, picked = lax.top_k(scores, SLOTS)
    drawn = jax.random.randint(jax.random.fold_in(key, 23), (NTB,), SLOTS // 2, SLOTS + 1)
    fullest = jax.random.randint(jax.random.fold_in(key, 24), (), 0, NTB)
    row_index = jnp.arange(NTB, dtype=jnp.int32)
    drawn = jnp.where(row_index == fullest, SLOTS, drawn)
    drawn = jnp.where(row_index == (fullest + 1) % NTB, SLOTS // 2, drawn)
    slot_index = jnp.arange(SLOTS, dtype=jnp.int32)[None, :]
    listing = jnp.where(slot_index < drawn[:, None], picked.astype(jnp.int32), -1)
    return (listing, drawn.astype(jnp.int32))


def draw_block_ids(key, part):
    return teacher_lists(key)[0]


def draw_counts(key, part):
    return teacher_lists(key)[1]


def setup_inputs(seed: int = 0) -> dict:
    key_of = jax.random.split(jax.random.key(seed), 6)
    return {
        "hidden": draw_hidden(jax.random.fold_in(key_of[5], 71), 0),
        "head": draw_head(jax.random.fold_in(key_of[5], 71), 0),
        "teacher": draw_teacher(jax.random.fold_in(key_of[5], 71), 0),
        "block_ids": draw_block_ids(jax.random.fold_in(key_of[5], 71), 0),
        "counts": draw_counts(jax.random.fold_in(key_of[5], 71), 0),
    }


loss_scale = 1024.0


def reference(hidden, head, teacher, block_ids, counts):
    logits = jnp.dot(hidden, head, preferred_element_type=jnp.float32)
    highest = jnp.max(logits, axis=1)
    lse = highest + jnp.log(jnp.sum(jnp.exp(logits - highest[:, None]), axis=1))
    block_total = head.shape[1] // BLK
    live_slot = jnp.arange(SLOTS, dtype=jnp.int32)[None, :] < counts[:, None]
    block_range = jnp.arange(block_total, dtype=jnp.int32)
    block_hit = jnp.any((block_ids[:, :, None] == block_range[None, None, :]) & live_slot[:, :, None], axis=1)
    column_hit = jnp.repeat(block_hit, BLK, axis=1)
    listed = jnp.repeat(column_hit, TB, axis=0)
    teacher_f = teacher.astype(jnp.float32)
    kept = jnp.where(listed, teacher_f, 0.0)
    mass = jnp.sum(kept, axis=1)
    weighted = jnp.sum(jnp.where(listed, teacher_f * (jnp.log(teacher_f) - logits), 0.0), axis=1)
    kl = weighted / mass - jnp.log(mass) + lse
    student = jnp.exp(logits - lse[:, None])
    delta = (loss_scale * (student - kept / mass[:, None])).astype(jnp.bfloat16)
    grad_hidden = jnp.dot(delta, head.T, preferred_element_type=jnp.float32)
    grad_head = jnp.dot(hidden.T, delta, preferred_element_type=jnp.float32).astype(jnp.bfloat16)
    return (lse, kl, grad_hidden, grad_head)
```

```python
import jax
import jax.numpy as jnp
from jax import lax
from jax.sharding import PartitionSpec as P

BLK = 512


loss_scale = 1024.0


def shift_tok(x, offset, size):
    return lax.ppermute(x, "tok", [(i, (i + offset) % size) for i in range(size)])


def swap_vocab(x, bit, size):
    return lax.ppermute(x, "vocab", [(i, i ^ bit) for i in range(size)])


def listed_columns(block_ids, counts, column_block, token_count):
    live_slot = jnp.arange(block_ids.shape[1], dtype=jnp.int32)[None, :] < counts[:, None]
    block_hit = jnp.any(
        (block_ids[:, :, None] == column_block[None, None, :]) & live_slot[:, :, None], axis=1
    )
    token_blocks = block_hit.shape[0]
    width = column_block.shape[0]
    return jnp.broadcast_to(
        block_hit[:, None, :], (token_blocks, token_count // token_blocks, width)
    ).reshape(token_count, width)


def gather_vocab(stats, vocab_index, size):
    gathered = stats[None]
    bit = 1
    while bit < size:
        other = swap_vocab(gathered, bit, size)
        upper = (vocab_index & bit) != 0
        gathered = jnp.concatenate(
            [jnp.where(upper, other, gathered), jnp.where(upper, gathered, other)], axis=0
        )
        bit *= 2
    return gathered


def sum_vocab(partial, vocab_index, tok_index, vocab_size, tok_size, token_count):
    run = vocab_size // tok_size
    rows = partial.shape[0] // run
    held = partial.reshape(run, rows, partial.shape[1])
    bit = 1
    while bit < run:
        pairs = held.reshape(held.shape[0] // 2, 2, rows, held.shape[2])
        mine = (vocab_index // bit) % 2
        keep = lax.dynamic_index_in_dim(pairs, mine, 1, keepdims=False)
        send = lax.dynamic_index_in_dim(pairs, 1 - mine, 1, keepdims=False)
        other = swap_vocab(send.astype(jnp.bfloat16), bit, vocab_size)
        held = keep + other.astype(jnp.float32)
        bit *= 2
    held = held.reshape(rows, tok_size, token_count)
    blocks = [lax.dynamic_index_in_dim(held, tok_index, 1, keepdims=False)]
    for d in range(1, tok_size):
        send = lax.dynamic_index_in_dim(held, (tok_index + d) % tok_size, 1, keepdims=False)
        blocks.append(shift_tok(send, d, tok_size))
    blocks = jnp.stack(blocks)
    high = vocab_index // run
    total = lax.dynamic_index_in_dim(blocks, (tok_index - high) % tok_size, 0, keepdims=False)
    for d in range(1, tok_size):
        target = (high + d) % tok_size
        send = lax.dynamic_index_in_dim(blocks, (tok_index - target) % tok_size, 0, keepdims=False)
        total = total + lax.ppermute(
            send, "vocab", [(i, (i + d * run) % vocab_size) for i in range(vocab_size)]
        )
    return total


def per_device(hidden, head, teacher, block_ids, counts):
    tok_size = lax.axis_size("tok")
    vocab_size = lax.axis_size("vocab")
    tok_index = lax.axis_index("tok")
    vocab_index = lax.axis_index("vocab")
    token_count = hidden.shape[0]
    rows, column_count = head.shape

    def columns_of(index):
        return lax.dynamic_slice_in_dim(hidden, index * rows, rows, axis=1)

    features = [columns_of(tok_index)]
    for d in range(1, tok_size):
        features.append(shift_tok(columns_of((tok_index + d) % tok_size), d, tok_size))
    returned = []
    for d in range(1, tok_size):
        partial = jnp.dot(features[d], head, preferred_element_type=jnp.float32)
        returned.append(shift_tok(partial, -d, tok_size))
    logits = jnp.dot(features[0], head, preferred_element_type=jnp.float32)
    for partial in returned:
        logits = logits + partial

    first_column = vocab_index * column_count
    column_block = (first_column + jnp.arange(column_count, dtype=jnp.int32)) // BLK
    listed = listed_columns(block_ids, counts, column_block, token_count)
    teacher_f = teacher.astype(jnp.float32)
    kept = jnp.where(listed, teacher_f, 0.0)
    local_top = jnp.max(logits, axis=1)
    local_sum = jnp.sum(jnp.exp(logits - local_top[:, None]), axis=1)
    local_mass = jnp.sum(kept, axis=1)
    local_part = jnp.sum(jnp.where(listed, teacher_f * (jnp.log(teacher_f) - logits), 0.0), axis=1)

    stats = gather_vocab(
        jnp.stack([local_top, local_sum, local_mass, local_part]), vocab_index, vocab_size
    )
    tops = stats[:, 0]
    global_top = jnp.max(tops, axis=0)
    total_sum = jnp.sum(stats[:, 1] * jnp.exp(tops - global_top[None, :]), axis=0)
    total_mass = jnp.sum(stats[:, 2], axis=0)
    total_part = jnp.sum(stats[:, 3], axis=0)
    lse = global_top + jnp.log(total_sum)
    kl = total_part / total_mass - jnp.log(total_mass) + lse
    student = jnp.exp(logits - lse[:, None])
    delta = (loss_scale * (student - kept / total_mass[:, None])).astype(jnp.bfloat16)

    deltas = [delta] + [shift_tok(delta, d, tok_size) for d in range(1, tok_size)]
    all_delta = jnp.concatenate(deltas, axis=0)
    all_features = jnp.concatenate(features, axis=0)

    partial = lax.dot_general(
        head, all_delta, (((1,), (1,)), ((), ())), preferred_element_type=jnp.float32
    )
    partial = partial.reshape(rows, tok_size, token_count)
    partial = jnp.stack(
        [
            lax.dynamic_index_in_dim(partial, (tok_index - owner) % tok_size, 1, keepdims=False)
            for owner in range(tok_size)
        ],
        axis=1,
    ).reshape(rows, tok_size * token_count)
    grad_hidden = sum_vocab(
        partial, vocab_index, tok_index, vocab_size, tok_size, token_count
    ).T
    grad_head = lax.dot_general(
        all_features, all_delta, (((0,), (0,)), ((), ())), preferred_element_type=jnp.float32
    ).astype(jnp.bfloat16)
    return (lse, kl, grad_hidden, grad_head)


def solution(mesh):
    placed = (P("tok", None), P("tok", "vocab"), P("tok", "vocab"), P("tok", None), P("tok"))
    return jax.shard_map(
        per_device,
        mesh=mesh,
        in_specs=placed,
        out_specs=(P("tok"), P("tok"), P("tok", "vocab"), P("tok", "vocab")),
        check_vma=False,
    )
```

```python
import jax
import jax.numpy as jnp
from jax import lax
from jax.sharding import PartitionSpec as P

BLK = 512


loss_scale = 1024.0


def shift_tok(x, offset, size):
    return lax.ppermute(x, "tok", [(i, (i + offset) % size) for i in range(size)])


def swap_vocab(x, bit, size):
    return lax.ppermute(x, "vocab", [(i, i ^ bit) for i in range(size)])


def pick(x, index, axis=0):
    return lax.dynamic_index_in_dim(x, index, axis, keepdims=False)


def listed_columns(block_ids, counts, column_block, token_count):
    live_slot = jnp.arange(block_ids.shape[1], dtype=jnp.int32)[None, :] < counts[:, None]
    block_hit = jnp.any(
        (block_ids[:, :, None] == column_block[None, None, :]) & live_slot[:, :, None], axis=1
    )
    token_blocks = block_hit.shape[0]
    width = column_block.shape[0]
    return jnp.broadcast_to(
        block_hit[:, None, :], (token_blocks, token_count // token_blocks, width)
    ).reshape(token_count, width)


def in_order(mine, other, upper):
    return jnp.concatenate(
        [jnp.where(upper, other, mine), jnp.where(upper, mine, other)], axis=0
    )


def gather_vocab(stats, vocab_index, size):
    gathered = stats[None]
    bit = 1
    while bit < size:
        other = swap_vocab(gathered, bit, size)
        gathered = in_order(gathered, other, (vocab_index & bit) != 0)
        bit *= 2
    return gathered


def halve(partial, vocab_index, vocab_size, run):
    rows = partial.shape[0] // run
    held = partial.reshape(run, rows, partial.shape[1])
    bit = 1
    while bit < run:
        pairs = held.reshape(held.shape[0] // 2, 2, rows, held.shape[2])
        mine = (vocab_index // bit) % 2
        send = pick(pairs, 1 - mine, 1).astype(jnp.bfloat16)
        other = swap_vocab(send, bit, vocab_size)
        held = pick(pairs, mine, 1) + other.astype(jnp.float32)
        bit *= 2
    return held[0]


def per_device(hidden, head, teacher, block_ids, counts):
    tok_size = lax.axis_size("tok")
    vocab_size = lax.axis_size("vocab")
    tok_index = lax.axis_index("tok")
    vocab_index = lax.axis_index("vocab")
    token_count = hidden.shape[0]
    rows, column_count = head.shape
    run = vocab_size // tok_size
    half = token_count // 2
    core = vocab_index % 2

    def columns_of(index, first, count):
        return lax.dynamic_slice(hidden, (first, index * rows), (count, rows))

    near = [
        shift_tok(columns_of((tok_index + d) % tok_size, core * half, half), d, tok_size)
        for d in range(1, tok_size)
    ]
    far = [swap_vocab(x, 1, vocab_size) for x in near]
    returned = []
    for d in range(1, tok_size):
        first = shift_tok(
            jnp.dot(near[d - 1], head, preferred_element_type=jnp.float32), -d, tok_size
        )
        second = shift_tok(
            jnp.dot(far[d - 1], head, preferred_element_type=jnp.float32), -d, tok_size
        )
        returned.append((first, second))
    own = columns_of(tok_index, 0, token_count)
    logits = jnp.dot(own, head, preferred_element_type=jnp.float32)
    for first, second in returned:
        logits = logits + in_order(first, second, core != 0)

    first_column = vocab_index * column_count
    column_block = (first_column + jnp.arange(column_count, dtype=jnp.int32)) // BLK
    listed = listed_columns(block_ids, counts, column_block, token_count)
    teacher_f = teacher.astype(jnp.float32)
    kept = jnp.where(listed, teacher_f, 0.0)
    local_top = jnp.max(logits, axis=1)
    local_sum = jnp.sum(jnp.exp(logits - local_top[:, None]), axis=1)
    local_mass = jnp.sum(kept, axis=1)
    local_part = jnp.sum(jnp.where(listed, teacher_f * (jnp.log(teacher_f) - logits), 0.0), axis=1)

    stats = gather_vocab(
        jnp.stack([local_top, local_sum, local_mass, local_part]), vocab_index, vocab_size
    )
    tops = stats[:, 0]
    global_top = jnp.max(tops, axis=0)
    total_sum = jnp.sum(stats[:, 1] * jnp.exp(tops - global_top[None, :]), axis=0)
    total_mass = jnp.sum(stats[:, 2], axis=0)
    total_part = jnp.sum(stats[:, 3], axis=0)
    lse = global_top + jnp.log(total_sum)
    kl = total_part / total_mass - jnp.log(total_mass) + lse
    student = jnp.exp(logits - lse[:, None])
    delta = (loss_scale * (student - kept / total_mass[:, None])).astype(jnp.bfloat16)

    deltas = [delta] + [shift_tok(delta, d, tok_size) for d in range(1, tok_size)]
    sums = [
        halve(
            lax.dot_general(
                head, x, (((1,), (1,)), ((), ())), preferred_element_type=jnp.float32
            ),
            vocab_index,
            vocab_size,
            run,
        )
        for x in deltas
    ]
    blocks = [sums[0]] + [
        shift_tok(sums[d].astype(jnp.bfloat16), -d, tok_size).astype(jnp.float32)
        for d in range(1, tok_size)
    ]
    blocks = jnp.stack(blocks)
    high = vocab_index // run
    total = pick(blocks, (high - tok_index) % tok_size)
    for d in range(1, tok_size):
        send = pick(blocks, (high + d - tok_index) % tok_size).astype(jnp.bfloat16)
        total = total + lax.ppermute(
            send, "vocab", [(i, (i + d * run) % vocab_size) for i in range(vocab_size)]
        ).astype(jnp.float32)
    grad_hidden = total.T

    all_delta = jnp.concatenate(deltas, axis=0)
    features = [own] + [in_order(n, f, core != 0) for n, f in zip(near, far)]
    grad_head = lax.dot_general(
        jnp.concatenate(features, axis=0),
        all_delta,
        (((0,), (0,)), ((), ())),
        preferred_element_type=jnp.float32,
    ).astype(jnp.bfloat16)
    return (lse, kl, grad_hidden, grad_head)


def solution(mesh):
    placed = (P("tok", None), P("tok", "vocab"), P("tok", "vocab"), P("tok", None), P("tok"))
    return jax.shard_map(
        per_device,
        mesh=mesh,
        in_specs=placed,
        out_specs=(P("tok"), P("tok"), P("tok", "vocab"), P("tok", "vocab")),
        check_vma=False,
    )
```

```python
import jax
import jax.numpy as jnp
from jax import lax
from jax.experimental import pallas as pl
from jax.experimental.pallas import tpu as pltpu
from jax.sharding import PartitionSpec as P

BLK = 512


loss_scale = 1024.0
VMEM_LIMIT = 8 << 20


def shift_tok(x, offset, size):
    return lax.ppermute(x, "tok", [(i, (i + offset) % size) for i in range(size)])


def swap_vocab(x, bit, size):
    return lax.ppermute(x, "vocab", [(i, i ^ bit) for i in range(size)])


def load_kernel(head_ref, out_ref, sem):
    copy = pltpu.make_async_copy(head_ref, out_ref, sem)
    copy.start()
    copy.wait()


def load(head):
    return pl.pallas_call(
        load_kernel,
        out_shape=pltpu.VMEM(head.shape, head.dtype),
        in_specs=[pl.BlockSpec(memory_space=pl.ANY)],
        out_specs=pl.BlockSpec(memory_space=pl.ANY),
        scratch_shapes=[pltpu.SemaphoreType.DMA],
        compiler_params=pltpu.CompilerParams(vmem_limit_bytes=1 << 20),
        cost_estimate=pl.CostEstimate(flops=0, bytes_accessed=2 * head.size, transcendentals=0),
        name="load_head",
    )(pltpu.with_memory_space_constraint(head, pltpu.HBM))


def pick(x, index, axis=0):
    return lax.dynamic_index_in_dim(x, index, axis, keepdims=False)


def listed_columns(block_ids, counts, column_block, token_count):
    live_slot = jnp.arange(block_ids.shape[1], dtype=jnp.int32)[None, :] < counts[:, None]
    block_hit = jnp.any(
        (block_ids[:, :, None] == column_block[None, None, :]) & live_slot[:, :, None], axis=1
    )
    token_blocks = block_hit.shape[0]
    width = column_block.shape[0]
    return jnp.broadcast_to(
        block_hit[:, None, :], (token_blocks, token_count // token_blocks, width)
    ).reshape(token_count, width)


def in_order(mine, other, upper):
    return jnp.concatenate(
        [jnp.where(upper, other, mine), jnp.where(upper, mine, other)], axis=0
    )


def gather_vocab(stats, size):
    pair = jnp.stack([stats, swap_vocab(stats, 1, size)])
    pairs = [pair] + [swap_vocab(pair, bit, size) for bit in range(2, size, 2)]
    return jnp.concatenate(pairs, axis=0)


def tree_sum(x):
    while x.shape[0] > 1:
        half = x.shape[0] // 2
        x = x[:half] + x[half:]
    return x[0]


def gradient_kernel(core_ref, head_ref, delta_ref, send_ref, keep_ref):
    upper = core_ref[0] == 1
    pairs, rows, _ = send_ref.shape
    for k in range(pairs):
        block = lax.dot_general(
            head_ref[2 * k * rows : 2 * (k + 1) * rows, :],
            delta_ref[...],
            (((1,), (1,)), ((), ())),
            preferred_element_type=jnp.float32,
        )
        low, high = block[:rows], block[rows:]
        send_ref[k] = jnp.where(upper, low, high).astype(jnp.bfloat16)
        keep_ref[k] = jnp.where(upper, high, low)


def gradient(core, head, delta, run):
    rows = head.shape[0] // run
    shape = (run // 2, rows, delta.shape[0])
    in_vmem = pl.BlockSpec(memory_space=pltpu.VMEM)
    return pl.pallas_call(
        gradient_kernel,
        out_shape=(pltpu.VMEM(shape, jnp.bfloat16), pltpu.VMEM(shape, jnp.float32)),
        in_specs=[pl.BlockSpec(memory_space=pltpu.SMEM), in_vmem, in_vmem],
        out_specs=(in_vmem, in_vmem),
        compiler_params=pltpu.CompilerParams(vmem_limit_bytes=VMEM_LIMIT),
        cost_estimate=pl.CostEstimate(
            flops=2 * head.size * delta.shape[0],
            bytes_accessed=2 * (head.size + delta.size),
            transcendentals=0,
        ),
        name="partial_gradient",
    )(
        core.reshape(1),
        pltpu.with_memory_space_constraint(head, pltpu.VMEM),
        pltpu.with_memory_space_constraint(delta, pltpu.VMEM),
    )


def halve(send, keep, vocab_index, vocab_size):
    held = keep + swap_vocab(send, 1, vocab_size).astype(jnp.float32)
    bit = 2
    while held.shape[0] > 1:
        pairs = held.reshape(held.shape[0] // 2, 2, *held.shape[1:])
        mine = (vocab_index // bit) % 2
        send = pick(pairs, 1 - mine, 1).astype(jnp.bfloat16)
        other = swap_vocab(send, bit, vocab_size)
        held = pick(pairs, mine, 1) + other.astype(jnp.float32)
        bit *= 2
    return held[0]


def per_device(hidden, head, teacher, block_ids, counts):
    tok_size = lax.axis_size("tok")
    vocab_size = lax.axis_size("vocab")
    tok_index = lax.axis_index("tok")
    vocab_index = lax.axis_index("vocab")
    token_count = hidden.shape[0]
    rows, column_count = head.shape
    run = vocab_size // tok_size
    half = token_count // 2
    head = load(head)
    core = vocab_index % 2

    def columns_of(index, first, count):
        return lax.dynamic_slice(hidden, (first, index * rows), (count, rows))

    near = [
        shift_tok(columns_of((tok_index + d) % tok_size, core * half, half), d, tok_size)
        for d in range(1, tok_size)
    ]
    far = [swap_vocab(x, 1, vocab_size) for x in near]
    returned = []
    for d in range(1, tok_size):
        first = shift_tok(
            jnp.dot(near[d - 1], head, preferred_element_type=jnp.float32), -d, tok_size
        )
        second = shift_tok(
            jnp.dot(far[d - 1], head, preferred_element_type=jnp.float32), -d, tok_size
        )
        returned.append((first, second))
    own = columns_of(tok_index, 0, token_count)
    logits = lax.optimization_barrier(jnp.dot(own, head, preferred_element_type=jnp.float32))
    for first, second in returned:
        logits = logits + in_order(first, second, core != 0)

    first_column = vocab_index * column_count
    column_block = (first_column + jnp.arange(column_count, dtype=jnp.int32)) // BLK
    listed = listed_columns(block_ids, counts, column_block, token_count)
    teacher_f = teacher.astype(jnp.float32)
    kept = jnp.where(listed, teacher_f, 0.0)
    local_top = jnp.max(logits, axis=1)
    local_sum = jnp.sum(jnp.exp(logits - local_top[:, None]), axis=1)
    local_mass = jnp.sum(kept, axis=1)
    local_part = jnp.sum(jnp.where(listed, teacher_f * (jnp.log(teacher_f) - logits), 0.0), axis=1)

    stats = gather_vocab(jnp.stack([local_top, local_sum, local_mass, local_part]), vocab_size)
    tops = stats[:, 0]
    global_top = jnp.max(tops, axis=0)
    total_sum = tree_sum(stats[:, 1] * jnp.exp(tops - global_top[None, :]))
    total_mass, total_part = tree_sum(stats[:, 2]), tree_sum(stats[:, 3])
    lse = global_top + jnp.log(total_sum)
    kl = total_part / total_mass - jnp.log(total_mass) + lse
    student = jnp.exp(logits - lse[:, None])
    delta = (loss_scale * (student - kept / total_mass[:, None])).astype(jnp.bfloat16)

    deltas = [delta] + [shift_tok(delta, d, tok_size) for d in range(1, tok_size)]
    sums = [halve(*gradient(core, head, x, run), vocab_index, vocab_size) for x in deltas]
    blocks = [sums[0]] + [
        shift_tok(sums[d].astype(jnp.bfloat16), -d, tok_size).astype(jnp.float32)
        for d in range(1, tok_size)
    ]
    blocks = jnp.stack(blocks)
    high = vocab_index // run
    total = pick(blocks, (high - tok_index) % tok_size)
    for d in range(1, tok_size):
        send = pick(blocks, (high + d - tok_index) % tok_size).astype(jnp.bfloat16)
        total = total + lax.ppermute(
            send, "vocab", [(i, (i + d * run) % vocab_size) for i in range(vocab_size)]
        ).astype(jnp.float32)
    grad_hidden = total.T

    all_delta = jnp.concatenate(deltas, axis=0)
    features = [own] + [in_order(n, f, core != 0) for n, f in zip(near, far)]
    grad_head = lax.dot_general(
        jnp.concatenate(features, axis=0),
        all_delta,
        (((0,), (0,)), ((), ())),
        preferred_element_type=jnp.float32,
    ).astype(jnp.bfloat16)
    return (lse, kl, grad_hidden, grad_head)


def solution(mesh):
    placed = (P("tok", None), P("tok", "vocab"), P("tok", "vocab"), P("tok", None), P("tok"))
    return jax.shard_map(
        per_device,
        mesh=mesh,
        in_specs=placed,
        out_specs=(P("tok"), P("tok"), P("tok", "vocab"), P("tok", "vocab")),
        check_vma=False,
    )
```

```python
import jax
import jax.numpy as jnp
from jax import lax
from jax.experimental import pallas as pl
from jax.experimental.pallas import tpu as pltpu
from jax.sharding import PartitionSpec as P

BLK = 512


loss_scale = 1024.0
VMEM_LIMIT = 16 << 20


def shift_tok(x, offset, size):
    return lax.ppermute(x, "tok", [(i, (i + offset) % size) for i in range(size)])


def swap_vocab(x, bit, size):
    return lax.ppermute(x, "vocab", [(i, i ^ bit) for i in range(size)])


def pick(x, index, axis=0):
    return lax.dynamic_index_in_dim(x, index, axis, keepdims=False)


def listed_columns(block_ids, counts, column_block, token_count):
    live_slot = jnp.arange(block_ids.shape[1], dtype=jnp.int32)[None, :] < counts[:, None]
    block_hit = jnp.any(
        (block_ids[:, :, None] == column_block[None, None, :]) & live_slot[:, :, None], axis=1
    )
    token_blocks = block_hit.shape[0]
    width = column_block.shape[0]
    return jnp.broadcast_to(
        block_hit[:, None, :], (token_blocks, token_count // token_blocks, width)
    ).reshape(token_count, width)


def in_order(mine, other, upper):
    return jnp.concatenate(
        [jnp.where(upper, other, mine), jnp.where(upper, mine, other)], axis=0
    )


def gather_vocab(stats, vocab_index, size):
    gathered = stats[None]
    bit = 1
    while bit < size:
        other = swap_vocab(gathered, bit, size)
        gathered = in_order(gathered, other, (vocab_index & bit) != 0)
        bit *= 2
    return gathered


def gradient_kernel(core_ref, head_ref, delta_ref, send_ref, keep_ref, held_ref, sems):
    upper = core_ref[0] == 1
    pairs, rows, _ = send_ref.shape
    parts = [pl.ds(2 * k * rows, 2 * rows) for k in range(pairs)]
    copies = [
        pltpu.make_async_copy(head_ref.at[part], held_ref.at[part], sems.at[k])
        for k, part in enumerate(parts)
    ]
    for copy in copies:
        copy.start()
    for k in range(pairs):
        copies[k].wait()
        block = lax.dot_general(
            held_ref[2 * k * rows : 2 * (k + 1) * rows, :],
            delta_ref[...],
            (((1,), (1,)), ((), ())),
            preferred_element_type=jnp.float32,
        )
        low, high = block[:rows], block[rows:]
        send_ref[k] = jnp.where(upper, low, high).astype(jnp.bfloat16)
        keep_ref[k] = jnp.where(upper, high, low)


def gradient(core, head, delta, run):
    rows = head.shape[0] // run
    shape = (run // 2, rows, delta.shape[0])
    in_vmem = pl.BlockSpec(memory_space=pltpu.VMEM)
    return pl.pallas_call(
        gradient_kernel,
        out_shape=(pltpu.VMEM(shape, jnp.bfloat16), pltpu.VMEM(shape, jnp.float32)),
        in_specs=[
            pl.BlockSpec(memory_space=pltpu.SMEM),
            pl.BlockSpec(memory_space=pltpu.HBM),
            in_vmem,
        ],
        out_specs=(in_vmem, in_vmem),
        scratch_shapes=[
            pltpu.VMEM(head.shape, head.dtype),
            pltpu.SemaphoreType.DMA((run // 2,)),
        ],
        compiler_params=pltpu.CompilerParams(vmem_limit_bytes=VMEM_LIMIT),
        cost_estimate=pl.CostEstimate(
            flops=2 * head.size * delta.shape[0],
            bytes_accessed=2 * (head.size + delta.size),
            transcendentals=0,
        ),
        name="partial_gradient",
    )(
        core.reshape(1),
        pltpu.with_memory_space_constraint(head, pltpu.HBM),
        pltpu.with_memory_space_constraint(delta, pltpu.VMEM),
    )


def halve(send, keep, vocab_index, vocab_size):
    held = keep + swap_vocab(send, 1, vocab_size).astype(jnp.float32)
    bit = 2
    while held.shape[0] > 1:
        pairs = held.reshape(held.shape[0] // 2, 2, *held.shape[1:])
        mine = (vocab_index // bit) % 2
        send = pick(pairs, 1 - mine, 1).astype(jnp.bfloat16)
        other = swap_vocab(send, bit, vocab_size)
        held = pick(pairs, mine, 1) + other.astype(jnp.float32)
        bit *= 2
    return held[0]


def per_device(hidden, head, teacher, block_ids, counts):
    tok_size = lax.axis_size("tok")
    vocab_size = lax.axis_size("vocab")
    tok_index = lax.axis_index("tok")
    vocab_index = lax.axis_index("vocab")
    token_count = hidden.shape[0]
    rows, column_count = head.shape
    run = vocab_size // tok_size
    half = token_count // 2
    core = vocab_index % 2

    def columns_of(index, first, count):
        return lax.dynamic_slice(hidden, (first, index * rows), (count, rows))

    near = [
        shift_tok(columns_of((tok_index + d) % tok_size, core * half, half), d, tok_size)
        for d in range(1, tok_size)
    ]
    own = columns_of(tok_index, 0, token_count)
    logits = jnp.dot(own, head, preferred_element_type=jnp.float32)
    near, logits = lax.optimization_barrier((near, logits))
    far = [swap_vocab(x, 1, vocab_size) for x in near]
    returned = []
    for d in range(1, tok_size):
        first = shift_tok(
            jnp.dot(near[d - 1], head, preferred_element_type=jnp.float32), -d, tok_size
        )
        second = shift_tok(
            jnp.dot(far[d - 1], head, preferred_element_type=jnp.float32), -d, tok_size
        )
        returned.append((first, second))
    for first, second in returned:
        logits = logits + in_order(first, second, core != 0)

    first_column = vocab_index * column_count
    column_block = (first_column + jnp.arange(column_count, dtype=jnp.int32)) // BLK
    listed = listed_columns(block_ids, counts, column_block, token_count)
    teacher_f = teacher.astype(jnp.float32)
    kept = jnp.where(listed, teacher_f, 0.0)
    local_top = jnp.max(logits, axis=1)
    local_sum = jnp.sum(jnp.exp(logits - local_top[:, None]), axis=1)
    local_mass = jnp.sum(kept, axis=1)
    local_part = jnp.sum(jnp.where(listed, teacher_f * (jnp.log(teacher_f) - logits), 0.0), axis=1)

    stats = gather_vocab(
        jnp.stack([local_top, local_sum, local_mass, local_part]), vocab_index, vocab_size
    )
    tops = stats[:, 0]
    global_top = jnp.max(tops, axis=0)
    total_sum = jnp.sum(stats[:, 1] * jnp.exp(tops - global_top[None, :]), axis=0)
    total_mass, total_part = jnp.sum(stats[:, 2], axis=0), jnp.sum(stats[:, 3], axis=0)
    lse = global_top + jnp.log(total_sum)
    kl = total_part / total_mass - jnp.log(total_mass) + lse
    student = jnp.exp(logits - lse[:, None])
    delta = (loss_scale * (student - kept / total_mass[:, None])).astype(jnp.bfloat16)

    deltas = [delta] + [shift_tok(delta, d, tok_size) for d in range(1, tok_size)]
    sums = [halve(*gradient(core, head, x, run), vocab_index, vocab_size) for x in deltas]
    high = vocab_index // run
    apart = (tok_index - high) % tok_size
    total = jnp.where(apart == 0, sums[0], 0.0)
    sums = jnp.stack([x.astype(jnp.bfloat16) for x in sums])
    for k in range(tok_size):
        pairs = []
        for v in range(vocab_size):
            for t in range(tok_size):
                d = (k + t - v // run) % tok_size
                target = (t * run + v % run) * tok_size + (t - d) % tok_size
                if target != v * tok_size + t:
                    pairs.append((v * tok_size + t, target))
        total = total + lax.ppermute(
            pick(sums, (k + apart) % tok_size), ("vocab", "tok"), pairs
        ).astype(jnp.float32)
    grad_hidden = total.T

    all_delta = jnp.concatenate(deltas, axis=0)
    features = [own] + [in_order(n, f, core != 0) for n, f in zip(near, far)]
    grad_head = lax.dot_general(
        jnp.concatenate(features, axis=0),
        all_delta,
        (((0,), (0,)), ((), ())),
        preferred_element_type=jnp.float32,
    ).astype(jnp.bfloat16)
    return (lse, kl, grad_hidden, grad_head)


def solution(mesh):
    placed = (P("tok", None), P("tok", "vocab"), P("tok", "vocab"), P("tok", None), P("tok"))
    return jax.shard_map(
        per_device,
        mesh=mesh,
        in_specs=placed,
        out_specs=(P("tok"), P("tok"), P("tok", "vocab"), P("tok", "vocab")),
        check_vma=False,
    )
```

```python
import functools

import jax
import jax.numpy as jnp
from jax import lax
from jax.experimental import pallas as pl
from jax.experimental.pallas import tpu as pltpu
from jax.sharding import PartitionSpec as P

BLK = 512


loss_scale = 1024.0
VMEM_LIMIT = 16 << 20


def shift_tok(x, offset, size):
    return lax.ppermute(x, "tok", [(i, (i + offset) % size) for i in range(size)])


def swap_vocab(x, bit, size):
    return lax.ppermute(x, "vocab", [(i, i ^ bit) for i in range(size)])


def pick(x, index, axis=0):
    return lax.dynamic_index_in_dim(x, index, axis, keepdims=False)


def listed_columns(block_ids, counts, column_block, token_count):
    live_slot = jnp.arange(block_ids.shape[1], dtype=jnp.int32)[None, :] < counts[:, None]
    block_hit = jnp.any(
        (block_ids[:, :, None] == column_block[None, None, :]) & live_slot[:, :, None], axis=1
    )
    token_blocks = block_hit.shape[0]
    width = column_block.shape[0]
    return jnp.broadcast_to(
        block_hit[:, None, :], (token_blocks, token_count // token_blocks, width)
    ).reshape(token_count, width)


def in_order(mine, other, upper):
    return jnp.concatenate(
        [jnp.where(upper, other, mine), jnp.where(upper, mine, other)], axis=0
    )


def gather_vocab(stats, vocab_index, size):
    gathered = stats[None]
    bit = 1
    while bit < size:
        other = swap_vocab(gathered, bit, size)
        gathered = in_order(gathered, other, (vocab_index & bit) != 0)
        bit *= 2
    return gathered


def write_pieces(k, head_rows, delta_ref, upper, send_ref, keep_ref):
    rows = send_ref.shape[1]
    block = lax.dot_general(
        head_rows, delta_ref[...], (((1,), (1,)), ((), ())), preferred_element_type=jnp.float32
    )
    low, high = block[:rows], block[rows:]
    send_ref[k] = jnp.where(upper, low, high).astype(jnp.bfloat16)
    keep_ref[k] = jnp.where(upper, high, low)


def first_gradient_kernel(core_ref, head_ref, delta_ref, send_ref, keep_ref, held_ref, sems):
    upper = core_ref[0] == 1
    pairs, rows, _ = send_ref.shape
    parts = [pl.ds(2 * k * rows, 2 * rows) for k in range(pairs)]
    copies = [
        pltpu.make_async_copy(head_ref.at[part], held_ref.at[part], sems.at[k])
        for k, part in enumerate(parts)
    ]
    for copy in copies[:2]:
        copy.start()
    for k in range(pairs):
        copies[k].wait()
        if k + 2 < pairs:
            copies[k + 2].start()
        head_rows = held_ref[2 * k * rows : 2 * (k + 1) * rows, :]
        write_pieces(k, head_rows, delta_ref, upper, send_ref, keep_ref)


def later_gradient_kernel(core_ref, head_ref, delta_ref, send_ref, keep_ref):
    upper = core_ref[0] == 1
    pairs, rows, _ = send_ref.shape
    for k in range(pairs):
        head_rows = head_ref[2 * k * rows : 2 * (k + 1) * rows, :]
        write_pieces(k, head_rows, delta_ref, upper, send_ref, keep_ref)


def gradient(core, head, delta, run, first):
    rows = head.shape[0] // run
    shape = (run // 2, rows, delta.shape[0])
    in_vmem = pl.BlockSpec(memory_space=pltpu.VMEM)
    space = pltpu.HBM if first else pltpu.VMEM
    outs = (pltpu.VMEM(shape, jnp.bfloat16), pltpu.VMEM(shape, jnp.float32))
    if first:
        outs = outs + (pltpu.VMEM(head.shape, head.dtype),)
    return pl.pallas_call(
        first_gradient_kernel if first else later_gradient_kernel,
        out_shape=outs,
        in_specs=[
            pl.BlockSpec(memory_space=pltpu.SMEM),
            pl.BlockSpec(memory_space=space),
            in_vmem,
        ],
        out_specs=(in_vmem,) * len(outs),
        scratch_shapes=[pltpu.SemaphoreType.DMA((run // 2,))] if first else [],
        compiler_params=pltpu.CompilerParams(vmem_limit_bytes=VMEM_LIMIT),
        cost_estimate=pl.CostEstimate(
            flops=2 * head.size * delta.shape[0],
            bytes_accessed=2 * (head.size + delta.size),
            transcendentals=0,
        ),
        name="partial_gradient",
    )(
        core.reshape(1),
        pltpu.with_memory_space_constraint(head, space),
        pltpu.with_memory_space_constraint(delta, pltpu.VMEM),
    )


def head_gradient_kernel(steps, start, width, *refs):
    features_ref, delta_ref, out_ref, held_ref, sems = refs[0], refs[1], *refs[-3:]
    copies = []
    for k in range(steps):
        block = lax.dot_general(
            features_ref[:, start + k * width : start + (k + 1) * width],
            delta_ref[...],
            (((0,), (0,)), ((), ())),
            preferred_element_type=jnp.float32,
        )
        held_ref[k] = block.astype(jnp.bfloat16)
        copy = pltpu.make_async_copy(
            held_ref.at[k], out_ref.at[pl.ds(start + k * width, width)], sems.at[k]
        )
        copy.start()
        copies.append(copy)
    for copy in copies:
        copy.wait()


def head_gradient(features, delta, out, start, steps, width):
    columns = delta.shape[1]
    in_vmem = pl.BlockSpec(memory_space=pltpu.VMEM)
    in_hbm = pl.BlockSpec(memory_space=pltpu.HBM)
    return pl.pallas_call(
        functools.partial(head_gradient_kernel, steps, start, width),
        out_shape=jax.ShapeDtypeStruct((features.shape[1], columns), jnp.bfloat16),
        in_specs=[in_vmem, in_vmem] + ([] if out is None else [in_hbm]),
        out_specs=in_hbm,
        scratch_shapes=[
            pltpu.VMEM((steps, width, columns), jnp.bfloat16),
            pltpu.SemaphoreType.DMA((steps,)),
        ],
        input_output_aliases={} if out is None else {2: 0},
        compiler_params=pltpu.CompilerParams(vmem_limit_bytes=VMEM_LIMIT),
        cost_estimate=pl.CostEstimate(
            flops=2 * steps * width * delta.size,
            bytes_accessed=2 * (features.size + delta.size + steps * width * columns),
            transcendentals=0,
        ),
        name="head_gradient",
    )(features, delta, *([] if out is None else [out]))


def per_device(hidden, head, teacher, block_ids, counts):
    tok_size = lax.axis_size("tok")
    vocab_size = lax.axis_size("vocab")
    tok_index = lax.axis_index("tok")
    vocab_index = lax.axis_index("vocab")
    token_count = hidden.shape[0]
    rows, column_count = head.shape
    run = vocab_size // tok_size
    half = token_count // 2
    core = vocab_index % 2

    def columns_of(index, first, count):
        return lax.dynamic_slice(hidden, (first, index * rows), (count, rows))

    near = [
        shift_tok(columns_of((tok_index + d) % tok_size, core * half, half), d, tok_size)
        for d in range(1, tok_size)
    ]
    own = columns_of(tok_index, 0, token_count)
    logits = jnp.dot(own, head, preferred_element_type=jnp.float32)
    near, logits = lax.optimization_barrier((near, logits))
    far = [swap_vocab(x, 1, vocab_size) for x in near]
    returned = []
    for d in range(1, tok_size):
        first = shift_tok(
            jnp.dot(near[d - 1], head, preferred_element_type=jnp.float32), -d, tok_size
        )
        second = shift_tok(
            jnp.dot(far[d - 1], head, preferred_element_type=jnp.float32), -d, tok_size
        )
        returned.append((first, second))
    features = [own] + [in_order(n, f, core != 0) for n, f in zip(near, far)]
    all_features = jnp.concatenate(features, axis=0)
    returned, all_features = lax.optimization_barrier((returned, all_features))
    for first, second in returned:
        logits = logits + in_order(first, second, core != 0)

    first_column = vocab_index * column_count
    column_block = (first_column + jnp.arange(column_count, dtype=jnp.int32)) // BLK
    listed = listed_columns(block_ids, counts, column_block, token_count)
    teacher_f = teacher.astype(jnp.float32)
    kept = jnp.where(listed, teacher_f, 0.0)
    local_top = jnp.max(logits, axis=1)
    local_sum = jnp.sum(jnp.exp(logits - local_top[:, None]), axis=1)
    local_mass = jnp.sum(kept, axis=1)
    local_part = jnp.sum(jnp.where(listed, teacher_f * (jnp.log(teacher_f) - logits), 0.0), axis=1)

    stats = gather_vocab(
        jnp.stack([local_top, local_sum, local_mass, local_part]), vocab_index, vocab_size
    )
    tops = stats[:, 0]
    global_top = jnp.max(tops, axis=0)
    total_sum = jnp.sum(stats[:, 1] * jnp.exp(tops - global_top[None, :]), axis=0)
    total_mass, total_part = jnp.sum(stats[:, 2], axis=0), jnp.sum(stats[:, 3], axis=0)
    lse = global_top + jnp.log(total_sum)
    kl = total_part / total_mass - jnp.log(total_mass) + lse
    student = jnp.exp(logits - lse[:, None])
    delta = (loss_scale * (student - kept / total_mass[:, None])).astype(jnp.bfloat16)

    deltas = [delta] + [shift_tok(delta, d, tok_size) for d in range(1, tok_size)]
    send, keep, head_here = gradient(core, head, delta, run, True)
    other = swap_vocab(send, 1, vocab_size)
    state = [(keep, other)]
    for x in deltas[1:]:
        send, keep = gradient(core, head_here, x, run, False)
        state[0], send = lax.optimization_barrier((state[0], send))
        state.append((keep, swap_vocab(send, 1, vocab_size)))
    all_delta = jnp.concatenate(deltas, axis=0)

    width = 256 if rows % 256 == 0 else rows
    chunks = rows // width
    shares = [(chunks + 1) // 2, chunks // 4]
    done = 0
    grad_head = None
    bit = 2
    held = jnp.stack([keep + other.astype(jnp.float32) for keep, other in state])
    while bit < run:
        pairs = held.reshape(tok_size, held.shape[1] // 2, 2, *held.shape[2:])
        mine = (vocab_index // bit) % 2
        send = pick(pairs, 1 - mine, 2).astype(jnp.bfloat16)
        send, all_delta = lax.optimization_barrier((send, all_delta))
        other = swap_vocab(send, bit, vocab_size)
        share = shares.pop(0) if shares else 0
        if share:
            grad_head = head_gradient(
                all_features, all_delta, grad_head, done * width, share, width
            )
            done += share
            other, grad_head = lax.optimization_barrier((other, grad_head))
        held = pick(pairs, mine, 2) + other.astype(jnp.float32)
        bit *= 2
    sums = held[:, 0]
    high = vocab_index // run
    apart = (tok_index - high) % tok_size
    total = jnp.where(apart == 0, sums[0], 0.0)
    sums = sums.astype(jnp.bfloat16)
    sends = [pick(sums, (k + apart) % tok_size) for k in range(tok_size)]
    sends, all_delta = lax.optimization_barrier((sends, all_delta))
    for k in range(tok_size):
        pairs = []
        for v in range(vocab_size):
            for t in range(tok_size):
                d = (k + t - v // run) % tok_size
                target = (t * run + v % run) * tok_size + (t - d) % tok_size
                if target != v * tok_size + t:
                    pairs.append((v * tok_size + t, target))
        total = total + lax.ppermute(sends[k], ("vocab", "tok"), pairs).astype(jnp.float32)
    grad_hidden = total.T
    if done < chunks:
        grad_head = head_gradient(
            all_features, all_delta, grad_head, done * width, chunks - done, width
        )
    return (lse, kl, grad_hidden, grad_head)


def solution(mesh):
    placed = (P("tok", None), P("tok", "vocab"), P("tok", "vocab"), P("tok", None), P("tok"))
    return jax.shard_map(
        per_device,
        mesh=mesh,
        in_specs=placed,
        out_specs=(P("tok"), P("tok"), P("tok", "vocab"), P("tok", "vocab")),
        check_vma=False,
    )
```

```python
import functools

import jax
import jax.numpy as jnp
from jax import lax
from jax.experimental import pallas as pl
from jax.experimental.pallas import tpu as pltpu
from jax.sharding import PartitionSpec as P

BLK = 512


loss_scale = 1024.0
VMEM_LIMIT = 16 << 20


def shift_tok(x, offset, size):
    return lax.ppermute(x, "tok", [(i, (i + offset) % size) for i in range(size)])


def swap_vocab(x, bit, size):
    return lax.ppermute(x, "vocab", [(i, i ^ bit) for i in range(size)])


def in_order(mine, other, upper):
    return jnp.concatenate(
        [jnp.where(upper, other, mine), jnp.where(upper, mine, other)], axis=0
    )


def gather_vocab(stats, upper, size):
    gathered = stats[None]
    for i, flag in enumerate(upper):
        gathered = in_order(gathered, swap_vocab(gathered, 1 << i, size), flag)
    return gathered


def own_kernel(own_ref, head_ref, out_ref, held_ref, sems):
    steps = sems.shape[0]
    depth = head_ref.shape[0] // steps
    parts = [pl.ds(k * depth, depth) for k in range(steps)]
    copies = [
        pltpu.make_async_copy(head_ref.at[part], held_ref.at[part], sems.at[k])
        for k, part in enumerate(parts)
    ]
    for copy in copies[:2]:
        copy.start()
    for k in range(steps):
        copies[k].wait()
        if k + 2 < steps:
            copies[k + 2].start()
        product = jnp.dot(
            own_ref[:, k * depth : (k + 1) * depth],
            held_ref[k * depth : (k + 1) * depth, :],
            preferred_element_type=jnp.float32,
        )
        out_ref[...] = product if k == 0 else out_ref[...] + product


def own_product(own, head):
    steps = 7 if head.shape[0] % (7 * 128) == 0 else 1
    in_vmem = pl.BlockSpec(memory_space=pltpu.VMEM)
    return pl.pallas_call(
        own_kernel,
        out_shape=(
            pltpu.VMEM((own.shape[0], head.shape[1]), jnp.float32),
            pltpu.VMEM(head.shape, head.dtype),
        ),
        in_specs=[in_vmem, pl.BlockSpec(memory_space=pltpu.HBM)],
        out_specs=(in_vmem, in_vmem),
        scratch_shapes=[pltpu.SemaphoreType.DMA((steps,))],
        compiler_params=pltpu.CompilerParams(vmem_limit_bytes=VMEM_LIMIT),
        cost_estimate=pl.CostEstimate(
            flops=2 * head.size * own.shape[0],
            bytes_accessed=2 * (head.size + own.size),
            transcendentals=0,
        ),
        name="own_product",
    )(own, pltpu.with_memory_space_constraint(head, pltpu.HBM))


def write_pieces(k, head_rows, delta_ref, upper, send_ref, keep_ref):
    rows = send_ref.shape[1]
    block = lax.dot_general(
        head_rows, delta_ref[...], (((1,), (1,)), ((), ())), preferred_element_type=jnp.float32
    )
    low, high = block[:rows], block[rows:]
    send_ref[k] = jnp.where(upper, low, high).astype(jnp.bfloat16)
    keep_ref[k] = jnp.where(upper, high, low)


def first_gradient_kernel(core_ref, head_ref, delta_ref, send_ref, keep_ref, held_ref, sems):
    upper = core_ref[0] == 1
    pairs, rows, _ = send_ref.shape
    parts = [pl.ds(2 * k * rows, 2 * rows) for k in range(pairs)]
    copies = [
        pltpu.make_async_copy(head_ref.at[part], held_ref.at[part], sems.at[k])
        for k, part in enumerate(parts)
    ]
    for copy in copies[:2]:
        copy.start()
    for k in range(pairs):
        copies[k].wait()
        if k + 2 < pairs:
            copies[k + 2].start()
        head_rows = held_ref[2 * k * rows : 2 * (k + 1) * rows, :]
        write_pieces(k, head_rows, delta_ref, upper, send_ref, keep_ref)


def later_gradient_kernel(core_ref, head_ref, delta_ref, send_ref, keep_ref):
    upper = core_ref[0] == 1
    pairs, rows, _ = send_ref.shape
    for k in range(pairs):
        head_rows = head_ref[2 * k * rows : 2 * (k + 1) * rows, :]
        write_pieces(k, head_rows, delta_ref, upper, send_ref, keep_ref)


def gradient(core, head, delta, run, first):
    rows = head.shape[0] // run
    shape = (run // 2, rows, delta.shape[0])
    in_vmem = pl.BlockSpec(memory_space=pltpu.VMEM)
    space = pltpu.HBM if first else pltpu.VMEM
    outs = (pltpu.VMEM(shape, jnp.bfloat16), pltpu.VMEM(shape, jnp.float32))
    if first:
        outs = outs + (pltpu.VMEM(head.shape, head.dtype),)
    return pl.pallas_call(
        first_gradient_kernel if first else later_gradient_kernel,
        out_shape=outs,
        in_specs=[
            pl.BlockSpec(memory_space=pltpu.SMEM),
            pl.BlockSpec(memory_space=space),
            in_vmem,
        ],
        out_specs=(in_vmem,) * len(outs),
        scratch_shapes=[pltpu.SemaphoreType.DMA((run // 2,))] if first else [],
        compiler_params=pltpu.CompilerParams(vmem_limit_bytes=VMEM_LIMIT),
        cost_estimate=pl.CostEstimate(
            flops=2 * head.size * delta.shape[0],
            bytes_accessed=2 * (head.size + delta.size),
            transcendentals=0,
        ),
        name="partial_gradient",
    )(
        core,
        pltpu.with_memory_space_constraint(head, space),
        pltpu.with_memory_space_constraint(delta, pltpu.VMEM),
    )


def head_gradient_kernel(steps, start, width, *refs):
    features_ref, delta_ref, out_ref, held_ref, sems = refs[0], refs[1], *refs[-3:]
    copies = []
    for k in range(steps):
        block = lax.dot_general(
            features_ref[:, start + k * width : start + (k + 1) * width],
            delta_ref[...],
            (((0,), (0,)), ((), ())),
            preferred_element_type=jnp.float32,
        )
        held_ref[k] = block.astype(jnp.bfloat16)
        copy = pltpu.make_async_copy(
            held_ref.at[k], out_ref.at[pl.ds(start + k * width, width)], sems.at[k]
        )
        copy.start()
        copies.append(copy)
    for copy in copies:
        copy.wait()


def head_gradient(features, delta, out, start, steps, width):
    columns = delta.shape[1]
    in_vmem = pl.BlockSpec(memory_space=pltpu.VMEM)
    in_hbm = pl.BlockSpec(memory_space=pltpu.HBM)
    return pl.pallas_call(
        functools.partial(head_gradient_kernel, steps, start, width),
        out_shape=jax.ShapeDtypeStruct((features.shape[1], columns), jnp.bfloat16),
        in_specs=[in_vmem, in_vmem] + ([] if out is None else [in_hbm]),
        out_specs=in_hbm,
        scratch_shapes=[
            pltpu.VMEM((steps, width, columns), jnp.bfloat16),
            pltpu.SemaphoreType.DMA((steps,)),
        ],
        input_output_aliases={} if out is None else {2: 0},
        compiler_params=pltpu.CompilerParams(vmem_limit_bytes=VMEM_LIMIT),
        cost_estimate=pl.CostEstimate(
            flops=2 * steps * width * delta.size,
            bytes_accessed=2 * (features.size + delta.size + steps * width * columns),
            transcendentals=0,
        ),
        name="head_gradient",
    )(features, delta, *([] if out is None else [out]))


def per_device(hidden, head, teacher, block_ids, counts):
    tok_size = lax.axis_size("tok")
    vocab_size = lax.axis_size("vocab")
    tok_index = lax.axis_index("tok")
    vocab_index = lax.axis_index("vocab")
    token_count = hidden.shape[0]
    rows, column_count = head.shape
    run = vocab_size // tok_size
    half = token_count // 2
    core = vocab_index & 1

    def columns_of(index, first, count):
        return lax.dynamic_slice(hidden, (first, index * rows), (count, rows))

    near = [
        shift_tok(columns_of(lax.rem(tok_index + d, tok_size), core * half, half), d, tok_size)
        for d in range(1, tok_size)
    ]
    own = columns_of(tok_index, 0, token_count)
    upper = []
    while 1 << len(upper) < vocab_size:
        upper.append((vocab_index & (1 << len(upper))) != 0)
    high = lax.div(vocab_index, run)
    apart = lax.rem(tok_index + tok_size - high, tok_size)
    apart_is = [apart == d for d in range(tok_size)]
    first_column = vocab_index * column_count
    column_block = (first_column + jnp.arange(column_count, dtype=jnp.int32)) // BLK
    live_slot = jnp.arange(block_ids.shape[1], dtype=jnp.int32)[None, :] < counts[:, None]
    block_hit = jnp.any(
        (block_ids[:, :, None] == column_block[None, None, :]) & live_slot[:, :, None], axis=1
    )
    core_word = core.reshape(1)
    own, upper, apart_is, block_hit, core_word = lax.optimization_barrier(
        (own, upper, apart_is, block_hit, core_word)
    )
    logits, head_here = own_product(own, head)
    near, logits = lax.optimization_barrier((near, logits))
    far = [swap_vocab(x, 1, vocab_size) for x in near]
    returned = []
    for d in range(1, tok_size):
        first = shift_tok(
            jnp.dot(near[d - 1], head_here, preferred_element_type=jnp.float32), -d, tok_size
        )
        second = shift_tok(
            jnp.dot(far[d - 1], head_here, preferred_element_type=jnp.float32), -d, tok_size
        )
        returned.append((first, second))
    features = [own] + [in_order(n, f, upper[0]) for n, f in zip(near, far)]
    all_features = jnp.concatenate(features, axis=0)
    returned, all_features = lax.optimization_barrier((returned, all_features))
    for first, second in returned:
        logits = logits + in_order(first, second, upper[0])

    blocks = block_hit.shape[0]
    listed = jnp.broadcast_to(
        block_hit[:, None, :], (blocks, token_count // blocks, column_count)
    ).reshape(token_count, column_count)
    teacher_f = teacher.astype(jnp.float32)
    kept = jnp.where(listed, teacher_f, 0.0)
    local_top = jnp.max(logits, axis=1)
    local_sum = jnp.sum(jnp.exp(logits - local_top[:, None]), axis=1)
    local_mass = jnp.sum(kept, axis=1)
    local_part = jnp.sum(jnp.where(listed, teacher_f * (jnp.log(teacher_f) - logits), 0.0), axis=1)

    stats = gather_vocab(
        jnp.stack([local_top, local_sum, local_mass, local_part]), upper, vocab_size
    )
    tops = stats[:, 0]
    global_top = jnp.max(tops, axis=0)
    total_sum = jnp.sum(stats[:, 1] * jnp.exp(tops - global_top[None, :]), axis=0)
    total_mass, total_part = jnp.sum(stats[:, 2], axis=0), jnp.sum(stats[:, 3], axis=0)
    lse = global_top + jnp.log(total_sum)
    kl = total_part / total_mass - jnp.log(total_mass) + lse
    student = jnp.exp(logits - lse[:, None])
    delta = (loss_scale * (student - kept / total_mass[:, None])).astype(jnp.bfloat16)

    deltas = [delta] + [shift_tok(delta, d, tok_size) for d in range(1, tok_size)]
    send, keep, head_here = gradient(core_word, head, delta, run, True)
    other = swap_vocab(send, 1, vocab_size)
    state = [(keep, other)]
    for x in deltas[1:]:
        send, keep = gradient(core_word, head_here, x, run, False)
        state[0], send = lax.optimization_barrier((state[0], send))
        state.append((keep, swap_vocab(send, 1, vocab_size)))
    all_delta = jnp.concatenate(deltas, axis=0)

    width = 256 if rows % 256 == 0 else rows
    chunks = rows // width
    shares = [(chunks + 1) // 2, chunks // 4]
    done = 0
    grad_head = None
    held = jnp.stack([keep + other.astype(jnp.float32) for keep, other in state])
    for i in range(1, len(upper)):
        if held.shape[1] == 1:
            break
        pairs = held.reshape(tok_size, held.shape[1] // 2, 2, *held.shape[2:])
        low, high = pairs[:, :, 0], pairs[:, :, 1]
        send = jnp.where(upper[i], low, high).astype(jnp.bfloat16)
        send, all_delta = lax.optimization_barrier((send, all_delta))
        other = swap_vocab(send, 1 << i, vocab_size)
        share = shares.pop(0) if shares else 0
        if share:
            grad_head = head_gradient(
                all_features, all_delta, grad_head, done * width, share, width
            )
            done += share
            other, grad_head = lax.optimization_barrier((other, grad_head))
        held = jnp.where(upper[i], high, low) + other.astype(jnp.float32)
    sums = held[:, 0]
    total = jnp.where(apart_is[0], sums[0], 0.0)
    sums = sums.astype(jnp.bfloat16)
    sends = []
    for k in range(tok_size):
        send = sums[k]
        for d in range(1, tok_size):
            send = jnp.where(apart_is[d], sums[(k + d) % tok_size], send)
        sends.append(send)
    sends, all_delta = lax.optimization_barrier((sends, all_delta))
    for k in range(tok_size):
        pairs = []
        for v in range(vocab_size):
            for t in range(tok_size):
                d = (k + t - v // run) % tok_size
                target = (t * run + v % run) * tok_size + (t - d) % tok_size
                if target != v * tok_size + t:
                    pairs.append((v * tok_size + t, target))
        total = total + lax.ppermute(sends[k], ("vocab", "tok"), pairs).astype(jnp.float32)
    grad_hidden = total.T
    if done < chunks:
        grad_head = head_gradient(
            all_features, all_delta, grad_head, done * width, chunks - done, width
        )
    return (lse, kl, grad_hidden, grad_head)


def solution(mesh):
    placed = (P("tok", None), P("tok", "vocab"), P("tok", "vocab"), P("tok", None), P("tok"))
    return jax.shard_map(
        per_device,
        mesh=mesh,
        in_specs=placed,
        out_specs=(P("tok"), P("tok"), P("tok", "vocab"), P("tok", "vocab")),
        check_vma=False,
    )
```

```python
import functools

import jax
import jax.numpy as jnp
from jax import lax
from jax.experimental import pallas as pl
from jax.experimental.pallas import tpu as pltpu
from jax.sharding import PartitionSpec as P

BLK = 512


loss_scale = 1024.0
VMEM_LIMIT = 16 << 20


def shift_tok(x, offset, size):
    return lax.ppermute(x, "tok", [(i, (i + offset) % size) for i in range(size)])


def swap_vocab(x, bit, size):
    return lax.ppermute(x, "vocab", [(i, i ^ bit) for i in range(size)])


def in_order(mine, other, upper):
    return jnp.concatenate(
        [jnp.where(upper, other, mine), jnp.where(upper, mine, other)], axis=0
    )


def gather_vocab(stats, upper, size):
    gathered = stats[None]
    for i, flag in enumerate(upper):
        gathered = in_order(gathered, swap_vocab(gathered, 1 << i, size), flag)
    return gathered


def load_kernel(head_ref, held_ref, sems):
    steps = sems.shape[0]
    depth = head_ref.shape[0] // steps
    parts = [pl.ds(k * depth, depth) for k in range(steps)]
    copies = [
        pltpu.make_async_copy(head_ref.at[part], held_ref.at[part], sems.at[k])
        for k, part in enumerate(parts)
    ]
    for copy in copies:
        copy.start()
    for copy in copies:
        copy.wait()


def load(head):
    steps = 4
    return pl.pallas_call(
        load_kernel,
        out_shape=pltpu.VMEM(head.shape, head.dtype),
        in_specs=[pl.BlockSpec(memory_space=pltpu.HBM)],
        out_specs=pl.BlockSpec(memory_space=pltpu.VMEM),
        scratch_shapes=[pltpu.SemaphoreType.DMA((steps,))],
        compiler_params=pltpu.CompilerParams(vmem_limit_bytes=VMEM_LIMIT),
        cost_estimate=pl.CostEstimate(
            flops=0, bytes_accessed=4 * head.size, transcendentals=0
        ),
        name="load_head",
    )(pltpu.with_memory_space_constraint(head, pltpu.HBM))


def write_pieces(k, head_rows, delta_ref, upper, send_ref, keep_ref):
    rows = send_ref.shape[1]
    block = lax.dot_general(
        head_rows, delta_ref[...], (((1,), (1,)), ((), ())), preferred_element_type=jnp.float32
    )
    low, high = block[:rows], block[rows:]
    send_ref[k] = jnp.where(upper, low, high).astype(jnp.bfloat16)
    keep_ref[k] = jnp.where(upper, high, low)


def first_gradient_kernel(core_ref, head_ref, delta_ref, send_ref, keep_ref, held_ref, sems):
    upper = core_ref[0] == 1
    pairs, rows, _ = send_ref.shape
    parts = [pl.ds(2 * k * rows, 2 * rows) for k in range(pairs)]
    copies = [
        pltpu.make_async_copy(head_ref.at[part], held_ref.at[part], sems.at[k])
        for k, part in enumerate(parts)
    ]
    for copy in copies[:2]:
        copy.start()
    for k in range(pairs):
        copies[k].wait()
        if k + 2 < pairs:
            copies[k + 2].start()
        head_rows = held_ref[2 * k * rows : 2 * (k + 1) * rows, :]
        write_pieces(k, head_rows, delta_ref, upper, send_ref, keep_ref)


def later_gradient_kernel(core_ref, head_ref, delta_ref, send_ref, keep_ref):
    upper = core_ref[0] == 1
    pairs, rows, _ = send_ref.shape
    for k in range(pairs):
        head_rows = head_ref[2 * k * rows : 2 * (k + 1) * rows, :]
        write_pieces(k, head_rows, delta_ref, upper, send_ref, keep_ref)


def gradient(core, head, delta, run, first):
    rows = head.shape[0] // run
    shape = (run // 2, rows, delta.shape[0])
    in_vmem = pl.BlockSpec(memory_space=pltpu.VMEM)
    space = pltpu.HBM if first else pltpu.VMEM
    outs = (pltpu.VMEM(shape, jnp.bfloat16), pltpu.VMEM(shape, jnp.float32))
    if first:
        outs = outs + (pltpu.VMEM(head.shape, head.dtype),)
    return pl.pallas_call(
        first_gradient_kernel if first else later_gradient_kernel,
        out_shape=outs,
        in_specs=[
            pl.BlockSpec(memory_space=pltpu.SMEM),
            pl.BlockSpec(memory_space=space),
            in_vmem,
        ],
        out_specs=(in_vmem,) * len(outs),
        scratch_shapes=[pltpu.SemaphoreType.DMA((run // 2,))] if first else [],
        compiler_params=pltpu.CompilerParams(vmem_limit_bytes=VMEM_LIMIT),
        cost_estimate=pl.CostEstimate(
            flops=2 * head.size * delta.shape[0],
            bytes_accessed=2 * (head.size + delta.size),
            transcendentals=0,
        ),
        name="partial_gradient",
    )(
        core,
        pltpu.with_memory_space_constraint(head, space),
        pltpu.with_memory_space_constraint(delta, pltpu.VMEM),
    )


def head_gradient_kernel(steps, start, width, *refs):
    features_ref, delta_ref, out_ref, held_ref, sems = refs[0], refs[1], *refs[-3:]
    copies = []
    for k in range(steps):
        block = lax.dot_general(
            features_ref[:, start + k * width : start + (k + 1) * width],
            delta_ref[...],
            (((0,), (0,)), ((), ())),
            preferred_element_type=jnp.float32,
        )
        held_ref[k] = block.astype(jnp.bfloat16)
        copy = pltpu.make_async_copy(
            held_ref.at[k], out_ref.at[pl.ds(start + k * width, width)], sems.at[k]
        )
        copy.start()
        copies.append(copy)
    for copy in copies:
        copy.wait()


def head_gradient(features, delta, out, start, steps, width):
    columns = delta.shape[1]
    in_vmem = pl.BlockSpec(memory_space=pltpu.VMEM)
    in_hbm = pl.BlockSpec(memory_space=pltpu.HBM)
    return pl.pallas_call(
        functools.partial(head_gradient_kernel, steps, start, width),
        out_shape=jax.ShapeDtypeStruct((features.shape[1], columns), jnp.bfloat16),
        in_specs=[in_vmem, in_vmem] + ([] if out is None else [in_hbm]),
        out_specs=in_hbm,
        scratch_shapes=[
            pltpu.VMEM((steps, width, columns), jnp.bfloat16),
            pltpu.SemaphoreType.DMA((steps,)),
        ],
        input_output_aliases={} if out is None else {2: 0},
        compiler_params=pltpu.CompilerParams(vmem_limit_bytes=VMEM_LIMIT),
        cost_estimate=pl.CostEstimate(
            flops=2 * steps * width * delta.size,
            bytes_accessed=2 * (features.size + delta.size + steps * width * columns),
            transcendentals=0,
        ),
        name="head_gradient",
    )(features, delta, *([] if out is None else [out]))


def per_device(hidden, head, teacher, block_ids, counts):
    tok_size = lax.axis_size("tok")
    vocab_size = lax.axis_size("vocab")
    tok_index = lax.axis_index("tok")
    vocab_index = lax.axis_index("vocab")
    token_count = hidden.shape[0]
    rows, column_count = head.shape
    run = vocab_size // tok_size
    half = token_count // 2
    core = vocab_index & 1

    def columns_of(index, first, count):
        return lax.dynamic_slice(hidden, (first, index * rows), (count, rows))

    near = [
        shift_tok(columns_of(lax.rem(tok_index + d, tok_size), core * half, half), d, tok_size)
        for d in range(1, tok_size)
    ]
    upper = []
    while 1 << len(upper) < vocab_size:
        upper.append((vocab_index & (1 << len(upper))) != 0)
    high = lax.div(vocab_index, run)
    apart = lax.rem(tok_index + tok_size - high, tok_size)
    apart_is = [apart == d for d in range(tok_size)]
    first_column = vocab_index * column_count
    column_block = (first_column + jnp.arange(column_count, dtype=jnp.int32)) // BLK
    live_slot = jnp.arange(block_ids.shape[1], dtype=jnp.int32)[None, :] < counts[:, None]
    core_word = core.reshape(1)
    own = columns_of(tok_index, 0, token_count)
    own, head, upper, apart_is, column_block, live_slot, core_word = lax.optimization_barrier(
        (own, head, upper, apart_is, column_block, live_slot, core_word)
    )
    head_here = load(head)
    near, head_here = lax.optimization_barrier((near, head_here))
    far = [swap_vocab(x, 1, vocab_size) for x in near]
    returned = []
    for d in range(1, tok_size):
        first = shift_tok(
            jnp.dot(near[d - 1], head_here, preferred_element_type=jnp.float32), -d, tok_size
        )
        second = shift_tok(
            jnp.dot(far[d - 1], head_here, preferred_element_type=jnp.float32), -d, tok_size
        )
        returned.append((first, second))
    logits = jnp.dot(own, head_here, preferred_element_type=jnp.float32)
    block_hit = jnp.any(
        (block_ids[:, :, None] == column_block[None, None, :]) & live_slot[:, :, None], axis=1
    )
    features = [own] + [in_order(n, f, upper[0]) for n, f in zip(near, far)]
    all_features = jnp.concatenate(features, axis=0)
    returned, all_features, logits, block_hit = lax.optimization_barrier(
        (returned, all_features, logits, block_hit)
    )
    for first, second in returned:
        logits = logits + in_order(first, second, upper[0])

    blocks = block_hit.shape[0]
    listed = jnp.broadcast_to(
        block_hit[:, None, :], (blocks, token_count // blocks, column_count)
    ).reshape(token_count, column_count)
    teacher_f = teacher.astype(jnp.float32)
    kept = jnp.where(listed, teacher_f, 0.0)
    local_top = jnp.max(logits, axis=1)
    local_sum = jnp.sum(jnp.exp(logits - local_top[:, None]), axis=1)
    local_mass = jnp.sum(kept, axis=1)
    local_part = jnp.sum(jnp.where(listed, teacher_f * (jnp.log(teacher_f) - logits), 0.0), axis=1)

    stats = gather_vocab(
        jnp.stack([local_top, local_sum, local_mass, local_part]), upper, vocab_size
    )
    tops = stats[:, 0]
    global_top = jnp.max(tops, axis=0)
    total_sum = jnp.sum(stats[:, 1] * jnp.exp(tops - global_top[None, :]), axis=0)
    total_mass, total_part = jnp.sum(stats[:, 2], axis=0), jnp.sum(stats[:, 3], axis=0)
    lse = global_top + jnp.log(total_sum)
    kl = total_part / total_mass - jnp.log(total_mass) + lse
    student = jnp.exp(logits - lse[:, None])
    delta = (loss_scale * (student - kept / total_mass[:, None])).astype(jnp.bfloat16)

    deltas = [delta] + [shift_tok(delta, d, tok_size) for d in range(1, tok_size)]
    send, keep, head_here = gradient(core_word, head, delta, run, True)
    other = swap_vocab(send, 1, vocab_size)
    state = [(keep, other)]
    for x in deltas[1:]:
        send, keep = gradient(core_word, head_here, x, run, False)
        state[0], send = lax.optimization_barrier((state[0], send))
        state.append((keep, swap_vocab(send, 1, vocab_size)))
    all_delta = jnp.concatenate(deltas, axis=0)

    width = 256 if rows % 256 == 0 else rows
    chunks = rows // width
    held = jnp.stack([keep + other.astype(jnp.float32) for keep, other in state], axis=1)
    pieces = held.shape[0]
    places = [i for i in range(1, len(upper)) if 1 << i < run]
    taken = []
    for offset in range(pieces):
        options = [held[j ^ offset] for j in range(pieces)]
        for i in places:
            options = [
                jnp.where(upper[i], high, low) for low, high in zip(options[::2], options[1::2])
            ]
        taken.append(options[0])
    sends = [x.astype(jnp.bfloat16) for x in taken[1:]]
    sends, all_delta = lax.optimization_barrier((sends, all_delta))
    others = [swap_vocab(x, 2 * (i + 1), vocab_size) for i, x in enumerate(sends)]
    done = (chunks + 1) // 2
    grad_head = head_gradient(all_features, all_delta, None, 0, done, width)
    others, grad_head = lax.optimization_barrier((others, grad_head))
    sums = taken[0]
    for other in others:
        sums = sums + other.astype(jnp.float32)
    total = jnp.where(apart_is[0], sums[0], 0.0)
    sums = sums.astype(jnp.bfloat16)
    sends = []
    for k in range(tok_size):
        send = sums[k]
        for d in range(1, tok_size):
            send = jnp.where(apart_is[d], sums[(k + d) % tok_size], send)
        sends.append(send)
    sends, all_delta = lax.optimization_barrier((sends, all_delta))
    for k in range(tok_size):
        pairs = []
        for v in range(vocab_size):
            for t in range(tok_size):
                d = (k + t - v // run) % tok_size
                target = (t * run + v % run) * tok_size + (t - d) % tok_size
                if target != v * tok_size + t:
                    pairs.append((v * tok_size + t, target))
        total = total + lax.ppermute(sends[k], ("vocab", "tok"), pairs).astype(jnp.float32)
    grad_hidden = total.T
    if done < chunks:
        grad_head = head_gradient(
            all_features, all_delta, grad_head, done * width, chunks - done, width
        )
    return (lse, kl, grad_hidden, grad_head)


def solution(mesh):
    placed = (P("tok", None), P("tok", "vocab"), P("tok", "vocab"), P("tok", None), P("tok"))
    return jax.shard_map(
        per_device,
        mesh=mesh,
        in_specs=placed,
        out_specs=(P("tok"), P("tok"), P("tok", "vocab"), P("tok", "vocab")),
        check_vma=False,
    )
```

```python
import functools

import jax
import jax.numpy as jnp
from jax import lax
from jax.experimental import pallas as pl
from jax.experimental.pallas import tpu as pltpu
from jax.sharding import PartitionSpec as P

BLK = 512


loss_scale = 1024.0
VMEM_LIMIT = 16 << 20
STEP = 16


def shift_tok(x, offset, size):
    return lax.ppermute(x, "tok", [(i, (i + offset) % size) for i in range(size)])


def swap_vocab(x, bit, size):
    return lax.ppermute(x, "vocab", [(i, i ^ bit) for i in range(size)])


def in_order(mine, other, upper):
    return jnp.concatenate(
        [jnp.where(upper, other, mine), jnp.where(upper, mine, other)], axis=0
    )


def gather_vocab(stats, upper, size):
    gathered = stats[None]
    for i, flag in enumerate(upper):
        gathered = in_order(gathered, swap_vocab(gathered, 1 << i, size), flag)
    return gathered


def load_kernel(head_ref, held_ref, sems):
    steps = sems.shape[0]
    depth = head_ref.shape[0] // steps
    parts = [pl.ds(k * depth, depth) for k in range(steps)]
    copies = [
        pltpu.make_async_copy(head_ref.at[part], held_ref.at[part], sems.at[k])
        for k, part in enumerate(parts)
    ]
    for copy in copies:
        copy.start()
    for copy in copies:
        copy.wait()


def load(head):
    steps = 4
    return pl.pallas_call(
        load_kernel,
        out_shape=pltpu.VMEM(head.shape, head.dtype),
        in_specs=[pl.BlockSpec(memory_space=pltpu.HBM)],
        out_specs=pl.BlockSpec(memory_space=pltpu.VMEM),
        scratch_shapes=[pltpu.SemaphoreType.DMA((steps,))],
        compiler_params=pltpu.CompilerParams(vmem_limit_bytes=VMEM_LIMIT),
        cost_estimate=pl.CostEstimate(
            flops=0, bytes_accessed=4 * head.size, transcendentals=0
        ),
        name="load_head",
    )(pltpu.with_memory_space_constraint(head, pltpu.HBM))


def stats_kernel(core_ref, own_ref, kept_ref, early_ref, *refs):
    parts, (logits_ref, stats_ref, turned_ref) = refs[:-3], refs[-3:]
    half = own_ref.shape[0] // 2
    lane = lax.broadcasted_iota(jnp.int32, (STEP, 128), 1)
    for place in range(2):
        start = (core_ref[0] if place == 0 else 1 - core_ref[0]) * half
        for r in range(0, half, STEP):
            rows = pl.ds(pl.multiple_of(start + r, STEP), STEP)
            logits = own_ref[rows, :]
            for part in parts[place::2]:
                logits = logits + part[r : r + STEP, :]
            logits_ref[rows, :] = logits
            top = jnp.max(logits, axis=1, keepdims=True)
            total = jnp.sum(jnp.exp(logits - top), axis=1, keepdims=True)
            dot = jnp.sum(kept_ref[rows, :].astype(jnp.float32) * logits, axis=1, keepdims=True)
            turned_ref[rows, :] = jnp.where(lane == 0, top, jnp.where(lane == 1, total, dot))
    turned = turned_ref[...].T
    stats_ref[0:2, :] = turned[0:2]
    stats_ref[2:3, :] = early_ref[0:1, :]
    stats_ref[3:4, :] = early_ref[1:2, :] - turned[2:3]


def local_stats(core, own_logits, kept, early, returned):
    in_vmem = pl.BlockSpec(memory_space=pltpu.VMEM)
    parts = [x for pair in returned for x in pair]
    arrays = [
        pltpu.with_memory_space_constraint(x, pltpu.VMEM) for x in (own_logits, kept, early, *parts)
    ]
    return pl.pallas_call(
        stats_kernel,
        out_shape=(
            pltpu.VMEM(own_logits.shape, jnp.float32),
            pltpu.VMEM((4, own_logits.shape[0]), jnp.float32),
        ),
        in_specs=[pl.BlockSpec(memory_space=pltpu.SMEM)] + [in_vmem] * len(arrays),
        out_specs=(in_vmem, in_vmem),
        scratch_shapes=[pltpu.VMEM((own_logits.shape[0], 128), jnp.float32)],
        compiler_params=pltpu.CompilerParams(vmem_limit_bytes=VMEM_LIMIT),
        cost_estimate=pl.CostEstimate(
            flops=8 * own_logits.size,
            bytes_accessed=12 * own_logits.size,
            transcendentals=own_logits.size,
        ),
        name="local_stats",
    )(core, *arrays)


def delta_kernel(gathered_ref, logits_ref, kept_ref, delta_ref, lse_ref, kl_ref):
    shards = [gathered_ref[i] for i in range(gathered_ref.shape[0])]
    top = shards[0][0:1]
    for x in shards[1:]:
        top = jnp.maximum(top, x[0:1])
    total, mass, part = 0.0, 0.0, 0.0
    for x in shards:
        total = total + x[1:2] * jnp.exp(x[0:1] - top)
        mass, part = mass + x[2:3], part + x[3:4]
    lse = top + jnp.log(total)
    lse_ref[...] = lse
    kl_ref[...] = part / mass - jnp.log(mass) + lse
    row = lax.broadcasted_iota(jnp.int32, (128, lse.shape[1]), 0)
    turned = jnp.where(row == 0, lse, 1.0 / mass).T
    lse_column, scale_column = turned[:, 0:1], turned[:, 1:2]
    for r in range(0, logits_ref.shape[0], STEP):
        rows = slice(r, r + STEP)
        student = jnp.exp(logits_ref[rows, :] - lse_column[rows])
        kept = kept_ref[rows, :].astype(jnp.float32) * scale_column[rows]
        delta_ref[rows, :] = (loss_scale * (student - kept)).astype(jnp.bfloat16)


def finish(gathered, logits, kept):
    tokens = logits.shape[0]
    in_vmem = pl.BlockSpec(memory_space=pltpu.VMEM)
    delta, lse, kl = pl.pallas_call(
        delta_kernel,
        out_shape=(
            pltpu.VMEM(logits.shape, jnp.bfloat16),
            jax.ShapeDtypeStruct((1, tokens), jnp.float32),
            jax.ShapeDtypeStruct((1, tokens), jnp.float32),
        ),
        in_specs=[in_vmem] * 3,
        out_specs=(in_vmem, in_vmem, in_vmem),
        compiler_params=pltpu.CompilerParams(vmem_limit_bytes=VMEM_LIMIT),
        cost_estimate=pl.CostEstimate(
            flops=8 * logits.size, bytes_accessed=8 * logits.size, transcendentals=logits.size
        ),
        name="delta",
    )(*[pltpu.with_memory_space_constraint(x, pltpu.VMEM) for x in (gathered, logits, kept)])
    return delta, lse.reshape(tokens), kl.reshape(tokens)


def write_pieces(k, head_rows, delta_ref, upper, send_ref, keep_ref):
    rows = send_ref.shape[1]
    block = lax.dot_general(
        head_rows, delta_ref[...], (((1,), (1,)), ((), ())), preferred_element_type=jnp.float32
    )
    low, high = block[:rows], block[rows:]
    send_ref[k] = jnp.where(upper, low, high).astype(jnp.bfloat16)
    keep_ref[k] = jnp.where(upper, high, low)


def first_gradient_kernel(core_ref, head_ref, delta_ref, send_ref, keep_ref, held_ref, sems):
    upper = core_ref[0] == 1
    pairs, rows, _ = send_ref.shape
    parts = [pl.ds(2 * k * rows, 2 * rows) for k in range(pairs)]
    copies = [
        pltpu.make_async_copy(head_ref.at[part], held_ref.at[part], sems.at[k])
        for k, part in enumerate(parts)
    ]
    for copy in copies[:2]:
        copy.start()
    for k in range(pairs):
        copies[k].wait()
        if k + 2 < pairs:
            copies[k + 2].start()
        head_rows = held_ref[2 * k * rows : 2 * (k + 1) * rows, :]
        write_pieces(k, head_rows, delta_ref, upper, send_ref, keep_ref)


def later_gradient_kernel(core_ref, head_ref, delta_ref, send_ref, keep_ref):
    upper = core_ref[0] == 1
    pairs, rows, _ = send_ref.shape
    for k in range(pairs):
        head_rows = head_ref[2 * k * rows : 2 * (k + 1) * rows, :]
        write_pieces(k, head_rows, delta_ref, upper, send_ref, keep_ref)


def gradient(core, head, delta, run, first):
    rows = head.shape[0] // run
    shape = (run // 2, rows, delta.shape[0])
    in_vmem = pl.BlockSpec(memory_space=pltpu.VMEM)
    space = pltpu.HBM if first else pltpu.VMEM
    outs = (pltpu.VMEM(shape, jnp.bfloat16), pltpu.VMEM(shape, jnp.float32))
    if first:
        outs = outs + (pltpu.VMEM(head.shape, head.dtype),)
    return pl.pallas_call(
        first_gradient_kernel if first else later_gradient_kernel,
        out_shape=outs,
        in_specs=[
            pl.BlockSpec(memory_space=pltpu.SMEM),
            pl.BlockSpec(memory_space=space),
            in_vmem,
        ],
        out_specs=(in_vmem,) * len(outs),
        scratch_shapes=[pltpu.SemaphoreType.DMA((run // 2,))] if first else [],
        compiler_params=pltpu.CompilerParams(vmem_limit_bytes=VMEM_LIMIT),
        cost_estimate=pl.CostEstimate(
            flops=2 * head.size * delta.shape[0],
            bytes_accessed=2 * (head.size + delta.size),
            transcendentals=0,
        ),
        name="partial_gradient",
    )(
        core,
        pltpu.with_memory_space_constraint(head, space),
        pltpu.with_memory_space_constraint(delta, pltpu.VMEM),
    )


def head_gradient_kernel(steps, start, width, *refs):
    features_ref, delta_ref, out_ref, held_ref, sems = refs[0], refs[1], *refs[-3:]
    copies = []
    for k in range(steps):
        block = lax.dot_general(
            features_ref[:, start + k * width : start + (k + 1) * width],
            delta_ref[...],
            (((0,), (0,)), ((), ())),
            preferred_element_type=jnp.float32,
        )
        held_ref[k] = block.astype(jnp.bfloat16)
        copy = pltpu.make_async_copy(
            held_ref.at[k], out_ref.at[pl.ds(start + k * width, width)], sems.at[k]
        )
        copy.start()
        copies.append(copy)
    for copy in copies:
        copy.wait()


def head_gradient(features, delta, out, start, steps, width):
    columns = delta.shape[1]
    in_vmem = pl.BlockSpec(memory_space=pltpu.VMEM)
    in_hbm = pl.BlockSpec(memory_space=pltpu.HBM)
    return pl.pallas_call(
        functools.partial(head_gradient_kernel, steps, start, width),
        out_shape=jax.ShapeDtypeStruct((features.shape[1], columns), jnp.bfloat16),
        in_specs=[in_vmem, in_vmem] + ([] if out is None else [in_hbm]),
        out_specs=in_hbm,
        scratch_shapes=[
            pltpu.VMEM((steps, width, columns), jnp.bfloat16),
            pltpu.SemaphoreType.DMA((steps,)),
        ],
        input_output_aliases={} if out is None else {2: 0},
        compiler_params=pltpu.CompilerParams(vmem_limit_bytes=VMEM_LIMIT),
        cost_estimate=pl.CostEstimate(
            flops=2 * steps * width * delta.size,
            bytes_accessed=2 * (features.size + delta.size + steps * width * columns),
            transcendentals=0,
        ),
        name="head_gradient",
    )(features, delta, *([] if out is None else [out]))


def per_device(hidden, head, teacher, block_ids, counts):
    tok_size = lax.axis_size("tok")
    vocab_size = lax.axis_size("vocab")
    tok_index = lax.axis_index("tok")
    vocab_index = lax.axis_index("vocab")
    token_count = hidden.shape[0]
    rows, column_count = head.shape
    run = vocab_size // tok_size
    half = token_count // 2
    core = vocab_index & 1

    def columns_of(index, first, count):
        return lax.dynamic_slice(hidden, (first, index * rows), (count, rows))

    near = [
        shift_tok(columns_of(lax.rem(tok_index + d, tok_size), core * half, half), d, tok_size)
        for d in range(1, tok_size)
    ]
    upper = []
    while 1 << len(upper) < vocab_size:
        upper.append((vocab_index & (1 << len(upper))) != 0)
    high = lax.div(vocab_index, run)
    apart = lax.rem(tok_index + tok_size - high, tok_size)
    apart_is = [apart == d for d in range(tok_size)]
    first_column = vocab_index * column_count
    column_block = (first_column + jnp.arange(column_count, dtype=jnp.int32)) // BLK
    live_slot = jnp.arange(block_ids.shape[1], dtype=jnp.int32)[None, :] < counts[:, None]
    core_word = core.reshape(1)
    own = columns_of(tok_index, 0, token_count)
    own, head, upper, apart_is, column_block, live_slot, core_word = lax.optimization_barrier(
        (own, head, upper, apart_is, column_block, live_slot, core_word)
    )
    head_here = load(head)
    near, head_here = lax.optimization_barrier((near, head_here))
    far = [swap_vocab(x, 1, vocab_size) for x in near]
    returned = []
    for d in range(1, tok_size):
        first = shift_tok(
            jnp.dot(near[d - 1], head_here, preferred_element_type=jnp.float32), -d, tok_size
        )
        second = shift_tok(
            jnp.dot(far[d - 1], head_here, preferred_element_type=jnp.float32), -d, tok_size
        )
        returned.append((first, second))
    logits = jnp.dot(own, head_here, preferred_element_type=jnp.float32)
    block_hit = jnp.any(
        (block_ids[:, :, None] == column_block[None, None, :]) & live_slot[:, :, None], axis=1
    )
    features = [own] + [in_order(n, f, upper[0]) for n, f in zip(near, far)]
    all_features = jnp.concatenate(features, axis=0)
    blocks = block_hit.shape[0]
    listed = jnp.broadcast_to(
        block_hit[:, None, :], (blocks, token_count // blocks, column_count)
    ).reshape(token_count, column_count)
    teacher_f = teacher.astype(jnp.float32)
    kept = jnp.where(listed, teacher_f, 0.0)
    mass = jnp.sum(kept, axis=1)
    entropy = jnp.sum(jnp.where(listed, teacher_f * jnp.log(teacher_f), 0.0), axis=1)
    kept, early = kept.astype(jnp.bfloat16), jnp.stack([mass, entropy])
    returned, all_features, logits, kept, early = lax.optimization_barrier(
        (returned, all_features, logits, kept, early)
    )
    logits, stats = local_stats(core_word, logits, kept, early, returned)
    delta, lse, kl = finish(gather_vocab(stats, upper, vocab_size), logits, kept)

    deltas = [delta] + [shift_tok(delta, d, tok_size) for d in range(1, tok_size)]
    send, keep, head_here = gradient(core_word, head, delta, run, True)
    other = swap_vocab(send, 1, vocab_size)
    state = [(keep, other)]
    for x in deltas[1:]:
        send, keep = gradient(core_word, head_here, x, run, False)
        state[0], send = lax.optimization_barrier((state[0], send))
        state.append((keep, swap_vocab(send, 1, vocab_size)))
    all_delta = jnp.concatenate(deltas, axis=0)

    width = 256 if rows % 256 == 0 else rows
    chunks = rows // width
    held = jnp.stack([keep + other.astype(jnp.float32) for keep, other in state], axis=1)
    pieces = held.shape[0]
    places = [i for i in range(1, len(upper)) if 1 << i < run]
    taken = []
    for offset in range(pieces):
        options = [held[j ^ offset] for j in range(pieces)]
        for i in places:
            options = [
                jnp.where(upper[i], high, low) for low, high in zip(options[::2], options[1::2])
            ]
        taken.append(options[0])
    sends = [x.astype(jnp.bfloat16) for x in taken[1:]]
    sends, all_delta = lax.optimization_barrier((sends, all_delta))
    others = [swap_vocab(x, 2 * (i + 1), vocab_size) for i, x in enumerate(sends)]
    done = (chunks + 1) // 2
    grad_head = head_gradient(all_features, all_delta, None, 0, done, width)
    others, grad_head = lax.optimization_barrier((others, grad_head))
    sums = taken[0]
    for other in others:
        sums = sums + other.astype(jnp.float32)
    sums = [
        sums[d]
        if d == 0
        else shift_tok(sums[d].astype(jnp.bfloat16), -d, tok_size).astype(jnp.float32)
        for d in range(tok_size)
    ]
    blocks = []
    for k in range(tok_size):
        block = sums[k]
        for d in range(1, tok_size):
            block = jnp.where(apart_is[d], sums[(k - d) % tok_size], block)
        blocks.append(block)
    total = blocks[0]
    if done < chunks:
        blocks[1:], all_delta = lax.optimization_barrier((blocks[1:], all_delta))
        grad_head = head_gradient(
            all_features, all_delta, grad_head, done * width, chunks - done, width
        )
    for k in range(1, tok_size):
        pairs = [(v, (v + k * run) % vocab_size) for v in range(vocab_size)]
        total = total + lax.ppermute(
            blocks[k].astype(jnp.bfloat16), "vocab", pairs
        ).astype(jnp.float32)
    grad_hidden = total.T
    return (lse, kl, grad_hidden, grad_head)


def solution(mesh):
    placed = (P("tok", None), P("tok", "vocab"), P("tok", "vocab"), P("tok", None), P("tok"))
    return jax.shard_map(
        per_device,
        mesh=mesh,
        in_specs=placed,
        out_specs=(P("tok"), P("tok"), P("tok", "vocab"), P("tok", "vocab")),
        check_vma=False,
    )
```

```python
import functools

import jax
import jax.numpy as jnp
from jax import lax
from jax.experimental import pallas as pl
from jax.experimental.pallas import tpu as pltpu
from jax.sharding import PartitionSpec as P

BLK = 512


loss_scale = 1024.0
VMEM_LIMIT = 16 << 20
STEP = 16


def shift_tok(x, offset, size):
    return lax.ppermute(x, "tok", [(i, (i + offset) % size) for i in range(size)])


def swap_vocab(x, bit, size):
    return lax.ppermute(x, "vocab", [(i, i ^ bit) for i in range(size)])


def in_order(mine, other, upper):
    return jnp.concatenate(
        [jnp.where(upper, other, mine), jnp.where(upper, mine, other)], axis=0
    )


def select(options, flags):
    for flag in flags:
        options = [jnp.where(flag, high, low) for low, high in zip(options[::2], options[1::2])]
    return options[0]


def gather_vocab(stats, upper, places, size):
    pair = in_order(stats[None], swap_vocab(stats[None], 1, size), upper[0])
    count = 1 << len(places)
    options = [pair] + [swap_vocab(pair, 2 * offset, size) for offset in range(1, count)]
    flags = [upper[i] for i in places]
    gathered = jnp.concatenate(
        [select([options[j ^ i] for i in range(count)], flags) for j in range(count)], axis=0
    )
    for i in range(len(places) + 1, len(upper)):
        gathered = in_order(gathered, swap_vocab(gathered, 1 << i, size), upper[i])
    return gathered


def load_kernel(head_ref, held_ref, sems):
    steps = sems.shape[0]
    depth = head_ref.shape[0] // steps
    parts = [pl.ds(k * depth, depth) for k in range(steps)]
    copies = [
        pltpu.make_async_copy(head_ref.at[part], held_ref.at[part], sems.at[k])
        for k, part in enumerate(parts)
    ]
    for copy in copies:
        copy.start()
    for copy in copies:
        copy.wait()


def load(head):
    steps = 4
    return pl.pallas_call(
        load_kernel,
        out_shape=pltpu.VMEM(head.shape, head.dtype),
        in_specs=[pl.BlockSpec(memory_space=pltpu.HBM)],
        out_specs=pl.BlockSpec(memory_space=pltpu.VMEM),
        scratch_shapes=[pltpu.SemaphoreType.DMA((steps,))],
        compiler_params=pltpu.CompilerParams(vmem_limit_bytes=VMEM_LIMIT),
        cost_estimate=pl.CostEstimate(
            flops=0, bytes_accessed=4 * head.size, transcendentals=0
        ),
        name="load_head",
    )(pltpu.with_memory_space_constraint(head, pltpu.HBM))


def stats_kernel(core_ref, own_ref, kept_ref, early_ref, *refs):
    parts, (logits_ref, stats_ref, turned_ref) = refs[:-3], refs[-3:]
    half = own_ref.shape[0] // 2
    lane = lax.broadcasted_iota(jnp.int32, (STEP, 128), 1)
    for place in range(2):
        start = (core_ref[0] if place == 0 else 1 - core_ref[0]) * half
        for r in range(0, half, STEP):
            rows = pl.ds(pl.multiple_of(start + r, STEP), STEP)
            logits = own_ref[rows, :]
            for part in parts[place::2]:
                logits = logits + part[r : r + STEP, :]
            logits_ref[rows, :] = logits
            top = jnp.max(logits, axis=1, keepdims=True)
            total = jnp.sum(jnp.exp(logits - top), axis=1, keepdims=True)
            dot = jnp.sum(kept_ref[rows, :].astype(jnp.float32) * logits, axis=1, keepdims=True)
            turned_ref[rows, :] = jnp.where(lane == 0, top, jnp.where(lane == 1, total, dot))
    turned = turned_ref[...].T
    stats_ref[0:2, :] = turned[0:2]
    stats_ref[2:3, :] = early_ref[0:1, :]
    stats_ref[3:4, :] = early_ref[1:2, :] - turned[2:3]


def local_stats(core, own_logits, kept, early, returned):
    in_vmem = pl.BlockSpec(memory_space=pltpu.VMEM)
    parts = [x for pair in returned for x in pair]
    arrays = [
        pltpu.with_memory_space_constraint(x, pltpu.VMEM) for x in (own_logits, kept, early, *parts)
    ]
    return pl.pallas_call(
        stats_kernel,
        out_shape=(
            pltpu.VMEM(own_logits.shape, jnp.float32),
            pltpu.VMEM((4, own_logits.shape[0]), jnp.float32),
        ),
        in_specs=[pl.BlockSpec(memory_space=pltpu.SMEM)] + [in_vmem] * len(arrays),
        out_specs=(in_vmem, in_vmem),
        scratch_shapes=[pltpu.VMEM((own_logits.shape[0], 128), jnp.float32)],
        compiler_params=pltpu.CompilerParams(vmem_limit_bytes=VMEM_LIMIT),
        cost_estimate=pl.CostEstimate(
            flops=8 * own_logits.size,
            bytes_accessed=12 * own_logits.size,
            transcendentals=own_logits.size,
        ),
        name="local_stats",
    )(core, *arrays)


def delta_kernel(gathered_ref, logits_ref, kept_ref, delta_ref, lse_ref, kl_ref):
    shards = [gathered_ref[i] for i in range(gathered_ref.shape[0])]
    top = shards[0][0:1]
    for x in shards[1:]:
        top = jnp.maximum(top, x[0:1])
    total, mass, part = 0.0, 0.0, 0.0
    for x in shards:
        total = total + x[1:2] * jnp.exp(x[0:1] - top)
        mass, part = mass + x[2:3], part + x[3:4]
    lse = top + jnp.log(total)
    lse_ref[...] = lse
    kl_ref[...] = part / mass - jnp.log(mass) + lse
    row = lax.broadcasted_iota(jnp.int32, (128, lse.shape[1]), 0)
    turned = jnp.where(row == 0, lse, 1.0 / mass).T
    lse_column, scale_column = turned[:, 0:1], turned[:, 1:2]
    for r in range(0, logits_ref.shape[0], STEP):
        rows = slice(r, r + STEP)
        student = jnp.exp(logits_ref[rows, :] - lse_column[rows])
        kept = kept_ref[rows, :].astype(jnp.float32) * scale_column[rows]
        delta_ref[rows, :] = (loss_scale * (student - kept)).astype(jnp.bfloat16)


def finish(gathered, logits, kept):
    tokens = logits.shape[0]
    in_vmem = pl.BlockSpec(memory_space=pltpu.VMEM)
    delta, lse, kl = pl.pallas_call(
        delta_kernel,
        out_shape=(
            pltpu.VMEM(logits.shape, jnp.bfloat16),
            jax.ShapeDtypeStruct((1, tokens), jnp.float32),
            jax.ShapeDtypeStruct((1, tokens), jnp.float32),
        ),
        in_specs=[in_vmem] * 3,
        out_specs=(in_vmem, in_vmem, in_vmem),
        compiler_params=pltpu.CompilerParams(vmem_limit_bytes=VMEM_LIMIT),
        cost_estimate=pl.CostEstimate(
            flops=8 * logits.size, bytes_accessed=8 * logits.size, transcendentals=logits.size
        ),
        name="delta",
    )(*[pltpu.with_memory_space_constraint(x, pltpu.VMEM) for x in (gathered, logits, kept)])
    return delta, lse.reshape(tokens), kl.reshape(tokens)


def write_pieces(k, head_rows, delta_ref, upper, send_ref, keep_ref):
    rows = send_ref.shape[1]
    block = lax.dot_general(
        head_rows, delta_ref[...], (((1,), (1,)), ((), ())), preferred_element_type=jnp.float32
    )
    low, high = block[:rows], block[rows:]
    send_ref[k] = jnp.where(upper, low, high).astype(jnp.bfloat16)
    keep_ref[k] = jnp.where(upper, high, low)


def gradient_kernel(core_ref, head_ref, delta_ref, send_ref, keep_ref):
    upper = core_ref[0] == 1
    pairs, rows, _ = send_ref.shape
    for k in range(pairs):
        head_rows = head_ref[2 * k * rows : 2 * (k + 1) * rows, :]
        write_pieces(k, head_rows, delta_ref, upper, send_ref, keep_ref)


def gradient(core, head, delta, run):
    rows = head.shape[0] // run
    shape = (run // 2, rows, delta.shape[0])
    in_vmem = pl.BlockSpec(memory_space=pltpu.VMEM)
    return pl.pallas_call(
        gradient_kernel,
        out_shape=(pltpu.VMEM(shape, jnp.bfloat16), pltpu.VMEM(shape, jnp.float32)),
        in_specs=[pl.BlockSpec(memory_space=pltpu.SMEM), in_vmem, in_vmem],
        out_specs=(in_vmem, in_vmem),
        compiler_params=pltpu.CompilerParams(vmem_limit_bytes=VMEM_LIMIT),
        cost_estimate=pl.CostEstimate(
            flops=2 * head.size * delta.shape[0],
            bytes_accessed=2 * (head.size + delta.size),
            transcendentals=0,
        ),
        name="partial_gradient",
    )(
        core,
        pltpu.with_memory_space_constraint(head, pltpu.VMEM),
        pltpu.with_memory_space_constraint(delta, pltpu.VMEM),
    )


def head_gradient_kernel(steps, start, width, *refs):
    features_ref, delta_ref, out_ref, held_ref, sems = refs[0], refs[1], *refs[-3:]
    copies = []
    for k in range(steps):
        block = lax.dot_general(
            features_ref[:, start + k * width : start + (k + 1) * width],
            delta_ref[...],
            (((0,), (0,)), ((), ())),
            preferred_element_type=jnp.float32,
        )
        held_ref[k] = block.astype(jnp.bfloat16)
        copy = pltpu.make_async_copy(
            held_ref.at[k], out_ref.at[pl.ds(start + k * width, width)], sems.at[k]
        )
        copy.start()
        copies.append(copy)
    for copy in copies:
        copy.wait()


def head_gradient(features, delta, out, start, steps, width):
    columns = delta.shape[1]
    in_vmem = pl.BlockSpec(memory_space=pltpu.VMEM)
    in_hbm = pl.BlockSpec(memory_space=pltpu.HBM)
    return pl.pallas_call(
        functools.partial(head_gradient_kernel, steps, start, width),
        out_shape=jax.ShapeDtypeStruct((features.shape[1], columns), jnp.bfloat16),
        in_specs=[in_vmem, in_vmem] + ([] if out is None else [in_hbm]),
        out_specs=in_hbm,
        scratch_shapes=[
            pltpu.VMEM((steps, width, columns), jnp.bfloat16),
            pltpu.SemaphoreType.DMA((steps,)),
        ],
        input_output_aliases={} if out is None else {2: 0},
        compiler_params=pltpu.CompilerParams(vmem_limit_bytes=VMEM_LIMIT),
        cost_estimate=pl.CostEstimate(
            flops=2 * steps * width * delta.size,
            bytes_accessed=2 * (features.size + delta.size + steps * width * columns),
            transcendentals=0,
        ),
        name="head_gradient",
    )(features, delta, *([] if out is None else [out]))


def per_device(hidden, head, teacher, block_ids, counts):
    tok_size = lax.axis_size("tok")
    vocab_size = lax.axis_size("vocab")
    tok_index = lax.axis_index("tok")
    vocab_index = lax.axis_index("vocab")
    token_count = hidden.shape[0]
    rows, column_count = head.shape
    run = vocab_size // tok_size
    half = token_count // 2
    core = vocab_index & 1

    def columns_of(index, first, count):
        return lax.dynamic_slice(hidden, (first, index * rows), (count, rows))

    near = [
        shift_tok(columns_of(lax.rem(tok_index + d, tok_size), core * half, half), d, tok_size)
        for d in range(1, tok_size)
    ]
    upper = []
    while 1 << len(upper) < vocab_size:
        upper.append((vocab_index & (1 << len(upper))) != 0)
    high = lax.div(vocab_index, run)
    apart = lax.rem(tok_index + tok_size - high, tok_size)
    apart_is = [apart == d for d in range(tok_size)]
    first_column = vocab_index * column_count
    column_block = (first_column + jnp.arange(column_count, dtype=jnp.int32)) // BLK
    live_slot = jnp.arange(block_ids.shape[1], dtype=jnp.int32)[None, :] < counts[:, None]
    core_word = core.reshape(1)
    own = columns_of(tok_index, 0, token_count)
    own, head, upper, apart_is, column_block, live_slot, core_word = lax.optimization_barrier(
        (own, head, upper, apart_is, column_block, live_slot, core_word)
    )
    head_here = load(head)
    near, head_here, column_block, teacher = lax.optimization_barrier(
        (near, head_here, column_block, teacher)
    )
    far = [swap_vocab(x, 1, vocab_size) for x in near]
    returned = []
    for d in range(1, tok_size):
        first = shift_tok(
            jnp.dot(near[d - 1], head_here, preferred_element_type=jnp.float32), -d, tok_size
        )
        second = shift_tok(
            jnp.dot(far[d - 1], head_here, preferred_element_type=jnp.float32), -d, tok_size
        )
        returned.append((first, second))
    logits = jnp.dot(own, head_here, preferred_element_type=jnp.float32)
    block_hit = jnp.any(
        (block_ids[:, :, None] == column_block[None, None, :]) & live_slot[:, :, None], axis=1
    )
    features = [own] + [in_order(n, f, upper[0]) for n, f in zip(near, far)]
    all_features = jnp.concatenate(features, axis=0)
    blocks = block_hit.shape[0]
    listed = jnp.broadcast_to(
        block_hit[:, None, :], (blocks, token_count // blocks, column_count)
    ).reshape(token_count, column_count)
    teacher_f = teacher.astype(jnp.float32)
    kept = jnp.where(listed, teacher_f, 0.0)
    mass = jnp.sum(kept, axis=1)
    entropy = jnp.sum(jnp.where(listed, teacher_f * jnp.log(teacher_f), 0.0), axis=1)
    kept, early = kept.astype(jnp.bfloat16), jnp.stack([mass, entropy])
    returned, all_features, logits, kept, early = lax.optimization_barrier(
        (returned, all_features, logits, kept, early)
    )
    places = [i for i in range(1, len(upper)) if 1 << i < run]
    logits, stats = local_stats(core_word, logits, kept, early, returned)
    delta, lse, kl = finish(gather_vocab(stats, upper, places, vocab_size), logits, kept)

    deltas = [delta] + [shift_tok(delta, d, tok_size) for d in range(1, tok_size)]
    send, keep = gradient(core_word, head_here, delta, run)
    other = swap_vocab(send, 1, vocab_size)
    state = [(keep, other)]
    for x in deltas[1:]:
        send, keep = gradient(core_word, head_here, x, run)
        state[0], send = lax.optimization_barrier((state[0], send))
        state.append((keep, swap_vocab(send, 1, vocab_size)))
    all_delta = jnp.concatenate(deltas, axis=0)

    width = 256 if rows % 256 == 0 else rows
    chunks = rows // width
    held = jnp.stack([keep + other.astype(jnp.float32) for keep, other in state], axis=1)
    pieces = held.shape[0]
    flags = [upper[i] for i in places]
    taken = [
        select([held[j ^ offset] for j in range(pieces)], flags) for offset in range(pieces)
    ]
    sends = [x.astype(jnp.bfloat16) for x in taken[1:]]
    sends, all_delta = lax.optimization_barrier((sends, all_delta))
    others = [swap_vocab(x, 2 * (i + 1), vocab_size) for i, x in enumerate(sends)]
    done = (chunks + 1) // 2
    grad_head = head_gradient(all_features, all_delta, None, 0, done, width)
    others, grad_head = lax.optimization_barrier((others, grad_head))
    sums = taken[0]
    for other in others:
        sums = sums + other.astype(jnp.float32)
    sends = [x.astype(jnp.bfloat16) for x in (sums[d] for d in range(1, tok_size))]
    sends, all_delta = lax.optimization_barrier((sends, all_delta))
    others = [shift_tok(x, -d, tok_size) for d, x in enumerate(sends, 1)]
    if done < chunks:
        grad_head = head_gradient(
            all_features, all_delta, grad_head, done * width, chunks - done, width
        )
        others, grad_head = lax.optimization_barrier((others, grad_head))
    sums = [sums[0]] + [x.astype(jnp.float32) for x in others]
    blocks = []
    for k in range(tok_size):
        block = sums[k]
        for d in range(1, tok_size):
            block = jnp.where(apart_is[d], sums[(k - d) % tok_size], block)
        blocks.append(block)
    total = blocks[0]
    for k in range(1, tok_size):
        pairs = [(v, (v + k * run) % vocab_size) for v in range(vocab_size)]
        total = total + lax.ppermute(
            blocks[k].astype(jnp.bfloat16), "vocab", pairs
        ).astype(jnp.float32)
    grad_hidden = total.T
    return (lse, kl, grad_hidden, grad_head)


def solution(mesh):
    placed = (P("tok", None), P("tok", "vocab"), P("tok", "vocab"), P("tok", None), P("tok"))
    return jax.shard_map(
        per_device,
        mesh=mesh,
        in_specs=placed,
        out_specs=(P("tok"), P("tok"), P("tok", "vocab"), P("tok", "vocab")),
        check_vma=False,
    )
```

```python
import functools

import jax
import jax.numpy as jnp
from jax import lax
from jax.experimental import pallas as pl
from jax.experimental.pallas import tpu as pltpu
from jax.sharding import PartitionSpec as P

BLK = 512


loss_scale = 1024.0
VMEM_LIMIT = 16 << 20
STEP = 16


def shift_tok(x, offset, size):
    return lax.ppermute(x, "tok", [(i, (i + offset) % size) for i in range(size)])


def swap_vocab(x, bit, size):
    return lax.ppermute(x, "vocab", [(i, i ^ bit) for i in range(size)])


def in_order(mine, other, upper):
    return jnp.concatenate(
        [jnp.where(upper, other, mine), jnp.where(upper, mine, other)], axis=0
    )


def select(options, flags):
    for flag in flags:
        options = [jnp.where(flag, high, low) for low, high in zip(options[::2], options[1::2])]
    return options[0]


def gather_vocab(stats, upper, places, size):
    pair = in_order(stats[None], swap_vocab(stats[None], 1, size), upper[0])
    count = 1 << len(places)
    options = [pair] + [swap_vocab(pair, 2 * offset, size) for offset in range(1, count)]
    flags = [upper[i] for i in places]
    gathered = jnp.concatenate(
        [select([options[j ^ i] for i in range(count)], flags) for j in range(count)], axis=0
    )
    for i in range(len(places) + 1, len(upper)):
        gathered = in_order(gathered, swap_vocab(gathered, 1 << i, size), upper[i])
    return gathered


def load_kernel(head_ref, held_ref, sems):
    steps = sems.shape[0]
    depth = head_ref.shape[0] // steps
    parts = [pl.ds(k * depth, depth) for k in range(steps)]
    copies = [
        pltpu.make_async_copy(head_ref.at[part], held_ref.at[part], sems.at[k])
        for k, part in enumerate(parts)
    ]
    for copy in copies:
        copy.start()
    for copy in copies:
        copy.wait()


def load(head):
    steps = 4
    return pl.pallas_call(
        load_kernel,
        out_shape=pltpu.VMEM(head.shape, head.dtype),
        in_specs=[pl.BlockSpec(memory_space=pltpu.HBM)],
        out_specs=pl.BlockSpec(memory_space=pltpu.VMEM),
        scratch_shapes=[pltpu.SemaphoreType.DMA((steps,))],
        compiler_params=pltpu.CompilerParams(vmem_limit_bytes=VMEM_LIMIT),
        cost_estimate=pl.CostEstimate(
            flops=0, bytes_accessed=4 * head.size, transcendentals=0
        ),
        name="load_head",
    )(pltpu.with_memory_space_constraint(head, pltpu.HBM))


def stats_kernel(core_ref, own_ref, kept_ref, early_ref, *refs):
    parts, (logits_ref, stats_ref, turned_ref) = refs[:-3], refs[-3:]
    half = own_ref.shape[0] // 2
    lane = lax.broadcasted_iota(jnp.int32, (STEP, 128), 1)
    for place in range(2):
        start = (core_ref[0] if place == 0 else 1 - core_ref[0]) * half
        for r in range(0, half, STEP):
            rows = pl.ds(pl.multiple_of(start + r, STEP), STEP)
            logits = own_ref[rows, :]
            for part in parts[place::2]:
                logits = logits + part[r : r + STEP, :]
            logits_ref[rows, :] = logits
            top = jnp.max(logits, axis=1, keepdims=True)
            total = jnp.sum(jnp.exp(logits - top), axis=1, keepdims=True)
            dot = jnp.sum(kept_ref[rows, :].astype(jnp.float32) * logits, axis=1, keepdims=True)
            turned_ref[rows, :] = jnp.where(lane == 0, top, jnp.where(lane == 1, total, dot))
    turned = turned_ref[...].T
    stats_ref[0:2, :] = turned[0:2]
    stats_ref[2:3, :] = early_ref[0:1, :]
    stats_ref[3:4, :] = early_ref[1:2, :] - turned[2:3]


def local_stats(core, own_logits, kept, early, returned):
    in_vmem = pl.BlockSpec(memory_space=pltpu.VMEM)
    parts = [x for pair in returned for x in pair]
    arrays = [
        pltpu.with_memory_space_constraint(x, pltpu.VMEM) for x in (own_logits, kept, early, *parts)
    ]
    return pl.pallas_call(
        stats_kernel,
        out_shape=(
            pltpu.VMEM(own_logits.shape, jnp.float32),
            pltpu.VMEM((4, own_logits.shape[0]), jnp.float32),
        ),
        in_specs=[pl.BlockSpec(memory_space=pltpu.SMEM)] + [in_vmem] * len(arrays),
        out_specs=(in_vmem, in_vmem),
        scratch_shapes=[pltpu.VMEM((own_logits.shape[0], 128), jnp.float32)],
        compiler_params=pltpu.CompilerParams(vmem_limit_bytes=VMEM_LIMIT),
        cost_estimate=pl.CostEstimate(
            flops=8 * own_logits.size,
            bytes_accessed=12 * own_logits.size,
            transcendentals=own_logits.size,
        ),
        name="local_stats",
    )(core, *arrays)


def delta_kernel(gathered_ref, logits_ref, kept_ref, delta_ref, lse_ref, kl_ref):
    shards = [gathered_ref[i] for i in range(gathered_ref.shape[0])]
    top = shards[0][0:1]
    for x in shards[1:]:
        top = jnp.maximum(top, x[0:1])
    total, mass, part = 0.0, 0.0, 0.0
    for x in shards:
        total = total + x[1:2] * jnp.exp(x[0:1] - top)
        mass, part = mass + x[2:3], part + x[3:4]
    lse = top + jnp.log(total)
    lse_ref[...] = lse
    kl_ref[...] = part / mass - jnp.log(mass) + lse
    row = lax.broadcasted_iota(jnp.int32, (128, lse.shape[1]), 0)
    turned = jnp.where(row == 0, lse, 1.0 / mass).T
    lse_column, scale_column = turned[:, 0:1], turned[:, 1:2]
    for r in range(0, logits_ref.shape[0], STEP):
        rows = slice(r, r + STEP)
        student = jnp.exp(logits_ref[rows, :] - lse_column[rows])
        kept = kept_ref[rows, :].astype(jnp.float32) * scale_column[rows]
        delta_ref[rows, :] = (loss_scale * (student - kept)).astype(jnp.bfloat16)


def finish(gathered, logits, kept):
    tokens = logits.shape[0]
    in_vmem = pl.BlockSpec(memory_space=pltpu.VMEM)
    delta, lse, kl = pl.pallas_call(
        delta_kernel,
        out_shape=(
            pltpu.VMEM(logits.shape, jnp.bfloat16),
            jax.ShapeDtypeStruct((1, tokens), jnp.float32),
            jax.ShapeDtypeStruct((1, tokens), jnp.float32),
        ),
        in_specs=[in_vmem] * 3,
        out_specs=(in_vmem, in_vmem, in_vmem),
        compiler_params=pltpu.CompilerParams(vmem_limit_bytes=VMEM_LIMIT),
        cost_estimate=pl.CostEstimate(
            flops=8 * logits.size, bytes_accessed=8 * logits.size, transcendentals=logits.size
        ),
        name="delta",
    )(*[pltpu.with_memory_space_constraint(x, pltpu.VMEM) for x in (gathered, logits, kept)])
    return delta, lse.reshape(tokens), kl.reshape(tokens)


def write_pieces(k, head_rows, delta_ref, upper, send_ref, keep_ref):
    rows = send_ref.shape[1]
    block = lax.dot_general(
        head_rows, delta_ref[...], (((1,), (1,)), ((), ())), preferred_element_type=jnp.float32
    )
    low, high = block[:rows], block[rows:]
    send_ref[k] = jnp.where(upper, low, high).astype(jnp.bfloat16)
    keep_ref[k] = jnp.where(upper, high, low)


def gradient_kernel(core_ref, head_ref, delta_ref, send_ref, keep_ref):
    upper = core_ref[0] == 1
    pairs, rows, _ = send_ref.shape
    for k in range(pairs):
        head_rows = head_ref[2 * k * rows : 2 * (k + 1) * rows, :]
        write_pieces(k, head_rows, delta_ref, upper, send_ref, keep_ref)


def own_gradient_kernel(head_ref, delta_ref, out_ref):
    pairs, _, rows, _ = out_ref.shape
    for k in range(pairs):
        block = lax.dot_general(
            head_ref[2 * k * rows : 2 * (k + 1) * rows, :],
            delta_ref[...],
            (((1,), (1,)), ((), ())),
            preferred_element_type=jnp.float32,
        )
        out_ref[k, 0] = block[:rows]
        out_ref[k, 1] = block[rows:]


def gradient(core, head, delta, run):
    rows = head.shape[0] // run
    shape = (run // 2, rows, delta.shape[0])
    in_vmem = pl.BlockSpec(memory_space=pltpu.VMEM)
    if core is None:
        outs = pltpu.VMEM((run // 2, 2, *shape[1:]), jnp.float32)
    else:
        outs = (pltpu.VMEM(shape, jnp.bfloat16), pltpu.VMEM(shape, jnp.float32))
    arrays = [pltpu.with_memory_space_constraint(x, pltpu.VMEM) for x in (head, delta)]
    return pl.pallas_call(
        own_gradient_kernel if core is None else gradient_kernel,
        out_shape=outs,
        in_specs=([] if core is None else [pl.BlockSpec(memory_space=pltpu.SMEM)]) + [in_vmem] * 2,
        out_specs=in_vmem if core is None else (in_vmem, in_vmem),
        compiler_params=pltpu.CompilerParams(vmem_limit_bytes=VMEM_LIMIT),
        cost_estimate=pl.CostEstimate(
            flops=2 * head.size * delta.shape[0],
            bytes_accessed=2 * (head.size + delta.size),
            transcendentals=0,
        ),
        name="partial_gradient",
    )(*([] if core is None else [core]), *arrays)


def head_gradient_kernel(steps, start, width, *refs):
    features_ref, delta_ref, out_ref, held_ref, sems = refs[0], refs[1], *refs[-3:]
    copies = []
    for k in range(steps):
        block = lax.dot_general(
            features_ref[:, start + k * width : start + (k + 1) * width],
            delta_ref[...],
            (((0,), (0,)), ((), ())),
            preferred_element_type=jnp.float32,
        )
        held_ref[k] = block.astype(jnp.bfloat16)
        copy = pltpu.make_async_copy(
            held_ref.at[k], out_ref.at[pl.ds(start + k * width, width)], sems.at[k]
        )
        copy.start()
        copies.append(copy)
    for copy in copies:
        copy.wait()


def head_gradient(features, delta, out, start, steps, width):
    columns = delta.shape[1]
    in_vmem = pl.BlockSpec(memory_space=pltpu.VMEM)
    in_hbm = pl.BlockSpec(memory_space=pltpu.HBM)
    return pl.pallas_call(
        functools.partial(head_gradient_kernel, steps, start, width),
        out_shape=jax.ShapeDtypeStruct((features.shape[1], columns), jnp.bfloat16),
        in_specs=[in_vmem, in_vmem] + ([] if out is None else [in_hbm]),
        out_specs=in_hbm,
        scratch_shapes=[
            pltpu.VMEM((steps, width, columns), jnp.bfloat16),
            pltpu.SemaphoreType.DMA((steps,)),
        ],
        input_output_aliases={} if out is None else {2: 0},
        compiler_params=pltpu.CompilerParams(vmem_limit_bytes=VMEM_LIMIT),
        cost_estimate=pl.CostEstimate(
            flops=2 * steps * width * delta.size,
            bytes_accessed=2 * (features.size + delta.size + steps * width * columns),
            transcendentals=0,
        ),
        name="head_gradient",
    )(features, delta, *([] if out is None else [out]))


def per_device(hidden, head, teacher, block_ids, counts):
    tok_size = lax.axis_size("tok")
    vocab_size = lax.axis_size("vocab")
    tok_index = lax.axis_index("tok")
    vocab_index = lax.axis_index("vocab")
    token_count = hidden.shape[0]
    rows, column_count = head.shape
    run = vocab_size // tok_size
    half = token_count // 2
    core = vocab_index & 1

    def columns_of(index, first, count):
        return lax.dynamic_slice(hidden, (first, index * rows), (count, rows))

    near = [
        shift_tok(columns_of(lax.rem(tok_index + d, tok_size), core * half, half), d, tok_size)
        for d in range(1, tok_size)
    ]
    upper = []
    while 1 << len(upper) < vocab_size:
        upper.append((vocab_index & (1 << len(upper))) != 0)
    high = lax.div(vocab_index, run)
    apart = lax.rem(tok_index + tok_size - high, tok_size)
    apart_is = [apart == d for d in range(tok_size)]
    first_column = vocab_index * column_count
    column_block = (first_column + jnp.arange(column_count, dtype=jnp.int32)) // BLK
    live_slot = jnp.arange(block_ids.shape[1], dtype=jnp.int32)[None, :] < counts[:, None]
    core_word = core.reshape(1)
    own = columns_of(tok_index, 0, token_count)
    own, head, upper, apart_is, column_block, live_slot, core_word = lax.optimization_barrier(
        (own, head, upper, apart_is, column_block, live_slot, core_word)
    )
    head_here = load(head)
    near, head_here, column_block, teacher = lax.optimization_barrier(
        (near, head_here, column_block, teacher)
    )
    far = [swap_vocab(x, 1, vocab_size) for x in near]
    returned = []
    for d in range(1, tok_size):
        first = shift_tok(
            jnp.dot(near[d - 1], head_here, preferred_element_type=jnp.float32), -d, tok_size
        )
        second = shift_tok(
            jnp.dot(far[d - 1], head_here, preferred_element_type=jnp.float32), -d, tok_size
        )
        returned.append((first, second))
    logits = jnp.dot(own, head_here, preferred_element_type=jnp.float32)
    block_hit = jnp.any(
        (block_ids[:, :, None] == column_block[None, None, :]) & live_slot[:, :, None], axis=1
    )
    features = [own] + [in_order(n, f, upper[0]) for n, f in zip(near, far)]
    all_features = jnp.concatenate(features, axis=0)
    blocks = block_hit.shape[0]
    listed = jnp.broadcast_to(
        block_hit[:, None, :], (blocks, token_count // blocks, column_count)
    ).reshape(token_count, column_count)
    teacher_f = teacher.astype(jnp.float32)
    kept = jnp.where(listed, teacher_f, 0.0)
    mass = jnp.sum(kept, axis=1)
    entropy = jnp.sum(jnp.where(listed, teacher_f * jnp.log(teacher_f), 0.0), axis=1)
    kept, early = kept.astype(jnp.bfloat16), jnp.stack([mass, entropy])
    returned, all_features, logits, kept, early = lax.optimization_barrier(
        (returned, all_features, logits, kept, early)
    )
    places = [i for i in range(1, len(upper)) if 1 << i < run]
    logits, stats = local_stats(core_word, logits, kept, early, returned)
    delta, lse, kl = finish(gather_vocab(stats, upper, places, vocab_size), logits, kept)

    deltas = [delta] + [shift_tok(delta, d, tok_size) for d in range(1, tok_size)]
    flags = [upper[i] for i in places]

    def direct(pieces):
        count = len(pieces)
        return [select([pieces[j ^ i] for j in range(count)], flags) for i in range(count)]

    own_pieces = direct(list(gradient(None, head_here, delta, run)))
    own_others = [
        swap_vocab(x.astype(jnp.bfloat16), 2 * i, vocab_size)
        for i, x in enumerate(own_pieces[1:], 1)
    ]
    state = []
    for x in deltas[1:]:
        send, keep = gradient(core_word, head_here, x, run)
        own_others, send = lax.optimization_barrier((own_others, send))
        state.append((keep, swap_vocab(send, 1, vocab_size)))
    all_delta = jnp.concatenate(deltas, axis=0)

    width = 256 if rows % 256 == 0 else rows
    chunks = rows // width
    held = jnp.stack([keep + other.astype(jnp.float32) for keep, other in state], axis=1)
    taken = direct(list(held))
    sends = [x.astype(jnp.bfloat16) for x in taken[1:]]
    sends, all_delta = lax.optimization_barrier((sends, all_delta))
    others = [swap_vocab(x, 2 * (i + 1), vocab_size) for i, x in enumerate(sends)]
    done = (chunks + 1) // 2
    grad_head = head_gradient(all_features, all_delta, None, 0, done, width)
    others, grad_head = lax.optimization_barrier((others, grad_head))
    sums = taken[0]
    for other in others:
        sums = sums + other.astype(jnp.float32)
    own_sum = own_pieces[0]
    for other in own_others:
        own_sum = own_sum + other.astype(jnp.float32)
    send = jnp.where(upper[0], own_sum[0], own_sum[1]).astype(jnp.bfloat16)
    own_sum = jnp.where(upper[0], own_sum[1], own_sum[0])
    own_sum = own_sum + swap_vocab(send, 1, vocab_size).astype(jnp.float32)
    sends = [x.astype(jnp.bfloat16) for x in sums]
    sends, all_delta = lax.optimization_barrier((sends, all_delta))
    others = [shift_tok(x, -d, tok_size) for d, x in enumerate(sends, 1)]
    if done < chunks:
        grad_head = head_gradient(
            all_features, all_delta, grad_head, done * width, chunks - done, width
        )
        others, grad_head = lax.optimization_barrier((others, grad_head))
    sums = [own_sum] + [x.astype(jnp.float32) for x in others]
    blocks = []
    for k in range(tok_size):
        block = sums[k]
        for d in range(1, tok_size):
            block = jnp.where(apart_is[d], sums[(k - d) % tok_size], block)
        blocks.append(block)
    total = blocks[0]
    for k in range(1, tok_size):
        pairs = [(v, (v + k * run) % vocab_size) for v in range(vocab_size)]
        total = total + lax.ppermute(
            blocks[k].astype(jnp.bfloat16), "vocab", pairs
        ).astype(jnp.float32)
    grad_hidden = total.T
    return (lse, kl, grad_hidden, grad_head)


def solution(mesh):
    placed = (P("tok", None), P("tok", "vocab"), P("tok", "vocab"), P("tok", None), P("tok"))
    return jax.shard_map(
        per_device,
        mesh=mesh,
        in_specs=placed,
        out_specs=(P("tok"), P("tok"), P("tok", "vocab"), P("tok", "vocab")),
        check_vma=False,
    )
```

```python
import functools

import jax
import jax.numpy as jnp
from jax import lax
from jax.experimental import pallas as pl
from jax.experimental.pallas import tpu as pltpu
from jax.sharding import PartitionSpec as P

BLK = 512


loss_scale = 1024.0
VMEM_LIMIT = 16 << 20
STEP = 16


def shift_tok(x, offset, size):
    return lax.ppermute(x, "tok", [(i, (i + offset) % size) for i in range(size)])


def swap_vocab(x, bit, size):
    return lax.ppermute(x, "vocab", [(i, i ^ bit) for i in range(size)])


def in_order(mine, other, upper):
    return jnp.concatenate(
        [jnp.where(upper, other, mine), jnp.where(upper, mine, other)], axis=0
    )


def select(options, flags):
    for flag in flags:
        options = [jnp.where(flag, high, low) for low, high in zip(options[::2], options[1::2])]
    return options[0]


def gather_vocab(stats, upper, places, size):
    pair = in_order(stats[None], swap_vocab(stats[None], 1, size), upper[0])
    count = 1 << len(places)
    options = [pair] + [swap_vocab(pair, 2 * offset, size) for offset in range(1, count)]
    flags = [upper[i] for i in places]
    gathered = jnp.concatenate(
        [select([options[j ^ i] for i in range(count)], flags) for j in range(count)], axis=0
    )
    for i in range(len(places) + 1, len(upper)):
        gathered = in_order(gathered, swap_vocab(gathered, 1 << i, size), upper[i])
    return gathered


def load_kernel(head_ref, held_ref, sems):
    steps = sems.shape[0]
    depth = head_ref.shape[0] // steps
    parts = [pl.ds(k * depth, depth) for k in range(steps)]
    copies = [
        pltpu.make_async_copy(head_ref.at[part], held_ref.at[part], sems.at[k])
        for k, part in enumerate(parts)
    ]
    for copy in copies:
        copy.start()
    for copy in copies:
        copy.wait()


def load(head):
    steps = 4
    return pl.pallas_call(
        load_kernel,
        out_shape=pltpu.VMEM(head.shape, head.dtype),
        in_specs=[pl.BlockSpec(memory_space=pltpu.HBM)],
        out_specs=pl.BlockSpec(memory_space=pltpu.VMEM),
        scratch_shapes=[pltpu.SemaphoreType.DMA((steps,))],
        compiler_params=pltpu.CompilerParams(vmem_limit_bytes=VMEM_LIMIT),
        cost_estimate=pl.CostEstimate(
            flops=0, bytes_accessed=4 * head.size, transcendentals=0
        ),
        name="load_head",
    )(pltpu.with_memory_space_constraint(head, pltpu.HBM))


def stats_kernel(core_ref, own_ref, kept_ref, early_ref, *refs):
    parts, (logits_ref, stats_ref, turned_ref) = refs[:-3], refs[-3:]
    half = own_ref.shape[0] // 2
    lane = lax.broadcasted_iota(jnp.int32, (STEP, 128), 1)
    groups = [(core_ref[0], 0, half // 2), (core_ref[0], half // 2, half // 2)]
    groups.append((1 - core_ref[0], 0, half))
    for place, (side, first, count) in enumerate(groups):
        start = side * half + first
        for r in range(0, count, STEP):
            rows = pl.ds(pl.multiple_of(start + r, STEP), STEP)
            logits = own_ref[rows, :]
            for part in parts[place::3]:
                logits = logits + part[r : r + STEP, :]
            logits_ref[rows, :] = logits
            top = jnp.max(logits, axis=1, keepdims=True)
            total = jnp.sum(jnp.exp(logits - top), axis=1, keepdims=True)
            dot = jnp.sum(kept_ref[rows, :].astype(jnp.float32) * logits, axis=1, keepdims=True)
            turned_ref[rows, :] = jnp.where(lane == 0, top, jnp.where(lane == 1, total, dot))
    turned = turned_ref[...].T
    stats_ref[0:2, :] = turned[0:2]
    stats_ref[2:3, :] = early_ref[0:1, :]
    stats_ref[3:4, :] = early_ref[1:2, :] - turned[2:3]


def local_stats(core, own_logits, kept, early, returned):
    in_vmem = pl.BlockSpec(memory_space=pltpu.VMEM)
    parts = [x for pair in returned for x in pair]
    arrays = [
        pltpu.with_memory_space_constraint(x, pltpu.VMEM) for x in (own_logits, kept, early, *parts)
    ]
    return pl.pallas_call(
        stats_kernel,
        out_shape=(
            pltpu.VMEM(own_logits.shape, jnp.float32),
            pltpu.VMEM((4, own_logits.shape[0]), jnp.float32),
        ),
        in_specs=[pl.BlockSpec(memory_space=pltpu.SMEM)] + [in_vmem] * len(arrays),
        out_specs=(in_vmem, in_vmem),
        scratch_shapes=[pltpu.VMEM((own_logits.shape[0], 128), jnp.float32)],
        compiler_params=pltpu.CompilerParams(vmem_limit_bytes=VMEM_LIMIT),
        cost_estimate=pl.CostEstimate(
            flops=8 * own_logits.size,
            bytes_accessed=12 * own_logits.size,
            transcendentals=own_logits.size,
        ),
        name="local_stats",
    )(core, *arrays)


def delta_kernel(gathered_ref, logits_ref, kept_ref, delta_ref, lse_ref, kl_ref):
    shards = [gathered_ref[i] for i in range(gathered_ref.shape[0])]
    top = shards[0][0:1]
    for x in shards[1:]:
        top = jnp.maximum(top, x[0:1])
    total, mass, part = 0.0, 0.0, 0.0
    for x in shards:
        total = total + x[1:2] * jnp.exp(x[0:1] - top)
        mass, part = mass + x[2:3], part + x[3:4]
    lse = top + jnp.log(total)
    lse_ref[...] = lse
    kl_ref[...] = part / mass - jnp.log(mass) + lse
    row = lax.broadcasted_iota(jnp.int32, (128, lse.shape[1]), 0)
    turned = jnp.where(row == 0, lse, 1.0 / mass).T
    lse_column, scale_column = turned[:, 0:1], turned[:, 1:2]
    for r in range(0, logits_ref.shape[0], STEP):
        rows = slice(r, r + STEP)
        student = jnp.exp(logits_ref[rows, :] - lse_column[rows])
        kept = kept_ref[rows, :].astype(jnp.float32) * scale_column[rows]
        delta_ref[rows, :] = (loss_scale * (student - kept)).astype(jnp.bfloat16)


def finish(gathered, logits, kept):
    tokens = logits.shape[0]
    in_vmem = pl.BlockSpec(memory_space=pltpu.VMEM)
    delta, lse, kl = pl.pallas_call(
        delta_kernel,
        out_shape=(
            pltpu.VMEM(logits.shape, jnp.bfloat16),
            jax.ShapeDtypeStruct((1, tokens), jnp.float32),
            jax.ShapeDtypeStruct((1, tokens), jnp.float32),
        ),
        in_specs=[in_vmem] * 3,
        out_specs=(in_vmem, in_vmem, in_vmem),
        compiler_params=pltpu.CompilerParams(vmem_limit_bytes=VMEM_LIMIT),
        cost_estimate=pl.CostEstimate(
            flops=8 * logits.size, bytes_accessed=8 * logits.size, transcendentals=logits.size
        ),
        name="delta",
    )(*[pltpu.with_memory_space_constraint(x, pltpu.VMEM) for x in (gathered, logits, kept)])
    return delta, lse.reshape(tokens), kl.reshape(tokens)


def write_pieces(k, head_rows, delta_ref, upper, send_ref, keep_ref):
    rows = send_ref.shape[1]
    block = lax.dot_general(
        head_rows, delta_ref[...], (((1,), (1,)), ((), ())), preferred_element_type=jnp.float32
    )
    low, high = block[:rows], block[rows:]
    send_ref[k] = jnp.where(upper, low, high).astype(jnp.bfloat16)
    keep_ref[k] = jnp.where(upper, high, low)


def gradient_kernel(core_ref, head_ref, delta_ref, send_ref, keep_ref):
    upper = core_ref[0] == 1
    pairs, rows, _ = send_ref.shape
    for k in range(pairs):
        head_rows = head_ref[2 * k * rows : 2 * (k + 1) * rows, :]
        write_pieces(k, head_rows, delta_ref, upper, send_ref, keep_ref)


def own_gradient_kernel(head_ref, delta_ref, out_ref):
    pairs, _, rows, _ = out_ref.shape
    for k in range(pairs):
        block = lax.dot_general(
            head_ref[2 * k * rows : 2 * (k + 1) * rows, :],
            delta_ref[...],
            (((1,), (1,)), ((), ())),
            preferred_element_type=jnp.float32,
        )
        out_ref[k, 0] = block[:rows]
        out_ref[k, 1] = block[rows:]


def gradient(core, head, delta, run):
    rows = head.shape[0] // run
    shape = (run // 2, rows, delta.shape[0])
    in_vmem = pl.BlockSpec(memory_space=pltpu.VMEM)
    if core is None:
        outs = pltpu.VMEM((run // 2, 2, *shape[1:]), jnp.float32)
    else:
        outs = (pltpu.VMEM(shape, jnp.bfloat16), pltpu.VMEM(shape, jnp.float32))
    arrays = [pltpu.with_memory_space_constraint(x, pltpu.VMEM) for x in (head, delta)]
    return pl.pallas_call(
        own_gradient_kernel if core is None else gradient_kernel,
        out_shape=outs,
        in_specs=([] if core is None else [pl.BlockSpec(memory_space=pltpu.SMEM)]) + [in_vmem] * 2,
        out_specs=in_vmem if core is None else (in_vmem, in_vmem),
        compiler_params=pltpu.CompilerParams(vmem_limit_bytes=VMEM_LIMIT),
        cost_estimate=pl.CostEstimate(
            flops=2 * head.size * delta.shape[0],
            bytes_accessed=2 * (head.size + delta.size),
            transcendentals=0,
        ),
        name="partial_gradient",
    )(*([] if core is None else [core]), *arrays)


def head_gradient_kernel(steps, start, width, *refs):
    features_ref, delta_ref, out_ref, held_ref, sems = refs[0], refs[1], *refs[-3:]
    copies = []
    for k in range(steps):
        block = lax.dot_general(
            features_ref[:, start + k * width : start + (k + 1) * width],
            delta_ref[...],
            (((0,), (0,)), ((), ())),
            preferred_element_type=jnp.float32,
        )
        held_ref[k] = block.astype(jnp.bfloat16)
        copy = pltpu.make_async_copy(
            held_ref.at[k], out_ref.at[pl.ds(start + k * width, width)], sems.at[k]
        )
        copy.start()
        copies.append(copy)
    for copy in copies:
        copy.wait()


def head_gradient(features, delta, out, start, steps, width):
    columns = delta.shape[1]
    in_vmem = pl.BlockSpec(memory_space=pltpu.VMEM)
    in_hbm = pl.BlockSpec(memory_space=pltpu.HBM)
    return pl.pallas_call(
        functools.partial(head_gradient_kernel, steps, start, width),
        out_shape=jax.ShapeDtypeStruct((features.shape[1], columns), jnp.bfloat16),
        in_specs=[in_vmem, in_vmem] + ([] if out is None else [in_hbm]),
        out_specs=in_hbm,
        scratch_shapes=[
            pltpu.VMEM((steps, width, columns), jnp.bfloat16),
            pltpu.SemaphoreType.DMA((steps,)),
        ],
        input_output_aliases={} if out is None else {2: 0},
        compiler_params=pltpu.CompilerParams(vmem_limit_bytes=VMEM_LIMIT),
        cost_estimate=pl.CostEstimate(
            flops=2 * steps * width * delta.size,
            bytes_accessed=2 * (features.size + delta.size + steps * width * columns),
            transcendentals=0,
        ),
        name="head_gradient",
    )(features, delta, *([] if out is None else [out]))


def per_device(hidden, head, teacher, block_ids, counts):
    tok_size = lax.axis_size("tok")
    vocab_size = lax.axis_size("vocab")
    tok_index = lax.axis_index("tok")
    vocab_index = lax.axis_index("vocab")
    token_count = hidden.shape[0]
    rows, column_count = head.shape
    run = vocab_size // tok_size
    half = token_count // 2
    core = vocab_index & 1

    def columns_of(index, first, count):
        return lax.dynamic_slice(hidden, (first, index * rows), (count, rows))

    quarter = half // 2
    near, later = [
        [
            shift_tok(
                columns_of(lax.rem(tok_index + d, tok_size), core * half + first, quarter),
                d,
                tok_size,
            )
            for d in range(1, tok_size)
        ]
        for first in (0, quarter)
    ]
    upper = []
    while 1 << len(upper) < vocab_size:
        upper.append((vocab_index & (1 << len(upper))) != 0)
    high = lax.div(vocab_index, run)
    apart = lax.rem(tok_index + tok_size - high, tok_size)
    apart_is = [apart == d for d in range(tok_size)]
    first_column = vocab_index * column_count
    column_block = (first_column + jnp.arange(column_count, dtype=jnp.int32)) // BLK
    live_slot = jnp.arange(block_ids.shape[1], dtype=jnp.int32)[None, :] < counts[:, None]
    core_word = core.reshape(1)
    tok_is = [tok_index == d for d in range(tok_size)]
    head, upper, apart_is, tok_is, column_block, live_slot, core_word = lax.optimization_barrier(
        (head, upper, apart_is, tok_is, column_block, live_slot, core_word)
    )
    head_here = load(head)
    near, head_here, column_block, teacher, hidden = lax.optimization_barrier(
        (near, head_here, column_block, teacher, hidden)
    )
    products = [jnp.dot(x, head_here, preferred_element_type=jnp.float32) for x in near]
    returned = [[shift_tok(x, -d, tok_size)] for d, x in enumerate(products, 1)]
    later, _ = lax.optimization_barrier((later, products))
    near = [jnp.concatenate(pair, axis=0) for pair in zip(near, later)]
    far = [swap_vocab(x, 1, vocab_size) for x in near]
    for d in range(1, tok_size):
        for x in (later[d - 1], far[d - 1]):
            returned[d - 1].append(
                shift_tok(
                    jnp.dot(x, head_here, preferred_element_type=jnp.float32), -d, tok_size
                )
            )
    own = hidden[:, :rows]
    for d in range(1, tok_size):
        own = jnp.where(tok_is[d], hidden[:, d * rows : (d + 1) * rows], own)
    logits = jnp.dot(own, head_here, preferred_element_type=jnp.float32)
    block_hit = jnp.any(
        (block_ids[:, :, None] == column_block[None, None, :]) & live_slot[:, :, None], axis=1
    )
    features = [own] + [in_order(n, f, upper[0]) for n, f in zip(near, far)]
    all_features = jnp.concatenate(features, axis=0)
    blocks = block_hit.shape[0]
    listed = jnp.broadcast_to(
        block_hit[:, None, :], (blocks, token_count // blocks, column_count)
    ).reshape(token_count, column_count)
    teacher_f = teacher.astype(jnp.float32)
    kept = jnp.where(listed, teacher_f, 0.0)
    mass = jnp.sum(kept, axis=1)
    entropy = jnp.sum(jnp.where(listed, teacher_f * jnp.log(teacher_f), 0.0), axis=1)
    kept, early = kept.astype(jnp.bfloat16), jnp.stack([mass, entropy])
    returned, all_features, logits, kept, early = lax.optimization_barrier(
        (returned, all_features, logits, kept, early)
    )
    places = [i for i in range(1, len(upper)) if 1 << i < run]
    logits, stats = local_stats(core_word, logits, kept, early, returned)
    delta, lse, kl = finish(gather_vocab(stats, upper, places, vocab_size), logits, kept)

    deltas = [delta] + [shift_tok(delta, d, tok_size) for d in range(1, tok_size)]
    flags = [upper[i] for i in places]

    def direct(pieces):
        count = len(pieces)
        return [select([pieces[j ^ i] for j in range(count)], flags) for i in range(count)]

    own_pieces = direct(list(gradient(None, head_here, delta, run)))
    own_others = [
        swap_vocab(x.astype(jnp.bfloat16), 2 * i, vocab_size)
        for i, x in enumerate(own_pieces[1:], 1)
    ]
    state = []
    for x in deltas[1:]:
        send, keep = gradient(core_word, head_here, x, run)
        own_others, send = lax.optimization_barrier((own_others, send))
        state.append((keep, swap_vocab(send, 1, vocab_size)))
    all_delta = jnp.concatenate(deltas, axis=0)

    width = 256 if rows % 256 == 0 else rows
    chunks = rows // width
    held = jnp.stack([keep + other.astype(jnp.float32) for keep, other in state], axis=1)
    taken = direct(list(held))
    sends = [x.astype(jnp.bfloat16) for x in taken[1:]]
    sends, all_delta = lax.optimization_barrier((sends, all_delta))
    others = [swap_vocab(x, 2 * (i + 1), vocab_size) for i, x in enumerate(sends)]
    done = (chunks + 1) // 2
    grad_head = head_gradient(all_features, all_delta, None, 0, done, width)
    others, grad_head = lax.optimization_barrier((others, grad_head))
    sums = taken[0]
    for other in others:
        sums = sums + other.astype(jnp.float32)
    own_sum = own_pieces[0]
    for other in own_others:
        own_sum = own_sum + other.astype(jnp.float32)
    send = jnp.where(upper[0], own_sum[0], own_sum[1]).astype(jnp.bfloat16)
    own_sum = jnp.where(upper[0], own_sum[1], own_sum[0])
    own_sum = own_sum + swap_vocab(send, 1, vocab_size).astype(jnp.float32)
    sends = [x.astype(jnp.bfloat16) for x in sums]
    sends, all_delta = lax.optimization_barrier((sends, all_delta))
    others = [shift_tok(x, -d, tok_size) for d, x in enumerate(sends, 1)]
    if done < chunks:
        grad_head = head_gradient(
            all_features, all_delta, grad_head, done * width, chunks - done, width
        )
        others, grad_head = lax.optimization_barrier((others, grad_head))
    sums = [own_sum] + [x.astype(jnp.float32) for x in others]
    blocks = []
    for k in range(tok_size):
        block = sums[k]
        for d in range(1, tok_size):
            block = jnp.where(apart_is[d], sums[(k - d) % tok_size], block)
        blocks.append(block)
    total = blocks[0]
    for k in range(1, tok_size):
        pairs = [(v, (v + k * run) % vocab_size) for v in range(vocab_size)]
        total = total + lax.ppermute(
            blocks[k].astype(jnp.bfloat16), "vocab", pairs
        ).astype(jnp.float32)
    grad_hidden = total.T
    return (lse, kl, grad_hidden, grad_head)


def solution(mesh):
    placed = (P("tok", None), P("tok", "vocab"), P("tok", "vocab"), P("tok", None), P("tok"))
    return jax.shard_map(
        per_device,
        mesh=mesh,
        in_specs=placed,
        out_specs=(P("tok"), P("tok"), P("tok", "vocab"), P("tok", "vocab")),
        check_vma=False,
    )
```

```python
import functools

import jax
import jax.numpy as jnp
from jax import lax
from jax.experimental import pallas as pl
from jax.experimental.pallas import tpu as pltpu
from jax.sharding import PartitionSpec as P

BLK = 512


loss_scale = 1024.0
VMEM_LIMIT = 16 << 20
STEP = 16


def shift_tok(x, offset, size):
    return lax.ppermute(x, "tok", [(i, (i + offset) % size) for i in range(size)])


def swap_vocab(x, bit, size):
    return lax.ppermute(x, "vocab", [(i, i ^ bit) for i in range(size)])


def in_order(mine, other, upper):
    return jnp.concatenate(
        [jnp.where(upper, other, mine), jnp.where(upper, mine, other)], axis=0
    )


def select(options, flags):
    for flag in flags:
        options = [jnp.where(flag, high, low) for low, high in zip(options[::2], options[1::2])]
    return options[0]


def gather_vocab(stats, upper, places, size):
    pair = in_order(stats[None], swap_vocab(stats[None], 1, size), upper[0])
    count = 1 << len(places)
    options = [pair] + [swap_vocab(pair, 2 * offset, size) for offset in range(1, count)]
    flags = [upper[i] for i in places]
    gathered = jnp.concatenate(
        [select([options[j ^ i] for i in range(count)], flags) for j in range(count)], axis=0
    )
    for i in range(len(places) + 1, len(upper)):
        gathered = in_order(gathered, swap_vocab(gathered, 1 << i, size), upper[i])
    return gathered


def load_kernel(head_ref, held_ref, sems):
    steps = sems.shape[0]
    depth = head_ref.shape[0] // steps
    parts = [pl.ds(k * depth, depth) for k in range(steps)]
    copies = [
        pltpu.make_async_copy(head_ref.at[part], held_ref.at[part], sems.at[k])
        for k, part in enumerate(parts)
    ]
    for copy in copies:
        copy.start()
    for copy in copies:
        copy.wait()


def load(head):
    steps = 4
    return pl.pallas_call(
        load_kernel,
        out_shape=pltpu.VMEM(head.shape, head.dtype),
        in_specs=[pl.BlockSpec(memory_space=pltpu.HBM)],
        out_specs=pl.BlockSpec(memory_space=pltpu.VMEM),
        scratch_shapes=[pltpu.SemaphoreType.DMA((steps,))],
        compiler_params=pltpu.CompilerParams(vmem_limit_bytes=VMEM_LIMIT),
        cost_estimate=pl.CostEstimate(
            flops=0, bytes_accessed=4 * head.size, transcendentals=0
        ),
        name="load_head",
    )(pltpu.with_memory_space_constraint(head, pltpu.HBM))


def stats_kernel(core_ref, own_ref, kept_ref, early_ref, *refs):
    parts, (logits_ref, stats_ref, turned_ref) = refs[:-3], refs[-3:]
    half = own_ref.shape[0] // 2
    lane = lax.broadcasted_iota(jnp.int32, (STEP, 128), 1)
    groups = [(core_ref[0], 0, half // 2), (core_ref[0], half // 2, half // 2)]
    groups.append((1 - core_ref[0], 0, half))
    for place, (side, first, count) in enumerate(groups):
        start = side * half + first
        for r in range(0, count, STEP):
            rows = pl.ds(pl.multiple_of(start + r, STEP), STEP)
            logits = own_ref[rows, :]
            for part in parts[place::3]:
                logits = logits + part[r : r + STEP, :]
            logits_ref[rows, :] = logits
            top = jnp.max(logits, axis=1, keepdims=True)
            total = jnp.sum(jnp.exp(logits - top), axis=1, keepdims=True)
            dot = jnp.sum(kept_ref[rows, :].astype(jnp.float32) * logits, axis=1, keepdims=True)
            turned_ref[rows, :] = jnp.where(lane == 0, top, jnp.where(lane == 1, total, dot))
    turned = turned_ref[...].T
    stats_ref[0:2, :] = turned[0:2]
    stats_ref[2:3, :] = early_ref[0:1, :]
    stats_ref[3:4, :] = early_ref[1:2, :] - turned[2:3]


def local_stats(core, own_logits, kept, early, returned):
    in_vmem = pl.BlockSpec(memory_space=pltpu.VMEM)
    parts = [x for pair in returned for x in pair]
    arrays = [
        pltpu.with_memory_space_constraint(x, pltpu.VMEM) for x in (own_logits, kept, early, *parts)
    ]
    return pl.pallas_call(
        stats_kernel,
        out_shape=(
            pltpu.VMEM(own_logits.shape, jnp.float32),
            pltpu.VMEM((4, own_logits.shape[0]), jnp.float32),
        ),
        in_specs=[pl.BlockSpec(memory_space=pltpu.SMEM)] + [in_vmem] * len(arrays),
        out_specs=(in_vmem, in_vmem),
        scratch_shapes=[pltpu.VMEM((own_logits.shape[0], 128), jnp.float32)],
        compiler_params=pltpu.CompilerParams(vmem_limit_bytes=VMEM_LIMIT),
        cost_estimate=pl.CostEstimate(
            flops=8 * own_logits.size,
            bytes_accessed=12 * own_logits.size,
            transcendentals=own_logits.size,
        ),
        name="local_stats",
    )(core, *arrays)


def delta_kernel(gathered_ref, logits_ref, kept_ref, delta_ref, lse_ref, kl_ref):
    shards = [gathered_ref[i] for i in range(gathered_ref.shape[0])]
    top = shards[0][0:1]
    for x in shards[1:]:
        top = jnp.maximum(top, x[0:1])
    total, mass, part = 0.0, 0.0, 0.0
    for x in shards:
        total = total + x[1:2] * jnp.exp(x[0:1] - top)
        mass, part = mass + x[2:3], part + x[3:4]
    lse = top + jnp.log(total)
    lse_ref[...] = lse
    kl_ref[...] = part / mass - jnp.log(mass) + lse
    row = lax.broadcasted_iota(jnp.int32, (128, lse.shape[1]), 0)
    turned = jnp.where(row == 0, lse, 1.0 / mass).T
    lse_column, scale_column = turned[:, 0:1], turned[:, 1:2]
    for r in range(0, logits_ref.shape[0], STEP):
        rows = slice(r, r + STEP)
        student = jnp.exp(logits_ref[rows, :] - lse_column[rows])
        kept = kept_ref[rows, :].astype(jnp.float32) * scale_column[rows]
        delta_ref[rows, :] = (loss_scale * (student - kept)).astype(jnp.bfloat16)


def finish(gathered, logits, kept):
    tokens = logits.shape[0]
    in_vmem = pl.BlockSpec(memory_space=pltpu.VMEM)
    delta, lse, kl = pl.pallas_call(
        delta_kernel,
        out_shape=(
            pltpu.VMEM(logits.shape, jnp.bfloat16),
            jax.ShapeDtypeStruct((1, tokens), jnp.float32),
            jax.ShapeDtypeStruct((1, tokens), jnp.float32),
        ),
        in_specs=[in_vmem] * 3,
        out_specs=(in_vmem, in_vmem, in_vmem),
        compiler_params=pltpu.CompilerParams(vmem_limit_bytes=VMEM_LIMIT),
        cost_estimate=pl.CostEstimate(
            flops=8 * logits.size, bytes_accessed=8 * logits.size, transcendentals=logits.size
        ),
        name="delta",
    )(*[pltpu.with_memory_space_constraint(x, pltpu.VMEM) for x in (gathered, logits, kept)])
    return delta, lse.reshape(tokens), kl.reshape(tokens)


def gradient_kernel(other, core_ref, head_ref, delta_ref, out_ref):
    side = 1 - core_ref[0] if other else core_ref[0]
    pairs, rows, _ = out_ref.shape
    for k in range(pairs):
        if rows % 16 == 0:
            start = pl.multiple_of((2 * k + side) * rows, 16)
            head_rows = head_ref[pl.ds(start, rows), :]
        else:
            head_rows = head_ref[2 * k * rows : 2 * (k + 1) * rows, :]
        block = lax.dot_general(
            head_rows, delta_ref[...], (((1,), (1,)), ((), ())), preferred_element_type=jnp.float32
        )
        if rows % 16:
            block = jnp.where(side == 0, block[:rows], block[rows:])
        out_ref[k] = block.astype(out_ref.dtype)


def own_gradient_kernel(head_ref, delta_ref, out_ref):
    pairs, _, rows, _ = out_ref.shape
    for k in range(pairs):
        block = lax.dot_general(
            head_ref[2 * k * rows : 2 * (k + 1) * rows, :],
            delta_ref[...],
            (((1,), (1,)), ((), ())),
            preferred_element_type=jnp.float32,
        )
        out_ref[k, 0] = block[:rows]
        out_ref[k, 1] = block[rows:]


def gradient(core, head, delta, run, other=False):
    rows = head.shape[0] // run
    shape = (run // 2, rows, delta.shape[0])
    in_vmem = pl.BlockSpec(memory_space=pltpu.VMEM)
    if core is None:
        out = pltpu.VMEM((run // 2, 2, *shape[1:]), jnp.float32)
        kernel = own_gradient_kernel
    else:
        out = pltpu.VMEM(shape, jnp.bfloat16 if other else jnp.float32)
        kernel = functools.partial(gradient_kernel, other)
    arrays = [pltpu.with_memory_space_constraint(x, pltpu.VMEM) for x in (head, delta)]
    return pl.pallas_call(
        kernel,
        out_shape=out,
        in_specs=([] if core is None else [pl.BlockSpec(memory_space=pltpu.SMEM)]) + [in_vmem] * 2,
        out_specs=in_vmem,
        compiler_params=pltpu.CompilerParams(vmem_limit_bytes=VMEM_LIMIT),
        cost_estimate=pl.CostEstimate(
            flops=2 * head.size * delta.shape[0],
            bytes_accessed=2 * (head.size + delta.size),
            transcendentals=0,
        ),
        name="partial_gradient",
    )(*([] if core is None else [core]), *arrays)


def head_gradient_kernel(steps, start, width, *refs):
    features_ref, delta_ref, out_ref, held_ref, sems = refs[0], refs[1], *refs[-3:]
    copies = []
    for k in range(steps):
        block = lax.dot_general(
            features_ref[:, start + k * width : start + (k + 1) * width],
            delta_ref[...],
            (((0,), (0,)), ((), ())),
            preferred_element_type=jnp.float32,
        )
        held_ref[k] = block.astype(jnp.bfloat16)
        copy = pltpu.make_async_copy(
            held_ref.at[k], out_ref.at[pl.ds(start + k * width, width)], sems.at[k]
        )
        copy.start()
        copies.append(copy)
    for copy in copies:
        copy.wait()


def head_gradient(features, delta, out, start, steps, width):
    columns = delta.shape[1]
    in_vmem = pl.BlockSpec(memory_space=pltpu.VMEM)
    in_hbm = pl.BlockSpec(memory_space=pltpu.HBM)
    return pl.pallas_call(
        functools.partial(head_gradient_kernel, steps, start, width),
        out_shape=jax.ShapeDtypeStruct((features.shape[1], columns), jnp.bfloat16),
        in_specs=[in_vmem, in_vmem] + ([] if out is None else [in_hbm]),
        out_specs=in_hbm,
        scratch_shapes=[
            pltpu.VMEM((steps, width, columns), jnp.bfloat16),
            pltpu.SemaphoreType.DMA((steps,)),
        ],
        input_output_aliases={} if out is None else {2: 0},
        compiler_params=pltpu.CompilerParams(vmem_limit_bytes=VMEM_LIMIT),
        cost_estimate=pl.CostEstimate(
            flops=2 * steps * width * delta.size,
            bytes_accessed=2 * (features.size + delta.size + steps * width * columns),
            transcendentals=0,
        ),
        name="head_gradient",
    )(features, delta, *([] if out is None else [out]))


def per_device(hidden, head, teacher, block_ids, counts):
    tok_size = lax.axis_size("tok")
    vocab_size = lax.axis_size("vocab")
    tok_index = lax.axis_index("tok")
    vocab_index = lax.axis_index("vocab")
    token_count = hidden.shape[0]
    rows, column_count = head.shape
    run = vocab_size // tok_size
    half = token_count // 2
    core = vocab_index & 1

    def columns_of(index, first, count):
        return lax.dynamic_slice(hidden, (first, index * rows), (count, rows))

    quarter = half // 2

    def fetched(first):
        return [
            columns_of(lax.rem(tok_index + d, tok_size), core * half + first, quarter)
            for d in range(1, tok_size)
        ]

    def fetch(slices):
        return [shift_tok(x, d, tok_size) for d, x in enumerate(slices, 1)]

    wanted = fetched(0)
    hidden, wanted = lax.optimization_barrier((hidden, wanted))
    near, later = fetch(wanted), fetched(quarter)
    upper = []
    while 1 << len(upper) < vocab_size:
        upper.append((vocab_index & (1 << len(upper))) != 0)
    high = lax.div(vocab_index, run)
    apart = lax.rem(tok_index + tok_size - high, tok_size)
    apart_is = [apart == d for d in range(tok_size)]
    first_column = vocab_index * column_count
    column_block = (first_column + jnp.arange(column_count, dtype=jnp.int32)) // BLK
    live_slot = jnp.arange(block_ids.shape[1], dtype=jnp.int32)[None, :] < counts[:, None]
    core_word = core.reshape(1)
    tok_is = [tok_index == d for d in range(tok_size)]
    later, head, upper, apart_is, tok_is, column_block, live_slot, core_word = lax.optimization_barrier(
        (later, head, upper, apart_is, tok_is, column_block, live_slot, core_word)
    )
    head_here = load(head)
    later, head_here = lax.optimization_barrier((later, head_here))
    later = fetch(later)
    near, head_here, column_block, teacher, hidden = lax.optimization_barrier(
        (near, head_here, column_block, teacher, hidden)
    )
    products = [jnp.dot(x, head_here, preferred_element_type=jnp.float32) for x in near]
    returned = [[shift_tok(x, -d, tok_size)] for d, x in enumerate(products, 1)]
    later, _ = lax.optimization_barrier((later, products))
    near = [jnp.concatenate(pair, axis=0) for pair in zip(near, later)]
    far = [swap_vocab(x, 1, vocab_size) for x in near]
    for d in range(1, tok_size):
        for x in (later[d - 1], far[d - 1]):
            returned[d - 1].append(
                shift_tok(
                    jnp.dot(x, head_here, preferred_element_type=jnp.float32), -d, tok_size
                )
            )
    own = hidden[:, :rows]
    for d in range(1, tok_size):
        own = jnp.where(tok_is[d], hidden[:, d * rows : (d + 1) * rows], own)
    logits = jnp.dot(own, head_here, preferred_element_type=jnp.float32)
    block_hit = jnp.any(
        (block_ids[:, :, None] == column_block[None, None, :]) & live_slot[:, :, None], axis=1
    )
    features = [own] + [in_order(n, f, upper[0]) for n, f in zip(near, far)]
    all_features = jnp.concatenate(features, axis=0)
    blocks = block_hit.shape[0]
    listed = jnp.broadcast_to(
        block_hit[:, None, :], (blocks, token_count // blocks, column_count)
    ).reshape(token_count, column_count)
    teacher_f = teacher.astype(jnp.float32)
    kept = jnp.where(listed, teacher_f, 0.0)
    mass = jnp.sum(kept, axis=1)
    entropy = jnp.sum(jnp.where(listed, teacher_f * jnp.log(teacher_f), 0.0), axis=1)
    kept, early = kept.astype(jnp.bfloat16), jnp.stack([mass, entropy])
    returned, all_features, logits, kept, early = lax.optimization_barrier(
        (returned, all_features, logits, kept, early)
    )
    places = [i for i in range(1, len(upper)) if 1 << i < run]
    logits, stats = local_stats(core_word, logits, kept, early, returned)
    delta, lse, kl = finish(gather_vocab(stats, upper, places, vocab_size), logits, kept)

    deltas = [delta] + [shift_tok(delta, d, tok_size) for d in range(1, tok_size)]
    flags = [upper[i] for i in places]

    def direct(pieces):
        count = len(pieces)
        return [select([pieces[j ^ i] for j in range(count)], flags) for i in range(count)]

    own_pieces = direct(list(gradient(None, head_here, delta, run)))
    own_others = [
        swap_vocab(x.astype(jnp.bfloat16), 2 * i, vocab_size)
        for i, x in enumerate(own_pieces[1:], 1)
    ]
    state = []
    for x in deltas[1:]:
        send = gradient(core_word, head_here, x, run, other=True)
        own_others, _ = lax.optimization_barrier((own_others, send))
        x, _ = lax.optimization_barrier((x, send))
        keep = gradient(core_word, head_here, x, run)
        state.append((keep, swap_vocab(send, 1, vocab_size)))
    all_delta = jnp.concatenate(deltas, axis=0)

    width = 256 if rows % 256 == 0 else rows
    chunks = rows // width
    held = jnp.stack([keep + other.astype(jnp.float32) for keep, other in state], axis=1)
    taken = direct(list(held))
    sends = [x.astype(jnp.bfloat16) for x in taken[1:]]
    sends, all_delta = lax.optimization_barrier((sends, all_delta))
    others = [swap_vocab(x, 2 * (i + 1), vocab_size) for i, x in enumerate(sends)]
    done = (chunks + 1) // 2
    grad_head = head_gradient(all_features, all_delta, None, 0, done, width)
    others, grad_head = lax.optimization_barrier((others, grad_head))
    sums = taken[0]
    for other in others:
        sums = sums + other.astype(jnp.float32)
    own_sum = own_pieces[0]
    for other in own_others:
        own_sum = own_sum + other.astype(jnp.float32)
    send = jnp.where(upper[0], own_sum[0], own_sum[1]).astype(jnp.bfloat16)
    own_sum = jnp.where(upper[0], own_sum[1], own_sum[0])
    own_sum = own_sum + swap_vocab(send, 1, vocab_size).astype(jnp.float32)
    sends = [x.astype(jnp.bfloat16) for x in sums]
    sends, all_delta = lax.optimization_barrier((sends, all_delta))
    others = [shift_tok(x, -d, tok_size) for d, x in enumerate(sends, 1)]
    if done < chunks:
        grad_head = head_gradient(
            all_features, all_delta, grad_head, done * width, chunks - done, width
        )
        others, grad_head = lax.optimization_barrier((others, grad_head))
    sums = [own_sum] + [x.astype(jnp.float32) for x in others]
    blocks = []
    for k in range(tok_size):
        block = sums[k]
        for d in range(1, tok_size):
            block = jnp.where(apart_is[d], sums[(k - d) % tok_size], block)
        blocks.append(block)
    total = blocks[0]
    for k in range(1, tok_size):
        pairs = [(v, (v + k * run) % vocab_size) for v in range(vocab_size)]
        total = total + lax.ppermute(
            blocks[k].astype(jnp.bfloat16), "vocab", pairs
        ).astype(jnp.float32)
    grad_hidden = total.T
    return (lse, kl, grad_hidden, grad_head)


def solution(mesh):
    placed = (P("tok", None), P("tok", "vocab"), P("tok", "vocab"), P("tok", None), P("tok"))
    return jax.shard_map(
        per_device,
        mesh=mesh,
        in_specs=placed,
        out_specs=(P("tok"), P("tok"), P("tok", "vocab"), P("tok", "vocab")),
        check_vma=False,
    )
```

```python
import functools

import jax
import jax.numpy as jnp
from jax import lax
from jax.experimental import pallas as pl
from jax.experimental.pallas import tpu as pltpu
from jax.sharding import PartitionSpec as P

BLK = 512


loss_scale = 1024.0
VMEM_LIMIT = 16 << 20
STEP = 16


def shift_tok(x, offset, size):
    return lax.ppermute(x, "tok", [(i, (i + offset) % size) for i in range(size)])


def swap_vocab(x, bit, size):
    return lax.ppermute(x, "vocab", [(i, i ^ bit) for i in range(size)])


def in_order(mine, other, upper):
    return jnp.concatenate(
        [jnp.where(upper, other, mine), jnp.where(upper, mine, other)], axis=0
    )


def select(options, flags):
    for flag in flags:
        options = [jnp.where(flag, high, low) for low, high in zip(options[::2], options[1::2])]
    return options[0]


def gather_vocab(stats, upper, places, size):
    pair = in_order(stats[None], swap_vocab(stats[None], 1, size), upper[0])
    count = 1 << len(places)
    options = [pair] + [swap_vocab(pair, 2 * offset, size) for offset in range(1, count)]
    flags = [upper[i] for i in places]
    gathered = jnp.concatenate(
        [select([options[j ^ i] for i in range(count)], flags) for j in range(count)], axis=0
    )
    for i in range(len(places) + 1, len(upper)):
        gathered = in_order(gathered, swap_vocab(gathered, 1 << i, size), upper[i])
    return gathered


def load_kernel(head_ref, held_ref, sems):
    steps = sems.shape[0]
    depth = head_ref.shape[0] // steps
    parts = [pl.ds(k * depth, depth) for k in range(steps)]
    copies = [
        pltpu.make_async_copy(head_ref.at[part], held_ref.at[part], sems.at[k])
        for k, part in enumerate(parts)
    ]
    for copy in copies:
        copy.start()
    for copy in copies:
        copy.wait()


def load(head):
    steps = 4
    return pl.pallas_call(
        load_kernel,
        out_shape=pltpu.VMEM(head.shape, head.dtype),
        in_specs=[pl.BlockSpec(memory_space=pltpu.HBM)],
        out_specs=pl.BlockSpec(memory_space=pltpu.VMEM),
        scratch_shapes=[pltpu.SemaphoreType.DMA((steps,))],
        compiler_params=pltpu.CompilerParams(vmem_limit_bytes=VMEM_LIMIT),
        cost_estimate=pl.CostEstimate(
            flops=0, bytes_accessed=4 * head.size, transcendentals=0
        ),
        name="load_head",
    )(pltpu.with_memory_space_constraint(head, pltpu.HBM))


def stats_kernel(core_ref, own_ref, kept_ref, early_ref, *refs):
    parts, (logits_ref, stats_ref, turned_ref) = refs[:-3], refs[-3:]
    half = own_ref.shape[0] // 2
    lane = lax.broadcasted_iota(jnp.int32, (STEP, 128), 1)
    groups = [(core_ref[0], 0, half // 2), (core_ref[0], half // 2, half // 2)]
    groups.append((1 - core_ref[0], 0, half))
    for place, (side, first, count) in enumerate(groups):
        start = side * half + first
        for r in range(0, count, STEP):
            rows = pl.ds(pl.multiple_of(start + r, STEP), STEP)
            logits = own_ref[rows, :]
            for part in parts[place::3]:
                logits = logits + part[r : r + STEP, :]
            logits_ref[rows, :] = logits
            top = jnp.max(logits, axis=1, keepdims=True)
            total = jnp.sum(jnp.exp(logits - top), axis=1, keepdims=True)
            dot = jnp.sum(kept_ref[rows, :].astype(jnp.float32) * logits, axis=1, keepdims=True)
            turned_ref[rows, :] = jnp.where(lane == 0, top, jnp.where(lane == 1, total, dot))
    turned = turned_ref[...].T
    stats_ref[0:2, :] = turned[0:2]
    stats_ref[2:3, :] = early_ref[0:1, :]
    stats_ref[3:4, :] = early_ref[1:2, :] - turned[2:3]


def local_stats(core, own_logits, kept, early, returned):
    in_vmem = pl.BlockSpec(memory_space=pltpu.VMEM)
    parts = [x for pair in returned for x in pair]
    arrays = [
        pltpu.with_memory_space_constraint(x, pltpu.VMEM) for x in (own_logits, kept, early, *parts)
    ]
    return pl.pallas_call(
        stats_kernel,
        out_shape=(
            pltpu.VMEM(own_logits.shape, jnp.float32),
            pltpu.VMEM((4, own_logits.shape[0]), jnp.float32),
        ),
        in_specs=[pl.BlockSpec(memory_space=pltpu.SMEM)] + [in_vmem] * len(arrays),
        out_specs=(in_vmem, in_vmem),
        scratch_shapes=[pltpu.VMEM((own_logits.shape[0], 128), jnp.float32)],
        compiler_params=pltpu.CompilerParams(vmem_limit_bytes=VMEM_LIMIT),
        cost_estimate=pl.CostEstimate(
            flops=8 * own_logits.size,
            bytes_accessed=12 * own_logits.size,
            transcendentals=own_logits.size,
        ),
        name="local_stats",
    )(core, *arrays)


def delta_kernel(gathered_ref, logits_ref, kept_ref, delta_ref, lse_ref, kl_ref):
    shards = [gathered_ref[i] for i in range(gathered_ref.shape[0])]
    top = shards[0][0:1]
    for x in shards[1:]:
        top = jnp.maximum(top, x[0:1])
    total, mass, part = 0.0, 0.0, 0.0
    for x in shards:
        total = total + x[1:2] * jnp.exp(x[0:1] - top)
        mass, part = mass + x[2:3], part + x[3:4]
    lse = top + jnp.log(total)
    lse_ref[...] = lse
    kl_ref[...] = part / mass - jnp.log(mass) + lse
    row = lax.broadcasted_iota(jnp.int32, (128, lse.shape[1]), 0)
    turned = jnp.where(row == 0, lse, 1.0 / mass).T
    lse_column, scale_column = turned[:, 0:1], turned[:, 1:2]
    for r in range(0, logits_ref.shape[0], STEP):
        rows = slice(r, r + STEP)
        student = jnp.exp(logits_ref[rows, :] - lse_column[rows])
        kept = kept_ref[rows, :].astype(jnp.float32) * scale_column[rows]
        delta_ref[rows, :] = (loss_scale * (student - kept)).astype(jnp.bfloat16)


def finish(gathered, logits, kept):
    tokens = logits.shape[0]
    in_vmem = pl.BlockSpec(memory_space=pltpu.VMEM)
    delta, lse, kl = pl.pallas_call(
        delta_kernel,
        out_shape=(
            pltpu.VMEM(logits.shape, jnp.bfloat16),
            jax.ShapeDtypeStruct((1, tokens), jnp.float32),
            jax.ShapeDtypeStruct((1, tokens), jnp.float32),
        ),
        in_specs=[in_vmem] * 3,
        out_specs=(in_vmem, in_vmem, in_vmem),
        compiler_params=pltpu.CompilerParams(vmem_limit_bytes=VMEM_LIMIT),
        cost_estimate=pl.CostEstimate(
            flops=8 * logits.size, bytes_accessed=8 * logits.size, transcendentals=logits.size
        ),
        name="delta",
    )(*[pltpu.with_memory_space_constraint(x, pltpu.VMEM) for x in (gathered, logits, kept)])
    return delta, lse.reshape(tokens), kl.reshape(tokens)


def gradient_kernel(other, core_ref, head_ref, delta_ref, out_ref):
    side = 1 - core_ref[0] if other else core_ref[0]
    pairs, rows, _ = out_ref.shape
    for k in range(pairs):
        if rows % 16 == 0:
            start = pl.multiple_of((2 * k + side) * rows, 16)
            head_rows = head_ref[pl.ds(start, rows), :]
        else:
            head_rows = head_ref[2 * k * rows : 2 * (k + 1) * rows, :]
        block = lax.dot_general(
            head_rows, delta_ref[...], (((1,), (1,)), ((), ())), preferred_element_type=jnp.float32
        )
        if rows % 16:
            block = jnp.where(side == 0, block[:rows], block[rows:])
        out_ref[k] = block.astype(out_ref.dtype)


def own_gradient_kernel(head_ref, delta_ref, out_ref):
    pairs, _, rows, _ = out_ref.shape
    for k in range(pairs):
        block = lax.dot_general(
            head_ref[2 * k * rows : 2 * (k + 1) * rows, :],
            delta_ref[...],
            (((1,), (1,)), ((), ())),
            preferred_element_type=jnp.float32,
        )
        out_ref[k, 0] = block[:rows]
        out_ref[k, 1] = block[rows:]


def gradient(core, head, delta, run, other=False):
    rows = head.shape[0] // run
    shape = (run // 2, rows, delta.shape[0])
    in_vmem = pl.BlockSpec(memory_space=pltpu.VMEM)
    if core is None:
        out = pltpu.VMEM((run // 2, 2, *shape[1:]), jnp.float32)
        kernel = own_gradient_kernel
    else:
        out = pltpu.VMEM(shape, jnp.bfloat16 if other else jnp.float32)
        kernel = functools.partial(gradient_kernel, other)
    arrays = [pltpu.with_memory_space_constraint(x, pltpu.VMEM) for x in (head, delta)]
    return pl.pallas_call(
        kernel,
        out_shape=out,
        in_specs=([] if core is None else [pl.BlockSpec(memory_space=pltpu.SMEM)]) + [in_vmem] * 2,
        out_specs=in_vmem,
        compiler_params=pltpu.CompilerParams(vmem_limit_bytes=VMEM_LIMIT),
        cost_estimate=pl.CostEstimate(
            flops=2 * head.size * delta.shape[0],
            bytes_accessed=2 * (head.size + delta.size),
            transcendentals=0,
        ),
        name="partial_gradient",
    )(*([] if core is None else [core]), *arrays)


def head_gradient_kernel(steps, start, width, *refs):
    features_ref, delta_ref, out_ref, held_ref, sems = refs[0], refs[1], *refs[-3:]
    copies = []
    for k in range(steps):
        block = lax.dot_general(
            features_ref[:, start + k * width : start + (k + 1) * width],
            delta_ref[...],
            (((0,), (0,)), ((), ())),
            preferred_element_type=jnp.float32,
        )
        held_ref[k] = block.astype(jnp.bfloat16)
        copy = pltpu.make_async_copy(
            held_ref.at[k], out_ref.at[pl.ds(start + k * width, width)], sems.at[k]
        )
        copy.start()
        copies.append(copy)
    for copy in copies:
        copy.wait()


def head_gradient(features, delta, out, start, steps, width):
    columns = delta.shape[1]
    in_vmem = pl.BlockSpec(memory_space=pltpu.VMEM)
    in_hbm = pl.BlockSpec(memory_space=pltpu.HBM)
    return pl.pallas_call(
        functools.partial(head_gradient_kernel, steps, start, width),
        out_shape=jax.ShapeDtypeStruct((features.shape[1], columns), jnp.bfloat16),
        in_specs=[in_vmem, in_vmem] + ([] if out is None else [in_hbm]),
        out_specs=in_hbm,
        scratch_shapes=[
            pltpu.VMEM((steps, width, columns), jnp.bfloat16),
            pltpu.SemaphoreType.DMA((steps,)),
        ],
        input_output_aliases={} if out is None else {2: 0},
        compiler_params=pltpu.CompilerParams(vmem_limit_bytes=VMEM_LIMIT),
        cost_estimate=pl.CostEstimate(
            flops=2 * steps * width * delta.size,
            bytes_accessed=2 * (features.size + delta.size + steps * width * columns),
            transcendentals=0,
        ),
        name="head_gradient",
    )(features, delta, *([] if out is None else [out]))


def per_device(hidden, head, teacher, block_ids, counts):
    tok_size = lax.axis_size("tok")
    vocab_size = lax.axis_size("vocab")
    tok_index = lax.axis_index("tok")
    vocab_index = lax.axis_index("vocab")
    token_count = hidden.shape[0]
    rows, column_count = head.shape
    run = vocab_size // tok_size
    half = token_count // 2
    core = vocab_index & 1

    def columns_of(index, first, count):
        return lax.dynamic_slice(hidden, (first, index * rows), (count, rows))

    quarter = half // 2
    part = quarter // 2
    second = lax.div(vocab_index, 2) & 1
    near, later = [
        [
            shift_tok(
                columns_of(lax.rem(tok_index + d, tok_size), core * half + first, count),
                d,
                tok_size,
            )
            for d in range(1, tok_size)
        ]
        for first, count in ((0, quarter), (quarter + second * part, part))
    ]
    upper = []
    while 1 << len(upper) < vocab_size:
        upper.append((vocab_index & (1 << len(upper))) != 0)
    high = lax.div(vocab_index, run)
    apart = lax.rem(tok_index + tok_size - high, tok_size)
    apart_is = [apart == d for d in range(tok_size)]
    first_column = vocab_index * column_count
    column_block = (first_column + jnp.arange(column_count, dtype=jnp.int32)) // BLK
    live_slot = jnp.arange(block_ids.shape[1], dtype=jnp.int32)[None, :] < counts[:, None]
    core_word = core.reshape(1)
    tok_is = [tok_index == d for d in range(tok_size)]
    head, upper, apart_is, tok_is, column_block, live_slot, core_word = lax.optimization_barrier(
        (head, upper, apart_is, tok_is, column_block, live_slot, core_word)
    )
    head_here = load(head)
    near, head_here, column_block, teacher, hidden = lax.optimization_barrier(
        (near, head_here, column_block, teacher, hidden)
    )
    products = [jnp.dot(x, head_here, preferred_element_type=jnp.float32) for x in near]
    returned = [[shift_tok(x, -d, tok_size)] for d, x in enumerate(products, 1)]
    later, _ = lax.optimization_barrier((later, products))
    later = [in_order(x, swap_vocab(x, 2, vocab_size), upper[1]) for x in later]
    near = [jnp.concatenate(pair, axis=0) for pair in zip(near, later)]
    far = [swap_vocab(x, 1, vocab_size) for x in near]
    for d in range(1, tok_size):
        for x in (later[d - 1], far[d - 1]):
            returned[d - 1].append(
                shift_tok(
                    jnp.dot(x, head_here, preferred_element_type=jnp.float32), -d, tok_size
                )
            )
    own = hidden[:, :rows]
    for d in range(1, tok_size):
        own = jnp.where(tok_is[d], hidden[:, d * rows : (d + 1) * rows], own)
    logits = jnp.dot(own, head_here, preferred_element_type=jnp.float32)
    block_hit = jnp.any(
        (block_ids[:, :, None] == column_block[None, None, :]) & live_slot[:, :, None], axis=1
    )
    features = [own] + [in_order(n, f, upper[0]) for n, f in zip(near, far)]
    all_features = jnp.concatenate(features, axis=0)
    blocks = block_hit.shape[0]
    listed = jnp.broadcast_to(
        block_hit[:, None, :], (blocks, token_count // blocks, column_count)
    ).reshape(token_count, column_count)
    teacher_f = teacher.astype(jnp.float32)
    kept = jnp.where(listed, teacher_f, 0.0)
    mass = jnp.sum(kept, axis=1)
    entropy = jnp.sum(jnp.where(listed, teacher_f * jnp.log(teacher_f), 0.0), axis=1)
    kept, early = kept.astype(jnp.bfloat16), jnp.stack([mass, entropy])
    returned, all_features, logits, kept, early = lax.optimization_barrier(
        (returned, all_features, logits, kept, early)
    )
    places = [i for i in range(1, len(upper)) if 1 << i < run]
    logits, stats = local_stats(core_word, logits, kept, early, returned)
    delta, lse, kl = finish(gather_vocab(stats, upper, places, vocab_size), logits, kept)

    deltas = [delta] + [shift_tok(delta, d, tok_size) for d in range(1, tok_size)]
    flags = [upper[i] for i in places]

    def direct(pieces):
        count = len(pieces)
        return [select([pieces[j ^ i] for j in range(count)], flags) for i in range(count)]

    own_pieces = direct(list(gradient(None, head_here, delta, run)))
    own_others = [
        swap_vocab(x.astype(jnp.bfloat16), 2 * i, vocab_size)
        for i, x in enumerate(own_pieces[1:], 1)
    ]
    state = []
    for x in deltas[1:]:
        send = gradient(core_word, head_here, x, run, other=True)
        own_others, _ = lax.optimization_barrier((own_others, send))
        x, _ = lax.optimization_barrier((x, send))
        keep = gradient(core_word, head_here, x, run)
        state.append((keep, swap_vocab(send, 1, vocab_size)))
    all_delta = jnp.concatenate(deltas, axis=0)

    width = 256 if rows % 256 == 0 else rows
    chunks = rows // width
    held = jnp.stack([keep + other.astype(jnp.float32) for keep, other in state], axis=1)
    taken = direct(list(held))
    sends = [x.astype(jnp.bfloat16) for x in taken[1:]]
    sends, all_delta = lax.optimization_barrier((sends, all_delta))
    others = [swap_vocab(x, 2 * (i + 1), vocab_size) for i, x in enumerate(sends)]
    done = (chunks + 1) // 2
    grad_head = head_gradient(all_features, all_delta, None, 0, done, width)
    others, grad_head = lax.optimization_barrier((others, grad_head))
    sums = taken[0]
    for other in others:
        sums = sums + other.astype(jnp.float32)
    own_sum = own_pieces[0]
    for other in own_others:
        own_sum = own_sum + other.astype(jnp.float32)
    send = jnp.where(upper[0], own_sum[0], own_sum[1]).astype(jnp.bfloat16)
    own_sum = jnp.where(upper[0], own_sum[1], own_sum[0])
    own_sum = own_sum + swap_vocab(send, 1, vocab_size).astype(jnp.float32)
    sends = [x.astype(jnp.bfloat16) for x in sums]
    sends, all_delta = lax.optimization_barrier((sends, all_delta))
    others = [shift_tok(x, -d, tok_size) for d, x in enumerate(sends, 1)]
    if done < chunks:
        grad_head = head_gradient(
            all_features, all_delta, grad_head, done * width, chunks - done, width
        )
        others, grad_head = lax.optimization_barrier((others, grad_head))
    sums = [own_sum] + [x.astype(jnp.float32) for x in others]
    blocks = []
    for k in range(tok_size):
        block = sums[k]
        for d in range(1, tok_size):
            block = jnp.where(apart_is[d], sums[(k - d) % tok_size], block)
        blocks.append(block)
    total = blocks[0]
    for k in range(1, tok_size):
        pairs = [(v, (v + k * run) % vocab_size) for v in range(vocab_size)]
        total = total + lax.ppermute(
            blocks[k].astype(jnp.bfloat16), "vocab", pairs
        ).astype(jnp.float32)
    grad_hidden = total.T
    return (lse, kl, grad_hidden, grad_head)


def solution(mesh):
    placed = (P("tok", None), P("tok", "vocab"), P("tok", "vocab"), P("tok", None), P("tok"))
    return jax.shard_map(
        per_device,
        mesh=mesh,
        in_specs=placed,
        out_specs=(P("tok"), P("tok"), P("tok", "vocab"), P("tok", "vocab")),
        check_vma=False,
    )
```

```python
import functools

import jax
import jax.numpy as jnp
from jax import lax
from jax.experimental import pallas as pl
from jax.experimental.pallas import tpu as pltpu
from jax.sharding import PartitionSpec as P

BLK = 512


loss_scale = 1024.0
VMEM_LIMIT = 16 << 20
STEP = 16


def shift_tok(x, offset, size):
    return lax.ppermute(x, "tok", [(i, (i + offset) % size) for i in range(size)])


def swap_vocab(x, bit, size):
    return lax.ppermute(x, "vocab", [(i, i ^ bit) for i in range(size)])


def in_order(mine, other, upper):
    return jnp.concatenate(
        [jnp.where(upper, other, mine), jnp.where(upper, mine, other)], axis=0
    )


def select(options, flags):
    for flag in flags:
        options = [jnp.where(flag, high, low) for low, high in zip(options[::2], options[1::2])]
    return options[0]


def gather_vocab(stats, upper, places, size):
    pair = in_order(stats[None], swap_vocab(stats[None], 1, size), upper[0])
    count = 1 << len(places)
    options = [pair] + [swap_vocab(pair, 2 * offset, size) for offset in range(1, count)]
    flags = [upper[i] for i in places]
    gathered = jnp.concatenate(
        [select([options[j ^ i] for i in range(count)], flags) for j in range(count)], axis=0
    )
    for i in range(len(places) + 1, len(upper)):
        gathered = in_order(gathered, swap_vocab(gathered, 1 << i, size), upper[i])
    return gathered


def load_kernel(head_ref, held_ref, sems):
    steps = sems.shape[0]
    depth = head_ref.shape[0] // steps
    parts = [pl.ds(k * depth, depth) for k in range(steps)]
    copies = [
        pltpu.make_async_copy(head_ref.at[part], held_ref.at[part], sems.at[k])
        for k, part in enumerate(parts)
    ]
    for copy in copies:
        copy.start()
    for copy in copies:
        copy.wait()


def load(head):
    steps = 4
    return pl.pallas_call(
        load_kernel,
        out_shape=pltpu.VMEM(head.shape, head.dtype),
        in_specs=[pl.BlockSpec(memory_space=pltpu.HBM)],
        out_specs=pl.BlockSpec(memory_space=pltpu.VMEM),
        scratch_shapes=[pltpu.SemaphoreType.DMA((steps,))],
        compiler_params=pltpu.CompilerParams(vmem_limit_bytes=VMEM_LIMIT),
        cost_estimate=pl.CostEstimate(
            flops=0, bytes_accessed=4 * head.size, transcendentals=0
        ),
        name="load_head",
    )(pltpu.with_memory_space_constraint(head, pltpu.HBM))


def stats_kernel(core_ref, own_ref, kept_ref, early_ref, *refs):
    parts, (logits_ref, stats_ref, turned_ref) = refs[:-3], refs[-3:]
    half = own_ref.shape[0] // 2
    lane = lax.broadcasted_iota(jnp.int32, (STEP, 128), 1)
    groups = [(core_ref[0], 0, half // 2), (core_ref[0], half // 2, half // 2)]
    groups.append((1 - core_ref[0], 0, half))
    for place, (side, first, count) in enumerate(groups):
        start = side * half + first
        for r in range(0, count, STEP):
            rows = pl.ds(pl.multiple_of(start + r, STEP), STEP)
            logits = own_ref[rows, :]
            for part in parts[place::3]:
                logits = logits + part[r : r + STEP, :]
            logits_ref[rows, :] = logits
            top = jnp.max(logits, axis=1, keepdims=True)
            total = jnp.sum(jnp.exp(logits - top), axis=1, keepdims=True)
            dot = jnp.sum(kept_ref[rows, :].astype(jnp.float32) * logits, axis=1, keepdims=True)
            turned_ref[rows, :] = jnp.where(lane == 0, top, jnp.where(lane == 1, total, dot))
    turned = turned_ref[...].T
    stats_ref[0:2, :] = turned[0:2]
    stats_ref[2:3, :] = early_ref[0:1, :]
    stats_ref[3:4, :] = early_ref[1:2, :] - turned[2:3]


def local_stats(core, own_logits, kept, early, returned):
    in_vmem = pl.BlockSpec(memory_space=pltpu.VMEM)
    parts = [x for pair in returned for x in pair]
    arrays = [
        pltpu.with_memory_space_constraint(x, pltpu.VMEM) for x in (own_logits, kept, early, *parts)
    ]
    return pl.pallas_call(
        stats_kernel,
        out_shape=(
            pltpu.VMEM(own_logits.shape, jnp.float32),
            pltpu.VMEM((4, own_logits.shape[0]), jnp.float32),
        ),
        in_specs=[pl.BlockSpec(memory_space=pltpu.SMEM)] + [in_vmem] * len(arrays),
        out_specs=(in_vmem, in_vmem),
        scratch_shapes=[pltpu.VMEM((own_logits.shape[0], 128), jnp.float32)],
        compiler_params=pltpu.CompilerParams(vmem_limit_bytes=VMEM_LIMIT),
        cost_estimate=pl.CostEstimate(
            flops=8 * own_logits.size,
            bytes_accessed=12 * own_logits.size,
            transcendentals=own_logits.size,
        ),
        name="local_stats",
    )(core, *arrays)


def delta_kernel(gathered_ref, logits_ref, kept_ref, delta_ref, lse_ref, kl_ref):
    shards = [gathered_ref[i] for i in range(gathered_ref.shape[0])]
    top = shards[0][0:1]
    for x in shards[1:]:
        top = jnp.maximum(top, x[0:1])
    total, mass, part = 0.0, 0.0, 0.0
    for x in shards:
        total = total + x[1:2] * jnp.exp(x[0:1] - top)
        mass, part = mass + x[2:3], part + x[3:4]
    lse = top + jnp.log(total)
    lse_ref[...] = lse
    kl_ref[...] = part / mass - jnp.log(mass) + lse
    row = lax.broadcasted_iota(jnp.int32, (128, lse.shape[1]), 0)
    turned = jnp.where(row == 0, lse, 1.0 / mass).T
    lse_column, scale_column = turned[:, 0:1], turned[:, 1:2]
    for r in range(0, logits_ref.shape[0], STEP):
        rows = slice(r, r + STEP)
        student = jnp.exp(logits_ref[rows, :] - lse_column[rows])
        kept = kept_ref[rows, :].astype(jnp.float32) * scale_column[rows]
        delta_ref[rows, :] = (loss_scale * (student - kept)).astype(jnp.bfloat16)


def finish(gathered, logits, kept):
    tokens = logits.shape[0]
    in_vmem = pl.BlockSpec(memory_space=pltpu.VMEM)
    delta, lse, kl = pl.pallas_call(
        delta_kernel,
        out_shape=(
            pltpu.VMEM(logits.shape, jnp.bfloat16),
            jax.ShapeDtypeStruct((1, tokens), jnp.float32),
            jax.ShapeDtypeStruct((1, tokens), jnp.float32),
        ),
        in_specs=[in_vmem] * 3,
        out_specs=(in_vmem, in_vmem, in_vmem),
        compiler_params=pltpu.CompilerParams(vmem_limit_bytes=VMEM_LIMIT),
        cost_estimate=pl.CostEstimate(
            flops=8 * logits.size, bytes_accessed=8 * logits.size, transcendentals=logits.size
        ),
        name="delta",
    )(*[pltpu.with_memory_space_constraint(x, pltpu.VMEM) for x in (gathered, logits, kept)])
    return delta, lse.reshape(tokens), kl.reshape(tokens)


def gradient_kernel(other, core_ref, head_ref, delta_ref, out_ref):
    side = 1 - core_ref[0] if other else core_ref[0]
    pairs, rows, _ = out_ref.shape
    for k in range(pairs):
        if rows % 16 == 0:
            start = pl.multiple_of((2 * k + side) * rows, 16)
            head_rows = head_ref[pl.ds(start, rows), :]
        else:
            head_rows = head_ref[2 * k * rows : 2 * (k + 1) * rows, :]
        block = lax.dot_general(
            head_rows, delta_ref[...], (((1,), (1,)), ((), ())), preferred_element_type=jnp.float32
        )
        if rows % 16:
            block = jnp.where(side == 0, block[:rows], block[rows:])
        out_ref[k] = block.astype(out_ref.dtype)


def own_gradient_kernel(head_ref, delta_ref, out_ref):
    pairs, _, rows, _ = out_ref.shape
    for k in range(pairs):
        block = lax.dot_general(
            head_ref[2 * k * rows : 2 * (k + 1) * rows, :],
            delta_ref[...],
            (((1,), (1,)), ((), ())),
            preferred_element_type=jnp.float32,
        )
        out_ref[k, 0] = block[:rows]
        out_ref[k, 1] = block[rows:]


def gradient(core, head, delta, run, other=False):
    rows = head.shape[0] // run
    shape = (run // 2, rows, delta.shape[0])
    in_vmem = pl.BlockSpec(memory_space=pltpu.VMEM)
    if core is None:
        out = pltpu.VMEM((run // 2, 2, *shape[1:]), jnp.float32)
        kernel = own_gradient_kernel
    else:
        out = pltpu.VMEM(shape, jnp.bfloat16 if other else jnp.float32)
        kernel = functools.partial(gradient_kernel, other)
    arrays = [pltpu.with_memory_space_constraint(x, pltpu.VMEM) for x in (head, delta)]
    return pl.pallas_call(
        kernel,
        out_shape=out,
        in_specs=([] if core is None else [pl.BlockSpec(memory_space=pltpu.SMEM)]) + [in_vmem] * 2,
        out_specs=in_vmem,
        compiler_params=pltpu.CompilerParams(vmem_limit_bytes=VMEM_LIMIT),
        cost_estimate=pl.CostEstimate(
            flops=2 * head.size * delta.shape[0],
            bytes_accessed=2 * (head.size + delta.size),
            transcendentals=0,
        ),
        name="partial_gradient",
    )(*([] if core is None else [core]), *arrays)


def head_gradient_kernel(steps, start, width, *refs):
    features_ref, delta_ref, out_ref, held_ref, sems = refs[0], refs[1], *refs[-3:]
    copies = []
    for k in range(steps):
        block = lax.dot_general(
            features_ref[:, start + k * width : start + (k + 1) * width],
            delta_ref[...],
            (((0,), (0,)), ((), ())),
            preferred_element_type=jnp.float32,
        )
        held_ref[k] = block.astype(jnp.bfloat16)
        copy = pltpu.make_async_copy(
            held_ref.at[k], out_ref.at[pl.ds(start + k * width, width)], sems.at[k]
        )
        copy.start()
        copies.append(copy)
    for copy in copies:
        copy.wait()


def head_gradient(features, delta, out, start, steps, width):
    columns = delta.shape[1]
    in_vmem = pl.BlockSpec(memory_space=pltpu.VMEM)
    in_hbm = pl.BlockSpec(memory_space=pltpu.HBM)
    return pl.pallas_call(
        functools.partial(head_gradient_kernel, steps, start, width),
        out_shape=jax.ShapeDtypeStruct((features.shape[1], columns), jnp.bfloat16),
        in_specs=[in_vmem, in_vmem] + ([] if out is None else [in_hbm]),
        out_specs=in_hbm,
        scratch_shapes=[
            pltpu.VMEM((steps, width, columns), jnp.bfloat16),
            pltpu.SemaphoreType.DMA((steps,)),
        ],
        input_output_aliases={} if out is None else {2: 0},
        compiler_params=pltpu.CompilerParams(vmem_limit_bytes=VMEM_LIMIT),
        cost_estimate=pl.CostEstimate(
            flops=2 * steps * width * delta.size,
            bytes_accessed=2 * (features.size + delta.size + steps * width * columns),
            transcendentals=0,
        ),
        name="head_gradient",
    )(features, delta, *([] if out is None else [out]))


def per_device(hidden, head, teacher, block_ids, counts):
    tok_size = lax.axis_size("tok")
    vocab_size = lax.axis_size("vocab")
    tok_index = lax.axis_index("tok")
    vocab_index = lax.axis_index("vocab")
    token_count = hidden.shape[0]
    rows, column_count = head.shape
    run = vocab_size // tok_size
    half = token_count // 2
    core = vocab_index & 1

    def columns_of(index, first, count):
        return lax.dynamic_slice(hidden, (first, index * rows), (count, rows))

    quarter = half // 2
    near, later = [
        [
            shift_tok(
                columns_of(lax.rem(tok_index + d, tok_size), core * half + first, quarter),
                d,
                tok_size,
            )
            for d in range(1, tok_size)
        ]
        for first in (0, quarter)
    ]
    upper = []
    while 1 << len(upper) < vocab_size:
        upper.append((vocab_index & (1 << len(upper))) != 0)
    high = lax.div(vocab_index, run)
    apart = lax.rem(tok_index + tok_size - high, tok_size)
    apart_is = [apart == d for d in range(tok_size)]
    first_column = vocab_index * column_count
    column_block = (first_column + jnp.arange(column_count, dtype=jnp.int32)) // BLK
    live_slot = jnp.arange(block_ids.shape[1], dtype=jnp.int32)[None, :] < counts[:, None]
    core_word = core.reshape(1)
    tok_is = [tok_index == d for d in range(tok_size)]
    head, upper, apart_is, tok_is, column_block, live_slot, core_word = lax.optimization_barrier(
        (head, upper, apart_is, tok_is, column_block, live_slot, core_word)
    )
    head_here = load(head)
    near, head_here, column_block, teacher, hidden = lax.optimization_barrier(
        (near, head_here, column_block, teacher, hidden)
    )
    products = [jnp.dot(x, head_here, preferred_element_type=jnp.float32) for x in near]
    returned = [[shift_tok(x, -d, tok_size)] for d, x in enumerate(products, 1)]
    later, _ = lax.optimization_barrier((later, products))
    near = [jnp.concatenate(pair, axis=0) for pair in zip(near, later)]
    far = [swap_vocab(x, 1, vocab_size) for x in near]
    for d in range(1, tok_size):
        for x in (later[d - 1], far[d - 1]):
            returned[d - 1].append(
                shift_tok(
                    jnp.dot(x, head_here, preferred_element_type=jnp.float32), -d, tok_size
                )
            )
    own = hidden[:, :rows]
    for d in range(1, tok_size):
        own = jnp.where(tok_is[d], hidden[:, d * rows : (d + 1) * rows], own)
    logits = jnp.dot(own, head_here, preferred_element_type=jnp.float32)
    block_hit = jnp.any(
        (block_ids[:, :, None] == column_block[None, None, :]) & live_slot[:, :, None], axis=1
    )
    features = [own] + [in_order(n, f, upper[0]) for n, f in zip(near, far)]
    all_features = jnp.concatenate(features, axis=0)
    blocks = block_hit.shape[0]
    listed = jnp.broadcast_to(
        block_hit[:, None, :], (blocks, token_count // blocks, column_count)
    ).reshape(token_count, column_count)
    teacher_f = teacher.astype(jnp.float32)
    kept = jnp.where(listed, teacher_f, 0.0)
    mass = jnp.sum(kept, axis=1)
    entropy = jnp.sum(jnp.where(listed, teacher_f * jnp.log(teacher_f), 0.0), axis=1)
    kept, early = kept.astype(jnp.bfloat16), jnp.stack([mass, entropy])
    returned, all_features, logits, kept, early = lax.optimization_barrier(
        (returned, all_features, logits, kept, early)
    )
    places = [i for i in range(1, len(upper)) if 1 << i < run]
    logits, stats = local_stats(core_word, logits, kept, early, returned)
    delta, lse, kl = finish(gather_vocab(stats, upper, places, vocab_size), logits, kept)

    deltas = [delta] + [shift_tok(delta, d, tok_size) for d in range(1, tok_size)]
    flags = [upper[i] for i in places]

    def direct(pieces):
        count = len(pieces)
        return [select([pieces[j ^ i] for j in range(count)], flags) for i in range(count)]

    own_pieces = direct(list(gradient(None, head_here, delta, run)))
    own_others = [
        swap_vocab(x.astype(jnp.bfloat16), 2 * i, vocab_size)
        for i, x in enumerate(own_pieces[1:], 1)
    ]
    state = []
    for x in deltas[1:]:
        send = gradient(core_word, head_here, x, run, other=True)
        own_others, _ = lax.optimization_barrier((own_others, send))
        x, _ = lax.optimization_barrier((x, send))
        keep = gradient(core_word, head_here, x, run)
        state.append((keep, swap_vocab(send, 1, vocab_size)))
    all_delta = jnp.concatenate(deltas, axis=0)

    width = 256 if rows % 256 == 0 else rows
    chunks = rows // width
    held = jnp.stack([keep + other.astype(jnp.float32) for keep, other in state], axis=1)
    taken = direct(list(held))
    sends = [x.astype(jnp.bfloat16) for x in taken[1:]]
    sends, all_delta = lax.optimization_barrier((sends, all_delta))
    others = [swap_vocab(x, 2 * (i + 1), vocab_size) for i, x in enumerate(sends)]
    done = (chunks + 1) // 2
    grad_head = head_gradient(all_features, all_delta, None, 0, done, width)
    others, grad_head = lax.optimization_barrier((others, grad_head))
    sums = taken[0]
    for other in others:
        sums = sums + other.astype(jnp.float32)
    own_sum = own_pieces[0]
    for other in own_others:
        own_sum = own_sum + other.astype(jnp.float32)
    send = jnp.where(upper[0], own_sum[0], own_sum[1]).astype(jnp.bfloat16)
    own_sum = jnp.where(upper[0], own_sum[1], own_sum[0])
    own_sum = own_sum + swap_vocab(send, 1, vocab_size).astype(jnp.float32)
    sends = [x.astype(jnp.bfloat16) for x in sums]
    sends, all_delta = lax.optimization_barrier((sends, all_delta))
    others = [shift_tok(x, -d, tok_size) for d, x in enumerate(sends, 1)]
    if done < chunks:
        grad_head = head_gradient(
            all_features, all_delta, grad_head, done * width, chunks - done, width
        )
        others, grad_head = lax.optimization_barrier((others, grad_head))
    sums = [own_sum] + [x.astype(jnp.float32) for x in others]
    blocks = []
    for k in range(tok_size):
        block = sums[k]
        for d in range(1, tok_size):
            block = jnp.where(apart_is[d], sums[(k - d) % tok_size], block)
        blocks.append(block)
    total = blocks[0]
    for k in range(1, tok_size):
        pairs = [(v, (v + k * run) % vocab_size) for v in range(vocab_size)]
        total = total + lax.ppermute(
            blocks[k].astype(jnp.bfloat16), "vocab", pairs
        ).astype(jnp.float32)
    grad_hidden = total.T
    return (lse, kl, grad_hidden, grad_head)


def solution(mesh):
    placed = (P("tok", None), P("tok", "vocab"), P("tok", "vocab"), P("tok", None), P("tok"))
    return jax.shard_map(
        per_device,
        mesh=mesh,
        in_specs=placed,
        out_specs=(P("tok"), P("tok"), P("tok", "vocab"), P("tok", "vocab")),
        check_vma=False,
    )
```

```python
import functools

import jax
import jax.numpy as jnp
from jax import lax
from jax.experimental import pallas as pl
from jax.experimental.pallas import tpu as pltpu
from jax.sharding import PartitionSpec as P

BLK = 512


loss_scale = 1024.0
VMEM_LIMIT = 16 << 20
STEP = 16


def shift_tok(x, offset, size):
    return lax.ppermute(x, "tok", [(i, (i + offset) % size) for i in range(size)])


def swap_vocab(x, bit, size):
    return lax.ppermute(x, "vocab", [(i, i ^ bit) for i in range(size)])


def in_order(mine, other, upper):
    return jnp.concatenate(
        [jnp.where(upper, other, mine), jnp.where(upper, mine, other)], axis=0
    )


def select(options, flags):
    for flag in flags:
        options = [jnp.where(flag, high, low) for low, high in zip(options[::2], options[1::2])]
    return options[0]


def gather_vocab(stats, upper, places, size):
    pair = in_order(stats[None], swap_vocab(stats[None], 1, size), upper[0])
    count = 1 << len(places)
    options = [pair] + [swap_vocab(pair, 2 * offset, size) for offset in range(1, count)]
    flags = [upper[i] for i in places]
    gathered = jnp.concatenate(
        [select([options[j ^ i] for i in range(count)], flags) for j in range(count)], axis=0
    )
    for i in range(len(places) + 1, len(upper)):
        gathered = in_order(gathered, swap_vocab(gathered, 1 << i, size), upper[i])
    return gathered


def load_kernel(head_ref, held_ref, sems):
    steps = sems.shape[0]
    depth = head_ref.shape[0] // steps
    parts = [pl.ds(k * depth, depth) for k in range(steps)]
    copies = [
        pltpu.make_async_copy(head_ref.at[part], held_ref.at[part], sems.at[k])
        for k, part in enumerate(parts)
    ]
    for copy in copies:
        copy.start()
    for copy in copies:
        copy.wait()


def load(head):
    steps = 4
    return pl.pallas_call(
        load_kernel,
        out_shape=pltpu.VMEM(head.shape, head.dtype),
        in_specs=[pl.BlockSpec(memory_space=pltpu.HBM)],
        out_specs=pl.BlockSpec(memory_space=pltpu.VMEM),
        scratch_shapes=[pltpu.SemaphoreType.DMA((steps,))],
        compiler_params=pltpu.CompilerParams(vmem_limit_bytes=VMEM_LIMIT),
        cost_estimate=pl.CostEstimate(
            flops=0, bytes_accessed=4 * head.size, transcendentals=0
        ),
        name="load_head",
    )(pltpu.with_memory_space_constraint(head, pltpu.HBM))


def stats_kernel(core_ref, own_ref, kept_ref, early_ref, *refs):
    parts, (logits_ref, stats_ref, turned_ref) = refs[:-3], refs[-3:]
    half = own_ref.shape[0] // 2
    lane = lax.broadcasted_iota(jnp.int32, (STEP, 128), 1)
    groups = [(core_ref[0], 0, half // 2), (core_ref[0], half // 2, half // 2)]
    groups.append((1 - core_ref[0], 0, half))
    for place, (side, first, count) in enumerate(groups):
        start = side * half + first
        for r in range(0, count, STEP):
            rows = pl.ds(pl.multiple_of(start + r, STEP), STEP)
            logits = own_ref[rows, :]
            for part in parts[place::3]:
                logits = logits + part[r : r + STEP, :]
            logits_ref[rows, :] = logits
            top = jnp.max(logits, axis=1, keepdims=True)
            total = jnp.sum(jnp.exp(logits - top), axis=1, keepdims=True)
            dot = jnp.sum(kept_ref[rows, :].astype(jnp.float32) * logits, axis=1, keepdims=True)
            turned_ref[rows, :] = jnp.where(lane == 0, top, jnp.where(lane == 1, total, dot))
    turned = turned_ref[...].T
    stats_ref[0:2, :] = turned[0:2]
    stats_ref[2:3, :] = early_ref[0:1, :]
    stats_ref[3:4, :] = early_ref[1:2, :] - turned[2:3]


def local_stats(core, own_logits, kept, early, returned):
    in_vmem = pl.BlockSpec(memory_space=pltpu.VMEM)
    parts = [x for pair in returned for x in pair]
    arrays = [
        pltpu.with_memory_space_constraint(x, pltpu.VMEM) for x in (own_logits, kept, early, *parts)
    ]
    return pl.pallas_call(
        stats_kernel,
        out_shape=(
            pltpu.VMEM(own_logits.shape, jnp.float32),
            pltpu.VMEM((4, own_logits.shape[0]), jnp.float32),
        ),
        in_specs=[pl.BlockSpec(memory_space=pltpu.SMEM)] + [in_vmem] * len(arrays),
        out_specs=(in_vmem, in_vmem),
        scratch_shapes=[pltpu.VMEM((own_logits.shape[0], 128), jnp.float32)],
        compiler_params=pltpu.CompilerParams(vmem_limit_bytes=VMEM_LIMIT),
        cost_estimate=pl.CostEstimate(
            flops=8 * own_logits.size,
            bytes_accessed=12 * own_logits.size,
            transcendentals=own_logits.size,
        ),
        name="local_stats",
    )(core, *arrays)


def delta_kernel(gathered_ref, logits_ref, kept_ref, delta_ref, lse_ref, kl_ref):
    shards = [gathered_ref[i] for i in range(gathered_ref.shape[0])]
    top = shards[0][0:1]
    for x in shards[1:]:
        top = jnp.maximum(top, x[0:1])
    total, mass, part = 0.0, 0.0, 0.0
    for x in shards:
        total = total + x[1:2] * jnp.exp(x[0:1] - top)
        mass, part = mass + x[2:3], part + x[3:4]
    lse = top + jnp.log(total)
    lse_ref[...] = lse
    kl_ref[...] = part / mass - jnp.log(mass) + lse
    row = lax.broadcasted_iota(jnp.int32, (128, lse.shape[1]), 0)
    turned = jnp.where(row == 0, lse, 1.0 / mass).T
    lse_column, scale_column = turned[:, 0:1], turned[:, 1:2]
    for r in range(0, logits_ref.shape[0], STEP):
        rows = slice(r, r + STEP)
        student = jnp.exp(logits_ref[rows, :] - lse_column[rows])
        kept = kept_ref[rows, :].astype(jnp.float32) * scale_column[rows]
        delta_ref[rows, :] = (loss_scale * (student - kept)).astype(jnp.bfloat16)


def finish(gathered, logits, kept):
    tokens = logits.shape[0]
    in_vmem = pl.BlockSpec(memory_space=pltpu.VMEM)
    delta, lse, kl = pl.pallas_call(
        delta_kernel,
        out_shape=(
            pltpu.VMEM(logits.shape, jnp.bfloat16),
            jax.ShapeDtypeStruct((1, tokens), jnp.float32),
            jax.ShapeDtypeStruct((1, tokens), jnp.float32),
        ),
        in_specs=[in_vmem] * 3,
        out_specs=(in_vmem, in_vmem, in_vmem),
        compiler_params=pltpu.CompilerParams(vmem_limit_bytes=VMEM_LIMIT),
        cost_estimate=pl.CostEstimate(
            flops=8 * logits.size, bytes_accessed=8 * logits.size, transcendentals=logits.size
        ),
        name="delta",
    )(*[pltpu.with_memory_space_constraint(x, pltpu.VMEM) for x in (gathered, logits, kept)])
    return delta, lse.reshape(tokens), kl.reshape(tokens)


def gradient_kernel(other, core_ref, head_ref, delta_ref, out_ref):
    side = 1 - core_ref[0] if other else core_ref[0]
    pairs, rows, _ = out_ref.shape
    for k in range(pairs):
        if rows % 16 == 0:
            start = pl.multiple_of((2 * k + side) * rows, 16)
            head_rows = head_ref[pl.ds(start, rows), :]
        else:
            head_rows = head_ref[2 * k * rows : 2 * (k + 1) * rows, :]
        block = lax.dot_general(
            head_rows, delta_ref[...], (((1,), (1,)), ((), ())), preferred_element_type=jnp.float32
        )
        if rows % 16:
            block = jnp.where(side == 0, block[:rows], block[rows:])
        out_ref[k] = block.astype(out_ref.dtype)


def own_gradient_kernel(head_ref, delta_ref, out_ref):
    pairs, _, rows, _ = out_ref.shape
    for k in range(pairs):
        block = lax.dot_general(
            head_ref[2 * k * rows : 2 * (k + 1) * rows, :],
            delta_ref[...],
            (((1,), (1,)), ((), ())),
            preferred_element_type=jnp.float32,
        )
        out_ref[k, 0] = block[:rows]
        out_ref[k, 1] = block[rows:]


def gradient(core, head, delta, run, other=False):
    rows = head.shape[0] // run
    shape = (run // 2, rows, delta.shape[0])
    in_vmem = pl.BlockSpec(memory_space=pltpu.VMEM)
    if core is None:
        out = pltpu.VMEM((run // 2, 2, *shape[1:]), jnp.float32)
        kernel = own_gradient_kernel
    else:
        out = pltpu.VMEM(shape, jnp.bfloat16 if other else jnp.float32)
        kernel = functools.partial(gradient_kernel, other)
    arrays = [pltpu.with_memory_space_constraint(x, pltpu.VMEM) for x in (head, delta)]
    return pl.pallas_call(
        kernel,
        out_shape=out,
        in_specs=([] if core is None else [pl.BlockSpec(memory_space=pltpu.SMEM)]) + [in_vmem] * 2,
        out_specs=in_vmem,
        compiler_params=pltpu.CompilerParams(vmem_limit_bytes=VMEM_LIMIT),
        cost_estimate=pl.CostEstimate(
            flops=2 * head.size * delta.shape[0],
            bytes_accessed=2 * (head.size + delta.size),
            transcendentals=0,
        ),
        name="partial_gradient",
    )(*([] if core is None else [core]), *arrays)


def head_gradient_kernel(steps, start, width, *refs):
    features_ref, delta_ref, out_ref, held_ref, sems = refs[0], refs[1], *refs[-3:]
    copies = []
    for k in range(steps):
        block = lax.dot_general(
            features_ref[:, start + k * width : start + (k + 1) * width],
            delta_ref[...],
            (((0,), (0,)), ((), ())),
            preferred_element_type=jnp.float32,
        )
        held_ref[k] = block.astype(jnp.bfloat16)
        copy = pltpu.make_async_copy(
            held_ref.at[k], out_ref.at[pl.ds(start + k * width, width)], sems.at[k]
        )
        copy.start()
        copies.append(copy)
    for copy in copies:
        copy.wait()


def head_gradient(features, delta, out, start, steps, width):
    columns = delta.shape[1]
    in_vmem = pl.BlockSpec(memory_space=pltpu.VMEM)
    in_hbm = pl.BlockSpec(memory_space=pltpu.HBM)
    return pl.pallas_call(
        functools.partial(head_gradient_kernel, steps, start, width),
        out_shape=jax.ShapeDtypeStruct((features.shape[1], columns), jnp.bfloat16),
        in_specs=[in_vmem, in_vmem] + ([] if out is None else [in_hbm]),
        out_specs=in_hbm,
        scratch_shapes=[
            pltpu.VMEM((steps, width, columns), jnp.bfloat16),
            pltpu.SemaphoreType.DMA((steps,)),
        ],
        input_output_aliases={} if out is None else {2: 0},
        compiler_params=pltpu.CompilerParams(vmem_limit_bytes=VMEM_LIMIT),
        cost_estimate=pl.CostEstimate(
            flops=2 * steps * width * delta.size,
            bytes_accessed=2 * (features.size + delta.size + steps * width * columns),
            transcendentals=0,
        ),
        name="head_gradient",
    )(features, delta, *([] if out is None else [out]))


def per_device(hidden, head, teacher, block_ids, counts):
    tok_size = lax.axis_size("tok")
    vocab_size = lax.axis_size("vocab")
    tok_index = lax.axis_index("tok")
    vocab_index = lax.axis_index("vocab")
    token_count = hidden.shape[0]
    rows, column_count = head.shape
    run = vocab_size // tok_size
    half = token_count // 2
    core = vocab_index & 1

    def columns_of(index, first, count):
        return lax.dynamic_slice(hidden, (first, index * rows), (count, rows))

    quarter = half // 2
    near, later = [
        [
            shift_tok(
                columns_of(lax.rem(tok_index + d, tok_size), core * half + first, quarter),
                d,
                tok_size,
            )
            for d in range(1, tok_size)
        ]
        for first in (0, quarter)
    ]
    upper = []
    while 1 << len(upper) < vocab_size:
        upper.append((vocab_index & (1 << len(upper))) != 0)
    high = lax.div(vocab_index, run)
    apart = lax.rem(tok_index + tok_size - high, tok_size)
    apart_is = [apart == d for d in range(tok_size)]
    first_column = vocab_index * column_count
    column_block = (first_column + jnp.arange(column_count, dtype=jnp.int32)) // BLK
    live_slot = jnp.arange(block_ids.shape[1], dtype=jnp.int32)[None, :] < counts[:, None]
    core_word = core.reshape(1)
    tok_is = [tok_index == d for d in range(tok_size)]
    head, upper, apart_is, tok_is, column_block, live_slot, core_word = lax.optimization_barrier(
        (head, upper, apart_is, tok_is, column_block, live_slot, core_word)
    )
    head_here = load(head)
    near, head_here, column_block, teacher, hidden = lax.optimization_barrier(
        (near, head_here, column_block, teacher, hidden)
    )
    products = [jnp.dot(x, head_here, preferred_element_type=jnp.float32) for x in near]
    returned = [[shift_tok(x, -d, tok_size)] for d, x in enumerate(products, 1)]
    later, _ = lax.optimization_barrier((later, products))
    near = [jnp.concatenate(pair, axis=0) for pair in zip(near, later)]
    far = [swap_vocab(x, 1, vocab_size) for x in near]
    for d in range(1, tok_size):
        for x in (later[d - 1], far[d - 1]):
            returned[d - 1].append(
                shift_tok(
                    jnp.dot(x, head_here, preferred_element_type=jnp.float32), -d, tok_size
                )
            )
    own = hidden[:, :rows]
    for d in range(1, tok_size):
        own = jnp.where(tok_is[d], hidden[:, d * rows : (d + 1) * rows], own)
    logits = jnp.dot(own, head_here, preferred_element_type=jnp.float32)
    block_hit = jnp.any(
        (block_ids[:, :, None] == column_block[None, None, :]) & live_slot[:, :, None], axis=1
    )
    features = [own] + [in_order(n, f, upper[0]) for n, f in zip(near, far)]
    all_features = jnp.concatenate(features, axis=0)
    blocks = block_hit.shape[0]
    listed = jnp.broadcast_to(
        block_hit[:, None, :], (blocks, token_count // blocks, column_count)
    ).reshape(token_count, column_count)
    teacher_f = teacher.astype(jnp.float32)
    kept = jnp.where(listed, teacher_f, 0.0)
    mass = jnp.sum(kept, axis=1)
    entropy = jnp.sum(jnp.where(listed, teacher_f * jnp.log(teacher_f), 0.0), axis=1)
    kept, early = kept.astype(jnp.bfloat16), jnp.stack([mass, entropy])
    returned, all_features, logits, kept, early = lax.optimization_barrier(
        (returned, all_features, logits, kept, early)
    )
    places = [i for i in range(1, len(upper)) if 1 << i < run]
    logits, stats = local_stats(core_word, logits, kept, early, returned)
    delta, lse, kl = finish(gather_vocab(stats, upper, places, vocab_size), logits, kept)

    deltas = [delta] + [shift_tok(delta, d, tok_size) for d in range(1, tok_size)]
    flags = [upper[i] for i in places]

    def direct(pieces):
        count = len(pieces)
        return [select([pieces[j ^ i] for j in range(count)], flags) for i in range(count)]

    own_pieces = direct(list(gradient(None, head_here, delta, run)))
    own_others = [
        swap_vocab(x.astype(jnp.bfloat16), 2 * i, vocab_size)
        for i, x in enumerate(own_pieces[1:], 1)
    ]
    state = []
    for x in deltas[1:]:
        send = gradient(core_word, head_here, x, run, other=True)
        own_others, _ = lax.optimization_barrier((own_others, send))
        x, _ = lax.optimization_barrier((x, send))
        keep = gradient(core_word, head_here, x, run)
        state.append((keep, swap_vocab(send, 1, vocab_size)))
    all_delta = jnp.concatenate(deltas, axis=0)

    width = 256 if rows % 256 == 0 else rows
    chunks = rows // width
    taken = [
        direct(list(keep + other.astype(jnp.float32))) for keep, other in state
    ]
    taken = [[x.astype(jnp.bfloat16) for x in pieces] for pieces in taken]
    taken, all_delta = lax.optimization_barrier((taken, all_delta))
    arrived = []
    for d, pieces in enumerate(taken, 1):
        block = []
        for offset, piece in enumerate(pieces):
            pairs = [
                (v * tok_size + t, (v ^ (2 * offset)) * tok_size + (t - d) % tok_size)
                for v in range(vocab_size)
                for t in range(tok_size)
            ]
            block.append(lax.ppermute(piece, ("vocab", "tok"), pairs))
        arrived.append(block)
    done = (chunks + 1) // 2
    grad_head = head_gradient(all_features, all_delta, None, 0, done, width)
    arrived, grad_head = lax.optimization_barrier((arrived, grad_head))
    own_sum = own_pieces[0]
    for other in own_others:
        own_sum = own_sum + other.astype(jnp.float32)
    send = jnp.where(upper[0], own_sum[0], own_sum[1]).astype(jnp.bfloat16)
    own_sum = jnp.where(upper[0], own_sum[1], own_sum[0])
    own_sum = own_sum + swap_vocab(send, 1, vocab_size).astype(jnp.float32)
    sums = [own_sum]
    for block in arrived:
        total = block[0].astype(jnp.float32)
        for x in block[1:]:
            total = total + x.astype(jnp.float32)
        sums.append(total)
    blocks = []
    for k in range(tok_size):
        block = sums[k]
        for d in range(1, tok_size):
            block = jnp.where(apart_is[d], sums[(k - d) % tok_size], block)
        blocks.append(block)
    total = blocks[0]
    if done < chunks:
        blocks[1:], all_delta = lax.optimization_barrier((blocks[1:], all_delta))
        grad_head = head_gradient(
            all_features, all_delta, grad_head, done * width, chunks - done, width
        )
    for k in range(1, tok_size):
        pairs = [(v, (v + k * run) % vocab_size) for v in range(vocab_size)]
        total = total + lax.ppermute(
            blocks[k].astype(jnp.bfloat16), "vocab", pairs
        ).astype(jnp.float32)
    grad_hidden = total.T
    return (lse, kl, grad_hidden, grad_head)


def solution(mesh):
    placed = (P("tok", None), P("tok", "vocab"), P("tok", "vocab"), P("tok", None), P("tok"))
    return jax.shard_map(
        per_device,
        mesh=mesh,
        in_specs=placed,
        out_specs=(P("tok"), P("tok"), P("tok", "vocab"), P("tok", "vocab")),
        check_vma=False,
    )
```

```python
import functools

import jax
import jax.numpy as jnp
from jax import lax
from jax.experimental import pallas as pl
from jax.experimental.pallas import tpu as pltpu
from jax.sharding import PartitionSpec as P

BLK = 512


loss_scale = 1024.0
VMEM_LIMIT = 16 << 20
STEP = 16


def shift_tok(x, offset, size):
    return lax.ppermute(x, "tok", [(i, (i + offset) % size) for i in range(size)])


def swap_vocab(x, bit, size):
    return lax.ppermute(x, "vocab", [(i, i ^ bit) for i in range(size)])


def in_order(mine, other, upper):
    return jnp.concatenate(
        [jnp.where(upper, other, mine), jnp.where(upper, mine, other)], axis=0
    )


def select(options, flags):
    for flag in flags:
        options = [jnp.where(flag, high, low) for low, high in zip(options[::2], options[1::2])]
    return options[0]


def gather_vocab(stats, upper, places, size):
    pair = in_order(stats[None], swap_vocab(stats[None], 1, size), upper[0])
    count = 1 << len(places)
    options = [pair] + [swap_vocab(pair, 2 * offset, size) for offset in range(1, count)]
    flags = [upper[i] for i in places]
    gathered = jnp.concatenate(
        [select([options[j ^ i] for i in range(count)], flags) for j in range(count)], axis=0
    )
    for i in range(len(places) + 1, len(upper)):
        gathered = in_order(gathered, swap_vocab(gathered, 1 << i, size), upper[i])
    return gathered


def load_kernel(head_ref, held_ref, sems):
    steps = sems.shape[0]
    depth = head_ref.shape[0] // steps
    parts = [pl.ds(k * depth, depth) for k in range(steps)]
    copies = [
        pltpu.make_async_copy(head_ref.at[part], held_ref.at[part], sems.at[k])
        for k, part in enumerate(parts)
    ]
    for copy in copies:
        copy.start()
    for copy in copies:
        copy.wait()


def load(head):
    steps = 4
    return pl.pallas_call(
        load_kernel,
        out_shape=pltpu.VMEM(head.shape, head.dtype),
        in_specs=[pl.BlockSpec(memory_space=pltpu.HBM)],
        out_specs=pl.BlockSpec(memory_space=pltpu.VMEM),
        scratch_shapes=[pltpu.SemaphoreType.DMA((steps,))],
        compiler_params=pltpu.CompilerParams(vmem_limit_bytes=VMEM_LIMIT),
        cost_estimate=pl.CostEstimate(
            flops=0, bytes_accessed=4 * head.size, transcendentals=0
        ),
        name="load_head",
    )(pltpu.with_memory_space_constraint(head, pltpu.HBM))


def stats_kernel(core_ref, own_ref, kept_ref, early_ref, *refs):
    parts, (powers_ref, stats_ref, turned_ref) = refs[:-3], refs[-3:]
    half = own_ref.shape[0] // 2
    lane = lax.broadcasted_iota(jnp.int32, (STEP, 128), 1)
    groups = [(core_ref[0], 0, half // 2), (core_ref[0], half // 2, half // 2)]
    groups.append((1 - core_ref[0], 0, half))
    for place, (side, first, count) in enumerate(groups):
        start = side * half + first
        for r in range(0, count, STEP):
            rows = pl.ds(pl.multiple_of(start + r, STEP), STEP)
            logits = own_ref[rows, :]
            for part in parts[place::3]:
                logits = logits + part[r : r + STEP, :]
            top = jnp.max(logits, axis=1, keepdims=True)
            powers = jnp.exp(logits - top)
            powers_ref[rows, :] = powers
            total = jnp.sum(powers, axis=1, keepdims=True)
            dot = jnp.sum(kept_ref[rows, :].astype(jnp.float32) * logits, axis=1, keepdims=True)
            turned_ref[rows, :] = jnp.where(lane == 0, top, jnp.where(lane == 1, total, dot))
    turned = turned_ref[...].T
    stats_ref[0:2, :] = turned[0:2]
    stats_ref[2:3, :] = early_ref[0:1, :]
    stats_ref[3:4, :] = early_ref[1:2, :] - turned[2:3]


def local_stats(core, own_logits, kept, early, returned):
    in_vmem = pl.BlockSpec(memory_space=pltpu.VMEM)
    parts = [x for pair in returned for x in pair]
    arrays = [
        pltpu.with_memory_space_constraint(x, pltpu.VMEM) for x in (own_logits, kept, early, *parts)
    ]
    return pl.pallas_call(
        stats_kernel,
        out_shape=(
            pltpu.VMEM(own_logits.shape, jnp.float32),
            pltpu.VMEM((4, own_logits.shape[0]), jnp.float32),
        ),
        in_specs=[pl.BlockSpec(memory_space=pltpu.SMEM)] + [in_vmem] * len(arrays),
        out_specs=(in_vmem, in_vmem),
        scratch_shapes=[pltpu.VMEM((own_logits.shape[0], 128), jnp.float32)],
        compiler_params=pltpu.CompilerParams(vmem_limit_bytes=VMEM_LIMIT),
        cost_estimate=pl.CostEstimate(
            flops=8 * own_logits.size,
            bytes_accessed=12 * own_logits.size,
            transcendentals=own_logits.size,
        ),
        name="local_stats",
    )(core, *arrays)


def delta_kernel(gathered_ref, stats_ref, powers_ref, kept_ref, delta_ref, lse_ref, kl_ref):
    shards = [gathered_ref[i] for i in range(gathered_ref.shape[0])]
    top = shards[0][0:1]
    for x in shards[1:]:
        top = jnp.maximum(top, x[0:1])
    total, mass, part = 0.0, 0.0, 0.0
    for x in shards:
        total = total + x[1:2] * jnp.exp(x[0:1] - top)
        mass, part = mass + x[2:3], part + x[3:4]
    lse = top + jnp.log(total)
    lse_ref[...] = lse
    kl_ref[...] = part / mass - jnp.log(mass) + lse
    row = lax.broadcasted_iota(jnp.int32, (128, lse.shape[1]), 0)
    student_scale = loss_scale * jnp.exp(stats_ref[0:1, :] - lse)
    turned = jnp.where(row == 0, student_scale, loss_scale / mass).T
    student_column, kept_column = turned[:, 0:1], turned[:, 1:2]
    for r in range(0, powers_ref.shape[0], STEP):
        rows = slice(r, r + STEP)
        student = powers_ref[rows, :] * student_column[rows]
        kept = kept_ref[rows, :].astype(jnp.float32) * kept_column[rows]
        delta_ref[rows, :] = (student - kept).astype(jnp.bfloat16)


def finish(gathered, stats, powers, kept):
    tokens = powers.shape[0]
    in_vmem = pl.BlockSpec(memory_space=pltpu.VMEM)
    delta, lse, kl = pl.pallas_call(
        delta_kernel,
        out_shape=(
            pltpu.VMEM(powers.shape, jnp.bfloat16),
            jax.ShapeDtypeStruct((1, tokens), jnp.float32),
            jax.ShapeDtypeStruct((1, tokens), jnp.float32),
        ),
        in_specs=[in_vmem] * 4,
        out_specs=(in_vmem, in_vmem, in_vmem),
        compiler_params=pltpu.CompilerParams(vmem_limit_bytes=VMEM_LIMIT),
        cost_estimate=pl.CostEstimate(
            flops=8 * powers.size, bytes_accessed=8 * powers.size, transcendentals=0
        ),
        name="delta",
    )(*[pltpu.with_memory_space_constraint(x, pltpu.VMEM) for x in (gathered, stats, powers, kept)])
    return delta, lse.reshape(tokens), kl.reshape(tokens)


def gradient_kernel(other, core_ref, head_ref, delta_ref, out_ref):
    side = 1 - core_ref[0] if other else core_ref[0]
    pairs, rows, _ = out_ref.shape
    for k in range(pairs):
        if rows % 16 == 0:
            start = pl.multiple_of((2 * k + side) * rows, 16)
            head_rows = head_ref[pl.ds(start, rows), :]
        else:
            head_rows = head_ref[2 * k * rows : 2 * (k + 1) * rows, :]
        block = lax.dot_general(
            head_rows, delta_ref[...], (((1,), (1,)), ((), ())), preferred_element_type=jnp.float32
        )
        if rows % 16:
            block = jnp.where(side == 0, block[:rows], block[rows:])
        out_ref[k] = block.astype(out_ref.dtype)


def own_gradient_kernel(head_ref, delta_ref, out_ref):
    pairs, _, rows, _ = out_ref.shape
    for k in range(pairs):
        block = lax.dot_general(
            head_ref[2 * k * rows : 2 * (k + 1) * rows, :],
            delta_ref[...],
            (((1,), (1,)), ((), ())),
            preferred_element_type=jnp.float32,
        )
        out_ref[k, 0] = block[:rows]
        out_ref[k, 1] = block[rows:]


def gradient(core, head, delta, run, other=False):
    rows = head.shape[0] // run
    shape = (run // 2, rows, delta.shape[0])
    in_vmem = pl.BlockSpec(memory_space=pltpu.VMEM)
    if core is None:
        out = pltpu.VMEM((run // 2, 2, *shape[1:]), jnp.float32)
        kernel = own_gradient_kernel
    else:
        out = pltpu.VMEM(shape, jnp.bfloat16 if other else jnp.float32)
        kernel = functools.partial(gradient_kernel, other)
    arrays = [pltpu.with_memory_space_constraint(x, pltpu.VMEM) for x in (head, delta)]
    return pl.pallas_call(
        kernel,
        out_shape=out,
        in_specs=([] if core is None else [pl.BlockSpec(memory_space=pltpu.SMEM)]) + [in_vmem] * 2,
        out_specs=in_vmem,
        compiler_params=pltpu.CompilerParams(vmem_limit_bytes=VMEM_LIMIT),
        cost_estimate=pl.CostEstimate(
            flops=2 * head.size * delta.shape[0],
            bytes_accessed=2 * (head.size + delta.size),
            transcendentals=0,
        ),
        name="partial_gradient",
    )(*([] if core is None else [core]), *arrays)


def head_gradient_kernel(steps, start, width, *refs):
    features_ref, delta_ref, out_ref, held_ref, sems = refs[0], refs[1], *refs[-3:]
    copies = []
    for k in range(steps):
        block = lax.dot_general(
            features_ref[:, start + k * width : start + (k + 1) * width],
            delta_ref[...],
            (((0,), (0,)), ((), ())),
            preferred_element_type=jnp.float32,
        )
        held_ref[k] = block.astype(jnp.bfloat16)
        copy = pltpu.make_async_copy(
            held_ref.at[k], out_ref.at[pl.ds(start + k * width, width)], sems.at[k]
        )
        copy.start()
        copies.append(copy)
    for copy in copies:
        copy.wait()


def head_gradient(features, delta, out, start, steps, width):
    columns = delta.shape[1]
    in_vmem = pl.BlockSpec(memory_space=pltpu.VMEM)
    in_hbm = pl.BlockSpec(memory_space=pltpu.HBM)
    return pl.pallas_call(
        functools.partial(head_gradient_kernel, steps, start, width),
        out_shape=jax.ShapeDtypeStruct((features.shape[1], columns), jnp.bfloat16),
        in_specs=[in_vmem, in_vmem] + ([] if out is None else [in_hbm]),
        out_specs=in_hbm,
        scratch_shapes=[
            pltpu.VMEM((steps, width, columns), jnp.bfloat16),
            pltpu.SemaphoreType.DMA((steps,)),
        ],
        input_output_aliases={} if out is None else {2: 0},
        compiler_params=pltpu.CompilerParams(vmem_limit_bytes=VMEM_LIMIT),
        cost_estimate=pl.CostEstimate(
            flops=2 * steps * width * delta.size,
            bytes_accessed=2 * (features.size + delta.size + steps * width * columns),
            transcendentals=0,
        ),
        name="head_gradient",
    )(features, delta, *([] if out is None else [out]))


def per_device(hidden, head, teacher, block_ids, counts):
    tok_size = lax.axis_size("tok")
    vocab_size = lax.axis_size("vocab")
    tok_index = lax.axis_index("tok")
    vocab_index = lax.axis_index("vocab")
    token_count = hidden.shape[0]
    rows, column_count = head.shape
    run = vocab_size // tok_size
    half = token_count // 2
    core = vocab_index & 1

    def columns_of(index, first, count):
        return lax.dynamic_slice(hidden, (first, index * rows), (count, rows))

    quarter = half // 2
    near, later = [
        [
            shift_tok(
                columns_of(lax.rem(tok_index + d, tok_size), core * half + first, quarter),
                d,
                tok_size,
            )
            for d in range(1, tok_size)
        ]
        for first in (0, quarter)
    ]
    upper = []
    while 1 << len(upper) < vocab_size:
        upper.append((vocab_index & (1 << len(upper))) != 0)
    high = lax.div(vocab_index, run)
    apart = lax.rem(tok_index + tok_size - high, tok_size)
    apart_is = [apart == d for d in range(tok_size)]
    first_column = vocab_index * column_count
    column_block = (first_column + jnp.arange(column_count, dtype=jnp.int32)) // BLK
    live_slot = jnp.arange(block_ids.shape[1], dtype=jnp.int32)[None, :] < counts[:, None]
    core_word = core.reshape(1)
    tok_is = [tok_index == d for d in range(tok_size)]
    head, upper, apart_is, tok_is, column_block, live_slot, core_word = lax.optimization_barrier(
        (head, upper, apart_is, tok_is, column_block, live_slot, core_word)
    )
    head_here = load(head)
    near, head_here, column_block, teacher, hidden = lax.optimization_barrier(
        (near, head_here, column_block, teacher, hidden)
    )
    products = [jnp.dot(x, head_here, preferred_element_type=jnp.float32) for x in near]
    returned = [[shift_tok(x, -d, tok_size)] for d, x in enumerate(products, 1)]
    later, _ = lax.optimization_barrier((later, products))
    near = [jnp.concatenate(pair, axis=0) for pair in zip(near, later)]
    far = [swap_vocab(x, 1, vocab_size) for x in near]
    for d in range(1, tok_size):
        for x in (later[d - 1], far[d - 1]):
            returned[d - 1].append(
                shift_tok(
                    jnp.dot(x, head_here, preferred_element_type=jnp.float32), -d, tok_size
                )
            )
    own = hidden[:, :rows]
    for d in range(1, tok_size):
        own = jnp.where(tok_is[d], hidden[:, d * rows : (d + 1) * rows], own)
    logits = jnp.dot(own, head_here, preferred_element_type=jnp.float32)
    block_hit = jnp.any(
        (block_ids[:, :, None] == column_block[None, None, :]) & live_slot[:, :, None], axis=1
    )
    features = [own] + [in_order(n, f, upper[0]) for n, f in zip(near, far)]
    all_features = jnp.concatenate(features, axis=0)
    blocks = block_hit.shape[0]
    listed = jnp.broadcast_to(
        block_hit[:, None, :], (blocks, token_count // blocks, column_count)
    ).reshape(token_count, column_count)
    teacher_f = teacher.astype(jnp.float32)
    kept = jnp.where(listed, teacher_f, 0.0)
    mass = jnp.sum(kept, axis=1)
    entropy = jnp.sum(jnp.where(listed, teacher_f * jnp.log(teacher_f), 0.0), axis=1)
    kept, early = kept.astype(jnp.bfloat16), jnp.stack([mass, entropy])
    returned, all_features, logits, kept, early = lax.optimization_barrier(
        (returned, all_features, logits, kept, early)
    )
    places = [i for i in range(1, len(upper)) if 1 << i < run]
    powers, stats = local_stats(core_word, logits, kept, early, returned)
    gathered = gather_vocab(stats, upper, places, vocab_size)
    delta, lse, kl = finish(gathered, stats, powers, kept)

    deltas = [delta] + [shift_tok(delta, d, tok_size) for d in range(1, tok_size)]
    flags = [upper[i] for i in places]

    def direct(pieces):
        count = len(pieces)
        return [select([pieces[j ^ i] for j in range(count)], flags) for i in range(count)]

    own_pieces = direct(list(gradient(None, head_here, delta, run)))
    own_others = [
        swap_vocab(x.astype(jnp.bfloat16), 2 * i, vocab_size)
        for i, x in enumerate(own_pieces[1:], 1)
    ]
    state = []
    for x in deltas[1:]:
        send = gradient(core_word, head_here, x, run, other=True)
        own_others, _ = lax.optimization_barrier((own_others, send))
        x, _ = lax.optimization_barrier((x, send))
        keep = gradient(core_word, head_here, x, run)
        state.append((keep, swap_vocab(send, 1, vocab_size)))
    all_delta = jnp.concatenate(deltas, axis=0)

    width = 256 if rows % 256 == 0 else rows
    chunks = rows // width
    taken = [
        direct(list(keep + other.astype(jnp.float32))) for keep, other in state
    ]
    taken = [[x.astype(jnp.bfloat16) for x in pieces] for pieces in taken]
    taken, all_delta = lax.optimization_barrier((taken, all_delta))
    arrived = []
    for d, pieces in enumerate(taken, 1):
        block = []
        for offset, piece in enumerate(pieces):
            pairs = [
                (v * tok_size + t, (v ^ (2 * offset)) * tok_size + (t - d) % tok_size)
                for v in range(vocab_size)
                for t in range(tok_size)
            ]
            block.append(lax.ppermute(piece, ("vocab", "tok"), pairs))
        arrived.append(block)
    done = (chunks + 1) // 2
    grad_head = head_gradient(all_features, all_delta, None, 0, done, width)
    arrived, grad_head = lax.optimization_barrier((arrived, grad_head))
    own_sum = own_pieces[0]
    for other in own_others:
        own_sum = own_sum + other.astype(jnp.float32)
    send = jnp.where(upper[0], own_sum[0], own_sum[1]).astype(jnp.bfloat16)
    own_sum = jnp.where(upper[0], own_sum[1], own_sum[0])
    own_sum = own_sum + swap_vocab(send, 1, vocab_size).astype(jnp.float32)
    sums = [own_sum]
    for block in arrived:
        total = block[0].astype(jnp.float32)
        for x in block[1:]:
            total = total + x.astype(jnp.float32)
        sums.append(total)
    blocks = []
    for k in range(tok_size):
        block = sums[k]
        for d in range(1, tok_size):
            block = jnp.where(apart_is[d], sums[(k - d) % tok_size], block)
        blocks.append(block)
    total = blocks[0]
    if done < chunks:
        blocks[1:], all_delta = lax.optimization_barrier((blocks[1:], all_delta))
        grad_head = head_gradient(
            all_features, all_delta, grad_head, done * width, chunks - done, width
        )
    for k in range(1, tok_size):
        pairs = [(v, (v + k * run) % vocab_size) for v in range(vocab_size)]
        total = total + lax.ppermute(
            blocks[k].astype(jnp.bfloat16), "vocab", pairs
        ).astype(jnp.float32)
    grad_hidden = total.T
    return (lse, kl, grad_hidden, grad_head)


def solution(mesh):
    placed = (P("tok", None), P("tok", "vocab"), P("tok", "vocab"), P("tok", None), P("tok"))
    return jax.shard_map(
        per_device,
        mesh=mesh,
        in_specs=placed,
        out_specs=(P("tok"), P("tok"), P("tok", "vocab"), P("tok", "vocab")),
        check_vma=False,
    )
```

```python
import functools

import jax
import jax.numpy as jnp
from jax import lax
from jax.experimental import pallas as pl
from jax.experimental.pallas import tpu as pltpu
from jax.sharding import PartitionSpec as P

BLK = 512


loss_scale = 1024.0
VMEM_LIMIT = 16 << 20
STEP = 16


def shift_tok(x, offset, size):
    return lax.ppermute(x, "tok", [(i, (i + offset) % size) for i in range(size)])


def swap_vocab(x, bit, size):
    return lax.ppermute(x, "vocab", [(i, i ^ bit) for i in range(size)])


def in_order(mine, other, upper):
    return jnp.concatenate(
        [jnp.where(upper, other, mine), jnp.where(upper, mine, other)], axis=0
    )


def select(options, flags):
    for flag in flags:
        options = [jnp.where(flag, high, low) for low, high in zip(options[::2], options[1::2])]
    return options[0]


def gather_vocab(stats, upper, places, size):
    pair = in_order(stats[None], swap_vocab(stats[None], 1, size), upper[0])
    count = 1 << len(places)
    options = [pair] + [swap_vocab(pair, 2 * offset, size) for offset in range(1, count)]
    flags = [upper[i] for i in places]
    gathered = jnp.concatenate(
        [select([options[j ^ i] for i in range(count)], flags) for j in range(count)], axis=0
    )
    for i in range(len(places) + 1, len(upper)):
        gathered = in_order(gathered, swap_vocab(gathered, 1 << i, size), upper[i])
    return gathered


def load_kernel(head_ref, held_ref, sems):
    steps = sems.shape[0]
    depth = head_ref.shape[0] // steps
    parts = [pl.ds(k * depth, depth) for k in range(steps)]
    copies = [
        pltpu.make_async_copy(head_ref.at[part], held_ref.at[part], sems.at[k])
        for k, part in enumerate(parts)
    ]
    for copy in copies:
        copy.start()
    for copy in copies:
        copy.wait()


def load(head):
    steps = 4
    return pl.pallas_call(
        load_kernel,
        out_shape=pltpu.VMEM(head.shape, head.dtype),
        in_specs=[pl.BlockSpec(memory_space=pltpu.HBM)],
        out_specs=pl.BlockSpec(memory_space=pltpu.VMEM),
        scratch_shapes=[pltpu.SemaphoreType.DMA((steps,))],
        compiler_params=pltpu.CompilerParams(vmem_limit_bytes=VMEM_LIMIT),
        cost_estimate=pl.CostEstimate(
            flops=0, bytes_accessed=4 * head.size, transcendentals=0
        ),
        name="load_head",
    )(pltpu.with_memory_space_constraint(head, pltpu.HBM))


def stats_kernel(core_ref, own_ref, kept_ref, early_ref, *refs):
    parts, (powers_ref, stats_ref, turned_ref) = refs[:-3], refs[-3:]
    half = own_ref.shape[0] // 2
    lane = lax.broadcasted_iota(jnp.int32, (STEP, 128), 1)
    groups = [(core_ref[0], 0, half // 2), (core_ref[0], half // 2, half // 2)]
    groups.append((1 - core_ref[0], 0, half))
    for place, (side, first, count) in enumerate(groups):
        start = side * half + first
        for r in range(0, count, STEP):
            rows = pl.ds(pl.multiple_of(start + r, STEP), STEP)
            logits = own_ref[rows, :]
            for part in parts[place::3]:
                logits = logits + part[r : r + STEP, :]
            top = jnp.max(logits, axis=1, keepdims=True)
            powers = jnp.exp(logits - top)
            powers_ref[rows, :] = powers
            total = jnp.sum(powers, axis=1, keepdims=True)
            dot = jnp.sum(kept_ref[rows, :].astype(jnp.float32) * logits, axis=1, keepdims=True)
            turned_ref[rows, :] = jnp.where(lane == 0, top, jnp.where(lane == 1, total, dot))
    turned = turned_ref[...].T
    stats_ref[0:2, :] = turned[0:2]
    stats_ref[2:3, :] = early_ref[0:1, :]
    stats_ref[3:4, :] = early_ref[1:2, :] - turned[2:3]


def local_stats(core, own_logits, kept, early, returned):
    in_vmem = pl.BlockSpec(memory_space=pltpu.VMEM)
    parts = [x for pair in returned for x in pair]
    arrays = [
        pltpu.with_memory_space_constraint(x, pltpu.VMEM) for x in (own_logits, kept, early, *parts)
    ]
    return pl.pallas_call(
        stats_kernel,
        out_shape=(
            pltpu.VMEM(own_logits.shape, jnp.float32),
            pltpu.VMEM((4, own_logits.shape[0]), jnp.float32),
        ),
        in_specs=[pl.BlockSpec(memory_space=pltpu.SMEM)] + [in_vmem] * len(arrays),
        out_specs=(in_vmem, in_vmem),
        scratch_shapes=[pltpu.VMEM((own_logits.shape[0], 128), jnp.float32)],
        compiler_params=pltpu.CompilerParams(vmem_limit_bytes=VMEM_LIMIT),
        cost_estimate=pl.CostEstimate(
            flops=8 * own_logits.size,
            bytes_accessed=12 * own_logits.size,
            transcendentals=own_logits.size,
        ),
        name="local_stats",
    )(core, *arrays)


def delta_kernel(gathered_ref, stats_ref, powers_ref, kept_ref, delta_ref, lse_ref, kl_ref):
    shards = [gathered_ref[i] for i in range(gathered_ref.shape[0])]
    top = shards[0][0:1]
    for x in shards[1:]:
        top = jnp.maximum(top, x[0:1])
    total, mass, part = 0.0, 0.0, 0.0
    for x in shards:
        total = total + x[1:2] * jnp.exp(x[0:1] - top)
        mass, part = mass + x[2:3], part + x[3:4]
    lse = top + jnp.log(total)
    lse_ref[...] = lse
    kl_ref[...] = part / mass - jnp.log(mass) + lse
    row = lax.broadcasted_iota(jnp.int32, (128, lse.shape[1]), 0)
    student_scale = loss_scale * jnp.exp(stats_ref[0:1, :] - lse)
    turned = jnp.where(row == 0, student_scale, loss_scale / mass).T
    student_column, kept_column = turned[:, 0:1], turned[:, 1:2]
    for r in range(0, powers_ref.shape[0], STEP):
        rows = slice(r, r + STEP)
        student = powers_ref[rows, :] * student_column[rows]
        kept = kept_ref[rows, :].astype(jnp.float32) * kept_column[rows]
        delta_ref[rows, :] = (student - kept).astype(jnp.bfloat16)


def finish(gathered, stats, powers, kept):
    tokens = powers.shape[0]
    in_vmem = pl.BlockSpec(memory_space=pltpu.VMEM)
    delta, lse, kl = pl.pallas_call(
        delta_kernel,
        out_shape=(
            pltpu.VMEM(powers.shape, jnp.bfloat16),
            jax.ShapeDtypeStruct((1, tokens), jnp.float32),
            jax.ShapeDtypeStruct((1, tokens), jnp.float32),
        ),
        in_specs=[in_vmem] * 4,
        out_specs=(in_vmem, in_vmem, in_vmem),
        compiler_params=pltpu.CompilerParams(vmem_limit_bytes=VMEM_LIMIT),
        cost_estimate=pl.CostEstimate(
            flops=8 * powers.size, bytes_accessed=8 * powers.size, transcendentals=0
        ),
        name="delta",
    )(*[pltpu.with_memory_space_constraint(x, pltpu.VMEM) for x in (gathered, stats, powers, kept)])
    return delta, lse.reshape(tokens), kl.reshape(tokens)


def gradient_kernel(other, core_ref, head_ref, delta_ref, out_ref):
    side = 1 - core_ref[0] if other else core_ref[0]
    pairs, rows, _ = out_ref.shape
    for k in range(pairs):
        if rows % 16 == 0:
            start = pl.multiple_of((2 * k + side) * rows, 16)
            head_rows = head_ref[pl.ds(start, rows), :]
        else:
            head_rows = head_ref[2 * k * rows : 2 * (k + 1) * rows, :]
        block = lax.dot_general(
            head_rows, delta_ref[...], (((1,), (1,)), ((), ())), preferred_element_type=jnp.float32
        )
        if rows % 16:
            block = jnp.where(side == 0, block[:rows], block[rows:])
        out_ref[k] = block.astype(out_ref.dtype)


def own_gradient_kernel(head_ref, delta_ref, out_ref):
    pairs, _, rows, _ = out_ref.shape
    for k in range(pairs):
        block = lax.dot_general(
            head_ref[2 * k * rows : 2 * (k + 1) * rows, :],
            delta_ref[...],
            (((1,), (1,)), ((), ())),
            preferred_element_type=jnp.float32,
        )
        out_ref[k, 0] = block[:rows]
        out_ref[k, 1] = block[rows:]


def gradient(core, head, delta, run, other=False):
    rows = head.shape[0] // run
    shape = (run // 2, rows, delta.shape[0])
    in_vmem = pl.BlockSpec(memory_space=pltpu.VMEM)
    if core is None:
        out = pltpu.VMEM((run // 2, 2, *shape[1:]), jnp.float32)
        kernel = own_gradient_kernel
    else:
        out = pltpu.VMEM(shape, jnp.bfloat16 if other else jnp.float32)
        kernel = functools.partial(gradient_kernel, other)
    arrays = [pltpu.with_memory_space_constraint(x, pltpu.VMEM) for x in (head, delta)]
    return pl.pallas_call(
        kernel,
        out_shape=out,
        in_specs=([] if core is None else [pl.BlockSpec(memory_space=pltpu.SMEM)]) + [in_vmem] * 2,
        out_specs=in_vmem,
        compiler_params=pltpu.CompilerParams(vmem_limit_bytes=VMEM_LIMIT),
        cost_estimate=pl.CostEstimate(
            flops=2 * head.size * delta.shape[0],
            bytes_accessed=2 * (head.size + delta.size),
            transcendentals=0,
        ),
        name="partial_gradient",
    )(*([] if core is None else [core]), *arrays)


def head_gradient_kernel(steps, start, width, *refs):
    features_ref, delta_ref, out_ref, held_ref, sems = refs[0], refs[1], *refs[-3:]
    copies = []
    for k in range(steps):
        block = lax.dot_general(
            features_ref[:, start + k * width : start + (k + 1) * width],
            delta_ref[...],
            (((0,), (0,)), ((), ())),
            preferred_element_type=jnp.float32,
        )
        held_ref[k] = block.astype(jnp.bfloat16)
        copy = pltpu.make_async_copy(
            held_ref.at[k], out_ref.at[pl.ds(start + k * width, width)], sems.at[k]
        )
        copy.start()
        copies.append(copy)
    for copy in copies:
        copy.wait()


def head_gradient(features, delta, out, start, steps, width):
    columns = delta.shape[1]
    in_vmem = pl.BlockSpec(memory_space=pltpu.VMEM)
    in_hbm = pl.BlockSpec(memory_space=pltpu.HBM)
    return pl.pallas_call(
        functools.partial(head_gradient_kernel, steps, start, width),
        out_shape=jax.ShapeDtypeStruct((features.shape[1], columns), jnp.bfloat16),
        in_specs=[in_vmem, in_vmem] + ([] if out is None else [in_hbm]),
        out_specs=in_hbm,
        scratch_shapes=[
            pltpu.VMEM((steps, width, columns), jnp.bfloat16),
            pltpu.SemaphoreType.DMA((steps,)),
        ],
        input_output_aliases={} if out is None else {2: 0},
        compiler_params=pltpu.CompilerParams(vmem_limit_bytes=VMEM_LIMIT),
        cost_estimate=pl.CostEstimate(
            flops=2 * steps * width * delta.size,
            bytes_accessed=2 * (features.size + delta.size + steps * width * columns),
            transcendentals=0,
        ),
        name="head_gradient",
    )(features, delta, *([] if out is None else [out]))


def per_device(hidden, head, teacher, block_ids, counts):
    tok_size = lax.axis_size("tok")
    vocab_size = lax.axis_size("vocab")
    tok_index = lax.axis_index("tok")
    vocab_index = lax.axis_index("vocab")
    token_count = hidden.shape[0]
    rows, column_count = head.shape
    run = vocab_size // tok_size
    half = token_count // 2
    core = vocab_index & 1

    def columns_of(index, first, count):
        return lax.dynamic_slice(hidden, (first, index * rows), (count, rows))

    quarter = half // 2
    part = quarter // 2
    second = lax.div(vocab_index, 2) & 1
    near, later = [
        [
            shift_tok(
                columns_of(lax.rem(tok_index + d, tok_size), core * half + first, count),
                d,
                tok_size,
            )
            for d in range(1, tok_size)
        ]
        for first, count in ((0, quarter), (quarter + second * part, part))
    ]
    upper = []
    while 1 << len(upper) < vocab_size:
        upper.append((vocab_index & (1 << len(upper))) != 0)
    high = lax.div(vocab_index, run)
    apart = lax.rem(tok_index + tok_size - high, tok_size)
    apart_is = [apart == d for d in range(tok_size)]
    first_column = vocab_index * column_count
    column_block = (first_column + jnp.arange(column_count, dtype=jnp.int32)) // BLK
    live_slot = jnp.arange(block_ids.shape[1], dtype=jnp.int32)[None, :] < counts[:, None]
    core_word = core.reshape(1)
    tok_is = [tok_index == d for d in range(tok_size)]
    head, upper, apart_is, tok_is, column_block, live_slot, core_word = lax.optimization_barrier(
        (head, upper, apart_is, tok_is, column_block, live_slot, core_word)
    )
    head_here = load(head)
    near, head_here, column_block, teacher, hidden = lax.optimization_barrier(
        (near, head_here, column_block, teacher, hidden)
    )
    products = [jnp.dot(x, head_here, preferred_element_type=jnp.float32) for x in near]
    returned = [[shift_tok(x, -d, tok_size)] for d, x in enumerate(products, 1)]
    later = [in_order(x, swap_vocab(x, 2, vocab_size), upper[1]) for x in later]
    later, _ = lax.optimization_barrier((later, products))
    near = [jnp.concatenate(pair, axis=0) for pair in zip(near, later)]
    far = [swap_vocab(x, 1, vocab_size) for x in near]
    for d in range(1, tok_size):
        for x in (later[d - 1], far[d - 1]):
            returned[d - 1].append(
                shift_tok(
                    jnp.dot(x, head_here, preferred_element_type=jnp.float32), -d, tok_size
                )
            )
    own = hidden[:, :rows]
    for d in range(1, tok_size):
        own = jnp.where(tok_is[d], hidden[:, d * rows : (d + 1) * rows], own)
    logits = jnp.dot(own, head_here, preferred_element_type=jnp.float32)
    block_hit = jnp.any(
        (block_ids[:, :, None] == column_block[None, None, :]) & live_slot[:, :, None], axis=1
    )
    features = [own] + [in_order(n, f, upper[0]) for n, f in zip(near, far)]
    all_features = jnp.concatenate(features, axis=0)
    blocks = block_hit.shape[0]
    listed = jnp.broadcast_to(
        block_hit[:, None, :], (blocks, token_count // blocks, column_count)
    ).reshape(token_count, column_count)
    teacher_f = teacher.astype(jnp.float32)
    kept = jnp.where(listed, teacher_f, 0.0)
    mass = jnp.sum(kept, axis=1)
    entropy = jnp.sum(jnp.where(listed, teacher_f * jnp.log(teacher_f), 0.0), axis=1)
    kept, early = kept.astype(jnp.bfloat16), jnp.stack([mass, entropy])
    returned, all_features, logits, kept, early = lax.optimization_barrier(
        (returned, all_features, logits, kept, early)
    )
    places = [i for i in range(1, len(upper)) if 1 << i < run]
    powers, stats = local_stats(core_word, logits, kept, early, returned)
    gathered = gather_vocab(stats, upper, places, vocab_size)
    delta, lse, kl = finish(gathered, stats, powers, kept)

    deltas = [delta] + [shift_tok(delta, d, tok_size) for d in range(1, tok_size)]
    flags = [upper[i] for i in places]

    def direct(pieces):
        count = len(pieces)
        return [select([pieces[j ^ i] for j in range(count)], flags) for i in range(count)]

    own_pieces = direct(list(gradient(None, head_here, delta, run)))
    own_others = [
        swap_vocab(x.astype(jnp.bfloat16), 2 * i, vocab_size)
        for i, x in enumerate(own_pieces[1:], 1)
    ]
    state = []
    for x in deltas[1:]:
        send = gradient(core_word, head_here, x, run, other=True)
        own_others, _ = lax.optimization_barrier((own_others, send))
        x, _ = lax.optimization_barrier((x, send))
        keep = gradient(core_word, head_here, x, run)
        state.append((keep, swap_vocab(send, 1, vocab_size)))
    all_delta = jnp.concatenate(deltas, axis=0)

    width = 256 if rows % 256 == 0 else rows
    chunks = rows // width
    taken = [
        direct(list(keep + other.astype(jnp.float32))) for keep, other in state
    ]
    taken = [[x.astype(jnp.bfloat16) for x in pieces] for pieces in taken]
    taken, all_delta = lax.optimization_barrier((taken, all_delta))
    arrived = []
    for d, pieces in enumerate(taken, 1):
        block = []
        for offset, piece in enumerate(pieces):
            pairs = [
                (v * tok_size + t, (v ^ (2 * offset)) * tok_size + (t - d) % tok_size)
                for v in range(vocab_size)
                for t in range(tok_size)
            ]
            block.append(lax.ppermute(piece, ("vocab", "tok"), pairs))
        arrived.append(block)
    done = (chunks + 1) // 2
    grad_head = head_gradient(all_features, all_delta, None, 0, done, width)
    arrived, grad_head = lax.optimization_barrier((arrived, grad_head))
    own_sum = own_pieces[0]
    for other in own_others:
        own_sum = own_sum + other.astype(jnp.float32)
    send = jnp.where(upper[0], own_sum[0], own_sum[1]).astype(jnp.bfloat16)
    own_sum = jnp.where(upper[0], own_sum[1], own_sum[0])
    own_sum = own_sum + swap_vocab(send, 1, vocab_size).astype(jnp.float32)
    sums = [own_sum]
    for block in arrived:
        total = block[0].astype(jnp.float32)
        for x in block[1:]:
            total = total + x.astype(jnp.float32)
        sums.append(total)
    blocks = []
    for k in range(tok_size):
        block = sums[k]
        for d in range(1, tok_size):
            block = jnp.where(apart_is[d], sums[(k - d) % tok_size], block)
        blocks.append(block)
    total = blocks[0]
    if done < chunks:
        blocks[1:], all_delta = lax.optimization_barrier((blocks[1:], all_delta))
        grad_head = head_gradient(
            all_features, all_delta, grad_head, done * width, chunks - done, width
        )
    for k in range(1, tok_size):
        pairs = [(v, (v + k * run) % vocab_size) for v in range(vocab_size)]
        total = total + lax.ppermute(
            blocks[k].astype(jnp.bfloat16), "vocab", pairs
        ).astype(jnp.float32)
    grad_hidden = total.T
    return (lse, kl, grad_hidden, grad_head)


def solution(mesh):
    placed = (P("tok", None), P("tok", "vocab"), P("tok", "vocab"), P("tok", None), P("tok"))
    return jax.shard_map(
        per_device,
        mesh=mesh,
        in_specs=placed,
        out_specs=(P("tok"), P("tok"), P("tok", "vocab"), P("tok", "vocab")),
        check_vma=False,
    )
```

```python
import functools

import jax
import jax.numpy as jnp
from jax import lax
from jax.experimental import pallas as pl
from jax.experimental.pallas import tpu as pltpu
from jax.sharding import PartitionSpec as P

BLK = 512


loss_scale = 1024.0
VMEM_LIMIT = 16 << 20
STEP = 32


def shift_tok(x, offset, size):
    return lax.ppermute(x, "tok", [(i, (i + offset) % size) for i in range(size)])


def swap_vocab(x, bit, size):
    return lax.ppermute(x, "vocab", [(i, i ^ bit) for i in range(size)])


def in_order(mine, other, upper):
    return jnp.concatenate(
        [jnp.where(upper, other, mine), jnp.where(upper, mine, other)], axis=0
    )


def select(options, flags):
    for flag in flags:
        options = [jnp.where(flag, high, low) for low, high in zip(options[::2], options[1::2])]
    return options[0]


def gather_vocab(stats, upper, places, size):
    pair = in_order(stats[None], swap_vocab(stats[None], 1, size), upper[0])
    count = 1 << len(places)
    options = [pair] + [swap_vocab(pair, 2 * offset, size) for offset in range(1, count)]
    flags = [upper[i] for i in places]
    gathered = jnp.concatenate(
        [select([options[j ^ i] for i in range(count)], flags) for j in range(count)], axis=0
    )
    for i in range(len(places) + 1, len(upper)):
        gathered = in_order(gathered, swap_vocab(gathered, 1 << i, size), upper[i])
    return gathered


def load_kernel(head_ref, held_ref, sems):
    steps = sems.shape[0]
    depth = head_ref.shape[0] // steps
    parts = [pl.ds(k * depth, depth) for k in range(steps)]
    copies = [
        pltpu.make_async_copy(head_ref.at[part], held_ref.at[part], sems.at[k])
        for k, part in enumerate(parts)
    ]
    for copy in copies:
        copy.start()
    for copy in copies:
        copy.wait()


def load(head):
    steps = 4
    return pl.pallas_call(
        load_kernel,
        out_shape=pltpu.VMEM(head.shape, head.dtype),
        in_specs=[pl.BlockSpec(memory_space=pltpu.HBM)],
        out_specs=pl.BlockSpec(memory_space=pltpu.VMEM),
        scratch_shapes=[pltpu.SemaphoreType.DMA((steps,))],
        compiler_params=pltpu.CompilerParams(vmem_limit_bytes=VMEM_LIMIT),
        cost_estimate=pl.CostEstimate(
            flops=0, bytes_accessed=4 * head.size, transcendentals=0
        ),
        name="load_head",
    )(pltpu.with_memory_space_constraint(head, pltpu.HBM))


def stats_kernel(core_ref, own_ref, kept_ref, early_ref, *refs):
    parts, (powers_ref, stats_ref, turned_ref) = refs[:-3], refs[-3:]
    half = own_ref.shape[0] // 2
    lane = lax.broadcasted_iota(jnp.int32, (STEP, 128), 1)
    groups = [(core_ref[0], 0, half // 2), (core_ref[0], half // 2, half // 2)]
    groups.append((1 - core_ref[0], 0, half))
    for place, (side, first, count) in enumerate(groups):
        start = side * half + first
        for r in range(0, count, STEP):
            rows = pl.ds(pl.multiple_of(start + r, STEP), STEP)
            logits = own_ref[rows, :]
            for part in parts[place::3]:
                logits = logits + part[r : r + STEP, :]
            top = jnp.max(logits, axis=1, keepdims=True)
            powers = jnp.exp(logits - top)
            powers_ref[rows, :] = powers
            total = jnp.sum(powers, axis=1, keepdims=True)
            dot = jnp.sum(kept_ref[rows, :].astype(jnp.float32) * logits, axis=1, keepdims=True)
            turned_ref[rows, :] = jnp.where(lane == 0, top, jnp.where(lane == 1, total, dot))
    turned = turned_ref[...].T
    stats_ref[0:2, :] = turned[0:2]
    stats_ref[2:3, :] = early_ref[0:1, :]
    stats_ref[3:4, :] = early_ref[1:2, :] - turned[2:3]


def local_stats(core, own_logits, kept, early, returned):
    in_vmem = pl.BlockSpec(memory_space=pltpu.VMEM)
    parts = [x for pair in returned for x in pair]
    arrays = [
        pltpu.with_memory_space_constraint(x, pltpu.VMEM) for x in (own_logits, kept, early, *parts)
    ]
    return pl.pallas_call(
        stats_kernel,
        out_shape=(
            pltpu.VMEM(own_logits.shape, jnp.float32),
            pltpu.VMEM((4, own_logits.shape[0]), jnp.float32),
        ),
        in_specs=[pl.BlockSpec(memory_space=pltpu.SMEM)] + [in_vmem] * len(arrays),
        out_specs=(in_vmem, in_vmem),
        scratch_shapes=[pltpu.VMEM((own_logits.shape[0], 128), jnp.float32)],
        compiler_params=pltpu.CompilerParams(vmem_limit_bytes=VMEM_LIMIT),
        cost_estimate=pl.CostEstimate(
            flops=8 * own_logits.size,
            bytes_accessed=12 * own_logits.size,
            transcendentals=own_logits.size,
        ),
        name="local_stats",
    )(core, *arrays)


def delta_kernel(gathered_ref, stats_ref, powers_ref, kept_ref, delta_ref, lse_ref, kl_ref):
    shards = [gathered_ref[i] for i in range(gathered_ref.shape[0])]
    top = shards[0][0:1]
    for x in shards[1:]:
        top = jnp.maximum(top, x[0:1])
    total, mass, part = 0.0, 0.0, 0.0
    for x in shards:
        total = total + x[1:2] * jnp.exp(x[0:1] - top)
        mass, part = mass + x[2:3], part + x[3:4]
    lse = top + jnp.log(total)
    lse_ref[...] = lse
    kl_ref[...] = part / mass - jnp.log(mass) + lse
    row = lax.broadcasted_iota(jnp.int32, (128, lse.shape[1]), 0)
    student_scale = loss_scale * jnp.exp(stats_ref[0:1, :] - lse)
    turned = jnp.where(row == 0, student_scale, loss_scale / mass).T
    student_column, kept_column = turned[:, 0:1], turned[:, 1:2]
    for r in range(0, powers_ref.shape[0], STEP):
        rows = slice(r, r + STEP)
        student = powers_ref[rows, :] * student_column[rows]
        kept = kept_ref[rows, :].astype(jnp.float32) * kept_column[rows]
        delta_ref[rows, :] = (student - kept).astype(jnp.bfloat16)


def finish(gathered, stats, powers, kept):
    tokens = powers.shape[0]
    in_vmem = pl.BlockSpec(memory_space=pltpu.VMEM)
    delta, lse, kl = pl.pallas_call(
        delta_kernel,
        out_shape=(
            pltpu.VMEM(powers.shape, jnp.bfloat16),
            jax.ShapeDtypeStruct((1, tokens), jnp.float32),
            jax.ShapeDtypeStruct((1, tokens), jnp.float32),
        ),
        in_specs=[in_vmem] * 4,
        out_specs=(in_vmem, in_vmem, in_vmem),
        compiler_params=pltpu.CompilerParams(vmem_limit_bytes=VMEM_LIMIT),
        cost_estimate=pl.CostEstimate(
            flops=8 * powers.size, bytes_accessed=8 * powers.size, transcendentals=0
        ),
        name="delta",
    )(*[pltpu.with_memory_space_constraint(x, pltpu.VMEM) for x in (gathered, stats, powers, kept)])
    return delta, lse.reshape(tokens), kl.reshape(tokens)


def gradient_kernel(other, core_ref, head_ref, delta_ref, out_ref):
    side = 1 - core_ref[0] if other else core_ref[0]
    pairs, rows, _ = out_ref.shape
    for k in range(pairs):
        if rows % 16 == 0:
            start = pl.multiple_of((2 * k + side) * rows, 16)
            head_rows = head_ref[pl.ds(start, rows), :]
        else:
            head_rows = head_ref[2 * k * rows : 2 * (k + 1) * rows, :]
        block = lax.dot_general(
            head_rows, delta_ref[...], (((1,), (1,)), ((), ())), preferred_element_type=jnp.float32
        )
        if rows % 16:
            block = jnp.where(side == 0, block[:rows], block[rows:])
        out_ref[k] = block.astype(out_ref.dtype)


def own_gradient_kernel(head_ref, delta_ref, out_ref):
    pairs, _, rows, _ = out_ref.shape
    for k in range(pairs):
        block = lax.dot_general(
            head_ref[2 * k * rows : 2 * (k + 1) * rows, :],
            delta_ref[...],
            (((1,), (1,)), ((), ())),
            preferred_element_type=jnp.float32,
        )
        out_ref[k, 0] = block[:rows]
        out_ref[k, 1] = block[rows:]


def gradient(core, head, delta, run, other=False):
    rows = head.shape[0] // run
    shape = (run // 2, rows, delta.shape[0])
    in_vmem = pl.BlockSpec(memory_space=pltpu.VMEM)
    if core is None:
        out = pltpu.VMEM((run // 2, 2, *shape[1:]), jnp.float32)
        kernel = own_gradient_kernel
    else:
        out = pltpu.VMEM(shape, jnp.bfloat16 if other else jnp.float32)
        kernel = functools.partial(gradient_kernel, other)
    arrays = [pltpu.with_memory_space_constraint(x, pltpu.VMEM) for x in (head, delta)]
    return pl.pallas_call(
        kernel,
        out_shape=out,
        in_specs=([] if core is None else [pl.BlockSpec(memory_space=pltpu.SMEM)]) + [in_vmem] * 2,
        out_specs=in_vmem,
        compiler_params=pltpu.CompilerParams(vmem_limit_bytes=VMEM_LIMIT),
        cost_estimate=pl.CostEstimate(
            flops=2 * head.size * delta.shape[0],
            bytes_accessed=2 * (head.size + delta.size),
            transcendentals=0,
        ),
        name="partial_gradient",
    )(*([] if core is None else [core]), *arrays)


def head_gradient_kernel(steps, start, width, *refs):
    features_ref, delta_ref, out_ref, held_ref, sems = refs[0], refs[1], *refs[-3:]
    copies = []
    for k in range(steps):
        block = lax.dot_general(
            features_ref[:, start + k * width : start + (k + 1) * width],
            delta_ref[...],
            (((0,), (0,)), ((), ())),
            preferred_element_type=jnp.float32,
        )
        held_ref[k] = block.astype(jnp.bfloat16)
        copy = pltpu.make_async_copy(
            held_ref.at[k], out_ref.at[pl.ds(start + k * width, width)], sems.at[k]
        )
        copy.start()
        copies.append(copy)
    for copy in copies:
        copy.wait()


def head_gradient(features, delta, out, start, steps, width):
    columns = delta.shape[1]
    in_vmem = pl.BlockSpec(memory_space=pltpu.VMEM)
    in_hbm = pl.BlockSpec(memory_space=pltpu.HBM)
    return pl.pallas_call(
        functools.partial(head_gradient_kernel, steps, start, width),
        out_shape=jax.ShapeDtypeStruct((features.shape[1], columns), jnp.bfloat16),
        in_specs=[in_vmem, in_vmem] + ([] if out is None else [in_hbm]),
        out_specs=in_hbm,
        scratch_shapes=[
            pltpu.VMEM((steps, width, columns), jnp.bfloat16),
            pltpu.SemaphoreType.DMA((steps,)),
        ],
        input_output_aliases={} if out is None else {2: 0},
        compiler_params=pltpu.CompilerParams(vmem_limit_bytes=VMEM_LIMIT),
        cost_estimate=pl.CostEstimate(
            flops=2 * steps * width * delta.size,
            bytes_accessed=2 * (features.size + delta.size + steps * width * columns),
            transcendentals=0,
        ),
        name="head_gradient",
    )(features, delta, *([] if out is None else [out]))


def per_device(hidden, head, teacher, block_ids, counts):
    tok_size = lax.axis_size("tok")
    vocab_size = lax.axis_size("vocab")
    tok_index = lax.axis_index("tok")
    vocab_index = lax.axis_index("vocab")
    token_count = hidden.shape[0]
    rows, column_count = head.shape
    run = vocab_size // tok_size
    half = token_count // 2
    core = vocab_index & 1

    def columns_of(index, first, count):
        return lax.dynamic_slice(hidden, (first, index * rows), (count, rows))

    quarter = half // 2
    near, later = [
        [
            shift_tok(
                columns_of(lax.rem(tok_index + d, tok_size), core * half + first, quarter),
                d,
                tok_size,
            )
            for d in range(1, tok_size)
        ]
        for first in (0, quarter)
    ]
    upper = []
    while 1 << len(upper) < vocab_size:
        upper.append((vocab_index & (1 << len(upper))) != 0)
    high = lax.div(vocab_index, run)
    apart = lax.rem(tok_index + tok_size - high, tok_size)
    apart_is = [apart == d for d in range(tok_size)]
    first_column = vocab_index * column_count
    column_block = (first_column + jnp.arange(column_count, dtype=jnp.int32)) // BLK
    live_slot = jnp.arange(block_ids.shape[1], dtype=jnp.int32)[None, :] < counts[:, None]
    core_word = core.reshape(1)
    tok_is = [tok_index == d for d in range(tok_size)]
    head, upper, apart_is, tok_is, column_block, live_slot, core_word = lax.optimization_barrier(
        (head, upper, apart_is, tok_is, column_block, live_slot, core_word)
    )
    head_here = load(head)
    near, head_here, column_block, teacher, hidden = lax.optimization_barrier(
        (near, head_here, column_block, teacher, hidden)
    )
    products = [jnp.dot(x, head_here, preferred_element_type=jnp.float32) for x in near]
    returned = [[shift_tok(x, -d, tok_size)] for d, x in enumerate(products, 1)]
    later, _ = lax.optimization_barrier((later, products))
    near = [jnp.concatenate(pair, axis=0) for pair in zip(near, later)]
    far = [swap_vocab(x, 1, vocab_size) for x in near]
    for d in range(1, tok_size):
        for x in (later[d - 1], far[d - 1]):
            returned[d - 1].append(
                shift_tok(
                    jnp.dot(x, head_here, preferred_element_type=jnp.float32), -d, tok_size
                )
            )
    own = hidden[:, :rows]
    for d in range(1, tok_size):
        own = jnp.where(tok_is[d], hidden[:, d * rows : (d + 1) * rows], own)
    logits = jnp.dot(own, head_here, preferred_element_type=jnp.float32)
    block_hit = jnp.any(
        (block_ids[:, :, None] == column_block[None, None, :]) & live_slot[:, :, None], axis=1
    )
    features = [own] + [in_order(n, f, upper[0]) for n, f in zip(near, far)]
    all_features = jnp.concatenate(features, axis=0)
    blocks = block_hit.shape[0]
    listed = jnp.broadcast_to(
        block_hit[:, None, :], (blocks, token_count // blocks, column_count)
    ).reshape(token_count, column_count)
    teacher_f = teacher.astype(jnp.float32)
    kept = jnp.where(listed, teacher_f, 0.0)
    mass = jnp.sum(kept, axis=1)
    entropy = jnp.sum(jnp.where(listed, teacher_f * jnp.log(teacher_f), 0.0), axis=1)
    kept, early = kept.astype(jnp.bfloat16), jnp.stack([mass, entropy])
    returned, all_features, logits, kept, early = lax.optimization_barrier(
        (returned, all_features, logits, kept, early)
    )
    places = [i for i in range(1, len(upper)) if 1 << i < run]
    powers, stats = local_stats(core_word, logits, kept, early, returned)
    gathered = gather_vocab(stats, upper, places, vocab_size)
    delta, lse, kl = finish(gathered, stats, powers, kept)

    deltas = [delta] + [shift_tok(delta, d, tok_size) for d in range(1, tok_size)]
    flags = [upper[i] for i in places]

    def direct(pieces):
        count = len(pieces)
        return [select([pieces[j ^ i] for j in range(count)], flags) for i in range(count)]

    own_pieces = direct(list(gradient(None, head_here, delta, run)))
    own_others = [
        swap_vocab(x.astype(jnp.bfloat16), 2 * i, vocab_size)
        for i, x in enumerate(own_pieces[1:], 1)
    ]
    state = []
    for x in deltas[1:]:
        send = gradient(core_word, head_here, x, run, other=True)
        own_others, _ = lax.optimization_barrier((own_others, send))
        x, _ = lax.optimization_barrier((x, send))
        keep = gradient(core_word, head_here, x, run)
        state.append((keep, swap_vocab(send, 1, vocab_size)))
    all_delta = jnp.concatenate(deltas, axis=0)

    width = 256 if rows % 256 == 0 else rows
    chunks = rows // width
    taken = [
        direct(list(keep + other.astype(jnp.float32))) for keep, other in state
    ]
    taken = [[x.astype(jnp.bfloat16) for x in pieces] for pieces in taken]
    taken, all_delta = lax.optimization_barrier((taken, all_delta))
    arrived = []
    for d, pieces in enumerate(taken, 1):
        block = []
        for offset, piece in enumerate(pieces):
            pairs = [
                (v * tok_size + t, (v ^ (2 * offset)) * tok_size + (t - d) % tok_size)
                for v in range(vocab_size)
                for t in range(tok_size)
            ]
            block.append(lax.ppermute(piece, ("vocab", "tok"), pairs))
        arrived.append(block)
    done = (chunks + 1) // 2
    grad_head = head_gradient(all_features, all_delta, None, 0, done, width)
    arrived, grad_head = lax.optimization_barrier((arrived, grad_head))
    own_sum = own_pieces[0]
    for other in own_others:
        own_sum = own_sum + other.astype(jnp.float32)
    send = jnp.where(upper[0], own_sum[0], own_sum[1]).astype(jnp.bfloat16)
    own_sum = jnp.where(upper[0], own_sum[1], own_sum[0])
    own_sum = own_sum + swap_vocab(send, 1, vocab_size).astype(jnp.float32)
    sums = [own_sum]
    for block in arrived:
        total = block[0].astype(jnp.float32)
        for x in block[1:]:
            total = total + x.astype(jnp.float32)
        sums.append(total)
    blocks = []
    for k in range(tok_size):
        block = sums[k]
        for d in range(1, tok_size):
            block = jnp.where(apart_is[d], sums[(k - d) % tok_size], block)
        blocks.append(block)
    total = blocks[0]
    if done < chunks:
        blocks[1:], all_delta = lax.optimization_barrier((blocks[1:], all_delta))
        grad_head = head_gradient(
            all_features, all_delta, grad_head, done * width, chunks - done, width
        )
    for k in range(1, tok_size):
        pairs = [(v, (v + k * run) % vocab_size) for v in range(vocab_size)]
        total = total + lax.ppermute(
            blocks[k].astype(jnp.bfloat16), "vocab", pairs
        ).astype(jnp.float32)
    grad_hidden = total.T
    return (lse, kl, grad_hidden, grad_head)


def solution(mesh):
    placed = (P("tok", None), P("tok", "vocab"), P("tok", "vocab"), P("tok", None), P("tok"))
    return jax.shard_map(
        per_device,
        mesh=mesh,
        in_specs=placed,
        out_specs=(P("tok"), P("tok"), P("tok", "vocab"), P("tok", "vocab")),
        check_vma=False,
    )
```
